128 devices in a mesh: dp: 8 (over y, z_lo), axial: 16 (over x, z_hi, core).
Axes of the slice: x: 4, y: 4, z: 4 (z_hi: 2, z_lo: 2; z = z_hi * 2 + z_lo), core: 2. Of those that a mesh axis runs over, the one named last changes fastest.
Arguments:
- single_state: bfloat16 [8, 256, 1024], P('dp', 'axial'), may hold values from -6 to 6
- pair_state: bfloat16 [8, 256, 256, 128], P('dp', 'axial'), may hold values from -6 to 6
- residue_mask: int32 [8, 256], P('dp'), may hold values from 0 to 1, as said below
- pair_cotangent: bfloat16 [8, 256, 256, 128], P('dp', 'axial'), may hold values from -6 to 6
- outer_norm_gain: float32 [1024], replicated, may hold values from 0.5 to 1.5
- outer_norm_bias: float32 [1024], replicated, may hold values from -1.5 to 1.5
- outer_left: bfloat16 [1024, 32], replicated, may hold values from -0.1875 to 0.1875
- outer_right: bfloat16 [1024, 32], replicated, may hold values from -0.1875 to 0.1875
- outer_proj: bfloat16 [1024, 128], replicated, may hold values from -0.1875 to 0.1875
- outer_bias: float32 [128], replicated, may hold values from -1.5 to 1.5
- triangle_norm_gain: float32 [2, 128], replicated, may hold values from 0.5 to 1.5
- triangle_norm_bias: float32 [2, 128], replicated, may hold values from -1.5 to 1.5
- triangle_proj: bfloat16 [2, 128, 512], replicated, may hold values from -0.5 to 0.5
- triangle_gate: bfloat16 [2, 128, 128], replicated, may hold values from -0.5 to 0.5
- triangle_out_gain: float32 [2, 128], replicated, may hold values from 0.5 to 1.5
- triangle_out_bias: float32 [2, 128], replicated, may hold values from -1.5 to 1.5
- triangle_out: bfloat16 [2, 128, 128], replicated, may hold values from -0.5 to 0.5
Outputs:
- single_gradient: bfloat16 [8, 256, 1024], P('dp', 'axial')
- pair_gradient: bfloat16 [8, 256, 256, 128], P('dp', 'axial')
- outer_norm_gain_gradient: float32 [1024], replicated
- outer_norm_bias_gradient: float32 [1024], replicated
- outer_left_gradient: float32 [1024, 32], replicated
- outer_right_gradient: float32 [1024, 32], replicated
- outer_proj_gradient: float32 [1024, 128], replicated
- outer_bias_gradient: float32 [128], replicated
- triangle_norm_gain_gradient: float32 [2, 128], replicated
- triangle_norm_bias_gradient: float32 [2, 128], replicated
- triangle_proj_gradient: float32 [2, 128, 512], replicated
- triangle_gate_gradient: float32 [2, 128, 128], replicated
- triangle_out_gain_gradient: float32 [2, 128], replicated
- triangle_out_bias_gradient: float32 [2, 128], replicated
- triangle_out_gradient: float32 [2, 128, 128], replicated
The draws below stay inside these ranges and needn't reach their ends.
Inputs may be any that keep to these rules, and one draw needn't show every extreme that they name: `residue_mask`: in each protein the ones form a prefix of at least 128 residues, and at least the last residue is 0.
All inputs are finite; a program needn't handle non-finite values.
Results may differ from the reference program's by a relative error of at most 0.023.
Values may be sent and summed in bfloat16 or wider, within the bound.
A program may use at most 320 MiB of HBM per device.

```python
import jax
import jax.numpy as jnp
from jax import lax

CS = 1024
CZ = 128
CH = 128
CO = 32
L = 256
PROTEINS = 8


def draw_residue_mask(key, part):
    key = jax.random.fold_in(key, 11)
    lengths = jax.random.randint(key, (PROTEINS, 1), L // 2, L)
    positions = jnp.arange(L, dtype=jnp.int32)[None, :]
    return (positions < lengths).astype(jnp.int32)


def level_of(own_key, dims, cuts, smallest, top_value):
    level = 1.0
    for axis_at, parts in cuts:
        steps = jax.random.uniform(jax.random.fold_in(jax.random.fold_in(own_key, 6), axis_at), (parts,), jnp.float32, smallest / len(cuts), top_value / len(cuts))
        level = level * jnp.repeat(jnp.exp(steps), dims[axis_at] // parts).reshape((-1,) + (1,) * (len(dims) - 1 - axis_at))
    return level


def normal_values(key, extent, scale, most, split=(), kind=jnp.bfloat16):
    values = scale * jax.random.normal(key, extent, jnp.float32)
    if split:
        values = values * level_of(key, extent, split, -0.22, 0.18)
    return jnp.clip(values, -most, most).astype(kind)


def setup_inputs(seed: int = 0) -> dict:
    keys = jax.random.split(jax.random.key(seed), 18)
    return {
        "single_state": normal_values(keys[0], (PROTEINS, L, CS), 1.0, 6.0, ((0, 8), (1, 16))),
        "pair_state": normal_values(keys[1], (PROTEINS, L, L, CZ), 1.0, 6.0, ((0, 8), (1, 16))),
        "residue_mask": draw_residue_mask(jax.random.fold_in(keys[17], 71), 0),
        "pair_cotangent": normal_values(keys[3], (PROTEINS, L, L, CZ), 1.0, 6.0, ((0, 8), (1, 16))),
        "outer_norm_gain": jnp.clip(1.0 + 0.1 * jax.random.normal(keys[4], (CS,), jnp.float32), 0.5, 1.5),
        "outer_norm_bias": normal_values(keys[5], (CS,), 0.3, 1.5, (), jnp.float32),
        "outer_left": normal_values(keys[6], (CS, CO), CS ** -0.5, 0.1875),
        "outer_right": normal_values(keys[7], (CS, CO), CS ** -0.5, 0.1875),
        "outer_proj": normal_values(keys[8], (CO * CO, CZ), (CO * CO) ** -0.5, 0.1875),
        "outer_bias": normal_values(keys[9], (CZ,), 0.3, 1.5, (), jnp.float32),
        "triangle_norm_gain": jnp.clip(1.0 + 0.1 * jax.random.normal(keys[10], (2, CZ), jnp.float32), 0.5, 1.5),
        "triangle_norm_bias": normal_values(keys[11], (2, CZ), 0.3, 1.5, (), jnp.float32),
        "triangle_proj": normal_values(keys[12], (2, CZ, 4 * CH), CZ ** -0.5, 0.5),
        "triangle_gate": normal_values(keys[13], (2, CZ, CZ), CZ ** -0.5, 0.5),
        "triangle_out_gain": jnp.clip(1.0 + 0.1 * jax.random.normal(keys[14], (2, CH), jnp.float32), 0.5, 1.5),
        "triangle_out_bias": normal_values(keys[15], (2, CH), 0.3, 1.5, (), jnp.float32),
        "triangle_out": normal_values(keys[16], (2, CH, CZ), CH ** -0.5, 0.5),
    }


EPSILON = 1e-05
HIGHEST = lax.Precision.HIGHEST

def norm_forward(values, weight_gain, weight_bias):
    average = lax.optimization_barrier(jnp.mean(values, axis=-1, keepdims=True))
    centred = values - average
    variance = lax.optimization_barrier(jnp.mean(centred * centred, axis=-1, keepdims=True))
    inverse = lax.rsqrt(variance + EPSILON)
    standard = centred * inverse
    return (standard * weight_gain + weight_bias, standard, inverse)

def norm_backward(cotangent, standard, inverse, weight_gain):
    scaled = cotangent * weight_gain
    centred = scaled - lax.optimization_barrier(jnp.mean(scaled, axis=-1, keepdims=True))
    return inverse * (centred - standard * lax.optimization_barrier(jnp.mean(scaled * standard, axis=-1, keepdims=True)))

def project(inputs, matrix):
    return jnp.einsum('...c,cd->...d', inputs.astype(jnp.float32), matrix.astype(jnp.float32))

def project_back(inputs, matrix):
    return jnp.einsum('...d,cd->...c', inputs.astype(jnp.float32), matrix.astype(jnp.float32))

def cell_sum(first_factor, second_factor):
    return jnp.einsum('ijc,ijd->cd', first_factor.astype(jnp.float32), second_factor.astype(jnp.float32))

def row_sum(first_factor, second_factor):
    return jnp.einsum('ic,id->cd', first_factor.astype(jnp.float32), second_factor.astype(jnp.float32))

def triangle_front(pair_in, pair_mask, weight_gain, weight_bias, proj_weight, gate_weight):
    normed, standard, inverse = norm_forward(pair_in.astype(jnp.float32), weight_gain, weight_bias)
    normed = normed.astype(jnp.bfloat16)
    projected = project(normed, proj_weight)
    hidden = projected.shape[-1] // 4
    left_side = (pair_mask * jax.nn.sigmoid(projected[..., :hidden]) * projected[..., hidden:2 * hidden]).astype(jnp.bfloat16)
    right_side = (pair_mask * jax.nn.sigmoid(projected[..., 2 * hidden:3 * hidden]) * projected[..., 3 * hidden:]).astype(jnp.bfloat16)
    gate_value = jax.nn.sigmoid(project(normed, gate_weight))
    return (normed, standard, inverse, projected, gate_value, left_side, right_side)

def triangle_finish(product, out_gain, out_bias, out_weight):
    product_norm, product_standard, product_inverse = norm_forward(product, out_gain, out_bias)
    product_norm = product_norm.astype(jnp.bfloat16)
    linear_out = project(product_norm, out_weight)
    return (product_norm, product_standard, product_inverse, linear_out)

def triangle_grad_out(cotangent, gate_value, linear_out, product_norm, product_standard, product_inverse, out_gain, out_weight):
    linear_grad = (cotangent * gate_value).astype(jnp.bfloat16)
    gate_grad = (cotangent * linear_out * gate_value * (1.0 - gate_value)).astype(jnp.bfloat16)
    out_weight_sum = cell_sum(product_norm, linear_grad)
    norm_grad = project_back(linear_grad, out_weight)
    out_gain_sum = lax.optimization_barrier(jnp.sum(norm_grad * product_standard, axis=(0, 1)))
    out_bias_sum = lax.optimization_barrier(jnp.sum(norm_grad, axis=(0, 1)))
    product_grad = norm_backward(norm_grad, product_standard, product_inverse, out_gain).astype(jnp.bfloat16)
    return (gate_grad, product_grad, (out_gain_sum, out_bias_sum, out_weight_sum))

def triangle_grad_in(cotangent, gate_grad, left_grad, right_grad, projected, pair_mask, normed, standard, inverse, weight_gain, proj_weight, gate_weight):
    hidden = projected.shape[-1] // 4
    left_gate = jax.nn.sigmoid(projected[..., :hidden])
    right_gate = jax.nn.sigmoid(projected[..., 2 * hidden:3 * hidden])
    left_masked = left_grad * pair_mask
    right_masked = right_grad * pair_mask
    proj_grad = jnp.concatenate([left_masked * projected[..., hidden:2 * hidden] * left_gate * (1.0 - left_gate), left_masked * left_gate, right_masked * projected[..., 3 * hidden:] * right_gate * (1.0 - right_gate), right_masked * right_gate], axis=-1).astype(jnp.bfloat16)
    proj_sum = cell_sum(normed, proj_grad)
    gate_sum = cell_sum(normed, gate_grad)
    normed_grad = project_back(proj_grad, proj_weight) + project_back(gate_grad, gate_weight)
    gain_sum = lax.optimization_barrier(jnp.sum(normed_grad * standard, axis=(0, 1)))
    bias_sum = lax.optimization_barrier(jnp.sum(normed_grad, axis=(0, 1)))
    input_grad = (cotangent + norm_backward(normed_grad, standard, inverse, weight_gain)).astype(jnp.bfloat16)
    return (input_grad, (gain_sum, bias_sum, proj_sum, gate_sum))

def core_forward(left_side, right_side, incoming):
    first_factor = left_side.astype(jnp.float32)
    second_factor = right_side.astype(jnp.float32)
    if incoming:
        return jnp.einsum('kic,kjc->ijc', first_factor, second_factor)
    return jnp.einsum('ikc,jkc->ijc', first_factor, second_factor)

def core_backward(product_grad, left_side, right_side, incoming):
    grad_values = product_grad.astype(jnp.float32)
    first_factor = left_side.astype(jnp.float32)
    second_factor = right_side.astype(jnp.float32)
    if incoming:
        return (jnp.einsum('ijc,kjc->kic', grad_values, second_factor), jnp.einsum('kic,ijc->kjc', first_factor, grad_values))
    return (jnp.einsum('ijc,jkc->ikc', grad_values, second_factor), jnp.einsum('ijc,ikc->jkc', grad_values, first_factor))

def triangle_forward(pair_in, pair_mask, params, incoming):
    weight_gain, weight_bias, proj_weight, gate_weight, out_gain, out_bias, out_weight = params
    normed, standard, inverse, projected, gate_value, left_side, right_side = triangle_front(pair_in, pair_mask, weight_gain, weight_bias, proj_weight, gate_weight)
    product = core_forward(left_side, right_side, incoming)
    product_norm, product_standard, product_inverse, linear_out = triangle_finish(product, out_gain, out_bias, out_weight)
    pair_out = (pair_in.astype(jnp.float32) + gate_value * linear_out).astype(jnp.bfloat16)
    kept = (normed, standard, inverse, projected, gate_value, left_side, right_side, product_norm, product_standard, product_inverse, linear_out)
    return (pair_out, kept)

def triangle_backward(pair_grad, kept, pair_mask, params, incoming):
    weight_gain, weight_bias, proj_weight, gate_weight, out_gain, out_bias, out_weight = params
    normed, standard, inverse, projected, gate_value, left_side, right_side, product_norm, product_standard, product_inverse, linear_out = kept
    cotangent = pair_grad.astype(jnp.float32)
    gate_grad, product_grad, out_sums = triangle_grad_out(cotangent, gate_value, linear_out, product_norm, product_standard, product_inverse, out_gain, out_weight)
    left_grad, right_grad = core_backward(product_grad, left_side, right_side, incoming)
    input_grad, in_sums = triangle_grad_in(cotangent, gate_grad, left_grad, right_grad, projected, pair_mask, normed, standard, inverse, weight_gain, proj_weight, gate_weight)
    return (input_grad, in_sums + out_sums)

def protein_backward(single_state, pair_state, residue_mask, pair_cotangent, weights):
    outer_norm_gain, outer_norm_bias, outer_left, outer_right, outer_proj, outer_bias, triangle_norm_gain, triangle_norm_bias, triangle_proj, triangle_gate, triangle_out_gain, triangle_out_bias, triangle_out = weights
    residue_weight = residue_mask.astype(jnp.float32)
    pair_mask = (residue_weight[:, None] * residue_weight[None, :])[:, :, None]
    single_norm, single_standard, single_inverse = norm_forward(single_state.astype(jnp.float32), outer_norm_gain, outer_norm_bias)
    single_norm = single_norm.astype(jnp.bfloat16)
    left_outer = (jnp.dot(single_norm, outer_left, preferred_element_type=jnp.float32) * residue_weight[:, None]).astype(jnp.bfloat16)
    right_outer = (jnp.dot(single_norm, outer_right, preferred_element_type=jnp.float32) * residue_weight[:, None]).astype(jnp.bfloat16)
    inner_width = outer_left.shape[1]
    outer_cube = outer_proj.reshape(inner_width, inner_width, -1).astype(jnp.float32)
    mixed = jnp.einsum('jb,abc->jac', right_outer.astype(jnp.float32), outer_cube).astype(jnp.bfloat16)
    outer_term = jnp.einsum('ia,jac->ijc', left_outer.astype(jnp.float32), mixed.astype(jnp.float32)) + outer_bias
    pair_first = (pair_state.astype(jnp.float32) + pair_mask * outer_term).astype(jnp.bfloat16)
    triangle_weights = (triangle_norm_gain, triangle_norm_bias, triangle_proj, triangle_gate, triangle_out_gain, triangle_out_bias, triangle_out)
    params_out = tuple((member[0] for member in triangle_weights))
    params_in = tuple((member[1] for member in triangle_weights))
    pair_second, kept_out = triangle_forward(pair_first, pair_mask, params_out, False)
    unused_pair, kept_in = triangle_forward(pair_second, pair_mask, params_in, True)
    grad_second, sums_in = triangle_backward(pair_cotangent, kept_in, pair_mask, params_in, True)
    grad_first, sums_out = triangle_backward(grad_second, kept_out, pair_mask, params_out, False)
    outer_grad = (grad_first.astype(jnp.float32) * pair_mask).astype(jnp.bfloat16)
    outer_bias_sum = lax.optimization_barrier(jnp.sum(outer_grad.astype(jnp.float32), axis=(0, 1)))
    left_grad = (jnp.einsum('ijc,jac->ia', outer_grad.astype(jnp.float32), mixed.astype(jnp.float32)) * residue_weight[:, None]).astype(jnp.bfloat16)
    mixed_grad = jnp.einsum('ia,ijc->jac', left_outer.astype(jnp.float32), outer_grad.astype(jnp.float32))
    right_total = jnp.einsum('jac,abc->jb', mixed_grad, outer_cube, precision=HIGHEST)
    right_grad = (right_total * residue_weight[:, None]).astype(jnp.bfloat16)
    cube_sum = jnp.einsum('jb,jac->abc', right_outer.astype(jnp.float32), mixed_grad, precision=HIGHEST)
    left_sum = row_sum(single_norm, left_grad)
    right_sum = row_sum(single_norm, right_grad)
    single_grad = project_back(left_grad, outer_left) + project_back(right_grad, outer_right)
    gain_sum = lax.optimization_barrier(jnp.sum(single_grad * single_standard, axis=0))
    bias_sum = lax.optimization_barrier(jnp.sum(single_grad, axis=0))
    single_gradient = norm_backward(single_grad, single_standard, single_inverse, outer_norm_gain).astype(jnp.bfloat16)
    stacked = tuple((jnp.stack([first_sum, second_sum]) for first_sum, second_sum in zip(sums_out, sums_in)))
    sums = (gain_sum, bias_sum, left_sum, right_sum, cube_sum.reshape(inner_width * inner_width, -1), outer_bias_sum) + stacked
    return (single_gradient, grad_first, sums)

def reference(single_state, pair_state, residue_mask, pair_cotangent, outer_norm_gain, outer_norm_bias, outer_left, outer_right, outer_proj, outer_bias, triangle_norm_gain, triangle_norm_bias, triangle_proj, triangle_gate, triangle_out_gain, triangle_out_bias, triangle_out):
    weights = (outer_norm_gain, outer_norm_bias, outer_left, outer_right, outer_proj, outer_bias, triangle_norm_gain, triangle_norm_bias, triangle_proj, triangle_gate, triangle_out_gain, triangle_out_bias, triangle_out)

    def per_protein(inputs):
        return protein_backward(inputs[0], inputs[1], inputs[2], inputs[3], weights)
    single_gradient, pair_gradient, sums = lax.map(per_protein, (single_state, pair_state, residue_mask, pair_cotangent))
    divisor = float(PROTEINS * L)
    totals = tuple((lax.optimization_barrier(jnp.sum(member, axis=0)) / divisor for member in sums))
    return (single_gradient, pair_gradient, totals[0], totals[1], totals[2], totals[3], totals[4], totals[5], totals[6], totals[7], totals[8], totals[9], totals[10], totals[11], totals[12])
```

```python
import functools

import jax
import jax.numpy as jnp
from jax import lax
from jax.experimental import pallas as pl
from jax.experimental.pallas import tpu as pltpu
from jax.sharding import PartitionSpec as P

EPSILON = 1e-05
F32 = jnp.float32
BF16 = jnp.bfloat16
MESH = pl.DeviceIdType.MESH
C = 128
I = 16
J = 256
B = 32
Q = 4
CQ = 4
PART = 208
VMEM_LIMIT = 56 * 2**20


def nn(a, b):
    return lax.dot_general(a, b, (((1,), (0,)), ((), ())), preferred_element_type=F32)


def nt(a, b):
    return lax.dot_general(a, b, (((1,), (1,)), ((), ())), preferred_element_type=F32)


def tn(a, b):
    return lax.dot_general(a, b, (((0,), (0,)), ((), ())), preferred_element_type=F32)


def sigmoid(x):
    return 0.5 * jnp.tanh(0.5 * x) + 0.5


def norm(x, axis=0):
    centred = x - jnp.mean(x, axis=axis, keepdims=True)
    variance = jnp.mean(centred * centred, axis=axis, keepdims=True)
    inverse = lax.rsqrt(variance + EPSILON)
    return centred * inverse, inverse


def norm_back(scaled, standard, inverse, axis=0):
    first = jnp.mean(scaled, axis=axis, keepdims=True)
    second = jnp.mean(scaled * standard, axis=axis, keepdims=True)
    return inverse * (scaled - first - standard * second)


def put_row(cells, i, value):
    cells[0, pl.ds(i, C, stride=I), :] = value[:, :C]
    cells[1, pl.ds(i, C, stride=I), :] = value[:, C:]


def get_row(cells, i):
    return jnp.concatenate(
        [cells[0, pl.ds(i, C, stride=I), :], cells[1, pl.ds(i, C, stride=I), :]], axis=1
    )


def cells_out(cells, out_ref):
    def step(n, _):
        for half in range(2):
            part = cells[half, pl.ds(pl.multiple_of(n * 256, 256), 256), :]
            out_ref[pl.ds(n * 16, 16), :, half * C : (half + 1) * C] = part.reshape(
                16, I, C
            ).astype(BF16)
        return 0

    lax.fori_loop(0, 8, step, 0)


def cells_in(in_ref, cells):
    def step(n, _):
        for half in range(2):
            part = in_ref[pl.ds(n * 16, 16), :, half * C : (half + 1) * C]
            cells[half, pl.ds(pl.multiple_of(n * 256, 256), 256), :] = part.astype(F32).reshape(
                256, C
            )
        return 0

    lax.fori_loop(0, 8, step, 0)


def wide(ref):
    return jnp.broadcast_to(ref[...], (C, J))


def send_factors(pair_in, mask_row, gain, bias, front_weight, left_cells, right_cells, i):
    standard, _ = norm(pair_in)
    normed = (standard * gain + bias).astype(BF16)
    projected = nn(front_weight[: 4 * C, :], normed)
    put_row(left_cells, i, mask_row * sigmoid(projected[:C]) * projected[C : 2 * C])
    put_row(right_cells, i, mask_row * sigmoid(projected[2 * C : 3 * C]) * projected[3 * C :])


def head_kernel(single_ref, gain_ref, bias_ref, weight_ref, own_ref, every_ref, send_sem, recv_sem):
    me = lax.axis_index("axial")
    dp = lax.axis_index("dp")
    barrier = pltpu.get_barrier_semaphore()

    def greet(t, _):
        pl.semaphore_signal(
            barrier, inc=1, device_id=(dp, lax.rem(me + t, 16)), device_id_type=MESH
        )
        return 0

    lax.fori_loop(1, 16, greet, 0)
    standard, _ = norm(single_ref[...].astype(F32), axis=1)
    normed = (standard * gain_ref[...] + bias_ref[...]).astype(BF16)
    both = nn(normed, weight_ref[...]) * own_ref[...]
    mine = pl.ds(pl.multiple_of(me * I, I), I)
    every_ref[mine, :] = both.astype(BF16)
    pl.semaphore_wait(barrier, 15)

    def copy(t):
        return pltpu.make_async_remote_copy(
            src_ref=every_ref.at[mine],
            dst_ref=every_ref.at[mine],
            send_sem=send_sem.at[t],
            recv_sem=recv_sem.at[t],
            device_id=(dp, lax.rem(me + t, 16)),
            device_id_type=MESH,
        )

    def begin(t, _):
        copy(t).start()
        return 0

    def finish(t, _):
        copy(t).wait()
        return 0

    lax.fori_loop(1, 16, begin, 0)
    lax.fori_loop(1, 16, finish, 0)


def mixed_rows(own_left, cube_ref, mixed_cells):
    for b in range(B):
        mixed_cells[b * I : (b + 1) * I, :] = nn(own_left, cube_ref[:, b * C : (b + 1) * C])


def front_first_kernel(
    pair_ref,
    every_ref,
    own_both_ref,
    cube_ref,
    mask_ref,
    outer_bias_ref,
    gain_ref,
    bias_ref,
    front_ref,
    first_ref,
    left_ref,
    right_ref,
    left_cells,
    right_cells,
    mixed_cells,
):
    right_rows = every_ref[...].astype(F32).T[B : 2 * B].astype(BF16)
    mixed_rows(own_both_ref[:, :B], cube_ref, mixed_cells)
    gain, bias, outer_bias = wide(gain_ref), wide(bias_ref), wide(outer_bias_ref)

    def step(i, _):
        mask_row = mask_ref[pl.ds(i, 1), :]
        mixed_left = mixed_cells[pl.ds(i, B, stride=I), :].astype(BF16)
        term = tn(mixed_left, right_rows) + outer_bias
        first = (pair_ref[i].astype(F32).T + mask_row * term).astype(BF16)
        first_ref[i] = first
        send_factors(
            first.astype(F32), mask_row, gain, bias, front_ref, left_cells, right_cells, i
        )
        return 0

    lax.fori_loop(0, I, step, 0)
    cells_out(left_cells, left_ref)
    cells_out(right_cells, right_ref)


def middle_kernel(
    product_ref,
    first_ref,
    mask_ref,
    gain0_ref,
    bias0_ref,
    front0_ref,
    out_gain0_ref,
    out_bias0_ref,
    out0_ref,
    gain1_ref,
    bias1_ref,
    front1_ref,
    second_ref,
    left_ref,
    right_ref,
    product_cells,
    left_cells,
    right_cells,
):
    cells_in(product_ref, product_cells)
    gain0, bias0, gain1, bias1 = wide(gain0_ref), wide(bias0_ref), wide(gain1_ref), wide(bias1_ref)
    out_gain0, out_bias0 = wide(out_gain0_ref), wide(out_bias0_ref)

    def step(i, _):
        mask_row = mask_ref[pl.ds(i, 1), :]
        product_standard, _ = norm(get_row(product_cells, i))
        product_norm = (product_standard * out_gain0 + out_bias0).astype(BF16)
        linear = tn(out0_ref[...], product_norm)
        first = first_ref[i].astype(F32)
        standard, _ = norm(first)
        normed = (standard * gain0 + bias0).astype(BF16)
        gate = sigmoid(nn(front0_ref[4 * C :, :], normed))
        second = (first + gate * linear).astype(BF16)
        second_ref[i] = second
        send_factors(
            second.astype(F32), mask_row, gain1, bias1, front1_ref, left_cells, right_cells, i
        )
        return 0

    lax.fori_loop(0, I, step, 0)
    cells_out(left_cells, left_ref)
    cells_out(right_cells, right_ref)


def back_out(cotangent, product, pair_in, gain, bias, front_ref, out_gain, out_bias, out_ref, sums):
    out_sum, out_gain_sum, out_bias_sum = sums
    product_standard, product_inverse = norm(product)
    product_norm = (product_standard * out_gain + out_bias).astype(BF16)
    linear = tn(out_ref[...], product_norm)
    standard, _ = norm(pair_in)
    normed = (standard * gain + bias).astype(BF16)
    gate = sigmoid(nn(front_ref[4 * C :, :], normed))
    linear_grad = (cotangent * gate).astype(BF16)
    gate_grad = (cotangent * linear * gate * (1.0 - gate)).astype(BF16)
    out_sum[...] += nt(product_norm, linear_grad)
    norm_grad = nn(out_ref[...], linear_grad)
    out_gain_sum[...] += norm_grad * product_standard
    out_bias_sum[...] += norm_grad
    return gate_grad, norm_back(norm_grad * out_gain, product_standard, product_inverse)


def back_in(
    cotangent,
    gate_grad,
    left_grad,
    right_grad,
    pair_in,
    mask_row,
    gain,
    bias,
    front_ref,
    back_ref,
    sums,
):
    front_sum, gain_sum, bias_sum = sums
    standard, inverse = norm(pair_in)
    normed = (standard * gain + bias).astype(BF16)
    projected = nn(front_ref[: 4 * C, :], normed)
    grads = []
    for at, side in ((0, left_grad), (2 * C, right_grad)):
        gate = sigmoid(projected[at : at + C])
        masked = side * mask_row * gate
        grads.append((masked * projected[at + C : at + 2 * C] * (1.0 - gate)).astype(BF16))
        grads.append(masked.astype(BF16))
    grads = jnp.concatenate(grads + [gate_grad], axis=0)
    front_sum[...] += nt(normed, grads)
    normed_grad = nn(back_ref[...], grads)
    gain_sum[...] += normed_grad * standard
    bias_sum[...] += normed_grad
    return (cotangent + norm_back(normed_grad * gain, standard, inverse)).astype(BF16)


def clear(*refs):
    for ref in refs:
        ref[...] = jnp.zeros(ref.shape, ref.dtype)


def columns(*refs):
    made = [jnp.sum(ref[...], axis=1, keepdims=True) for ref in refs]
    lane = lax.broadcasted_iota(jnp.int32, (C, C), 1)
    total = jnp.zeros((C, C), F32)
    for n, column in enumerate(made):
        total = jnp.where(lane == n, column, total)
    return total


def back_second_kernel(
    product_ref,
    second_ref,
    cotangent_ref,
    gain_ref,
    bias_ref,
    front_ref,
    out_gain_ref,
    out_bias_ref,
    out_ref,
    grad_ref,
    gate_grad_ref,
    out_sum,
    small_ref,
    product_cells,
    grad_cells,
    out_gain_sum,
    out_bias_sum,
):
    cells_in(product_ref, product_cells)
    gain, bias = wide(gain_ref), wide(bias_ref)
    out_gain, out_bias = wide(out_gain_ref), wide(out_bias_ref)
    clear(out_sum, out_gain_sum, out_bias_sum)

    def step(i, _):
        gate_grad, product_grad = back_out(
            cotangent_ref[i].astype(F32).T,
            get_row(product_cells, i),
            second_ref[i].astype(F32),
            gain,
            bias,
            front_ref,
            out_gain,
            out_bias,
            out_ref,
            (out_sum, out_gain_sum, out_bias_sum),
        )
        gate_grad_ref[i] = gate_grad
        put_row(grad_cells, i, product_grad)
        return 0

    lax.fori_loop(0, I, step, 0)
    cells_out(grad_cells, grad_ref)
    small_ref[...] = columns(out_gain_sum, out_bias_sum)


def back_middle_kernel(
    left_ref,
    right_ref,
    second_ref,
    cotangent_ref,
    gate_grad1_ref,
    product_ref,
    first_ref,
    mask_ref,
    gain1_ref,
    bias1_ref,
    front1_ref,
    back1_ref,
    gain0_ref,
    bias0_ref,
    front0_ref,
    out_gain0_ref,
    out_bias0_ref,
    out0_ref,
    grad_second_ref,
    grad_ref,
    gate_grad0_ref,
    front_sum,
    out_sum,
    small_ref,
    left_cells,
    right_cells,
    product_cells,
    grad_cells,
    gain_sum,
    bias_sum,
    out_gain_sum,
    out_bias_sum,
):
    cells_in(left_ref, left_cells)
    cells_in(right_ref, right_cells)
    cells_in(product_ref, product_cells)
    gain1, bias1, gain0, bias0 = wide(gain1_ref), wide(bias1_ref), wide(gain0_ref), wide(bias0_ref)
    out_gain0, out_bias0 = wide(out_gain0_ref), wide(out_bias0_ref)
    clear(front_sum, out_sum, gain_sum, bias_sum, out_gain_sum, out_bias_sum)

    def step(i, _):
        grad_second = back_in(
            cotangent_ref[i].astype(F32).T,
            gate_grad1_ref[i],
            get_row(left_cells, i),
            get_row(right_cells, i),
            second_ref[i].astype(F32),
            mask_ref[pl.ds(i, 1), :],
            gain1,
            bias1,
            front1_ref,
            back1_ref,
            (front_sum, gain_sum, bias_sum),
        )
        grad_second_ref[i] = grad_second
        gate_grad, product_grad = back_out(
            grad_second.astype(F32),
            get_row(product_cells, i),
            first_ref[i].astype(F32),
            gain0,
            bias0,
            front0_ref,
            out_gain0,
            out_bias0,
            out0_ref,
            (out_sum, out_gain_sum, out_bias_sum),
        )
        gate_grad0_ref[i] = gate_grad
        put_row(grad_cells, i, product_grad)
        return 0

    lax.fori_loop(0, I, step, 0)
    cells_out(grad_cells, grad_ref)
    small_ref[...] = columns(gain_sum, bias_sum, out_gain_sum, out_bias_sum)


def back_first_kernel(
    left_ref,
    right_ref,
    first_ref,
    grad_second_ref,
    gate_grad_ref,
    mask_ref,
    every_ref,
    own_both_ref,
    cube_ref,
    gain_ref,
    bias_ref,
    front_ref,
    back_ref,
    pair_grad_ref,
    front_sum,
    small_ref,
    cube_sum_ref,
    left_single_ref,
    right_total_ref,
    left_cells,
    right_cells,
    mixed_cells,
    outer_cells,
    gain_sum,
    bias_sum,
    outer_bias_sum,
    right_total,
):
    cells_in(left_ref, left_cells)
    cells_in(right_ref, right_cells)
    right_rows = every_ref[...].astype(F32).T[B : 2 * B].astype(BF16)
    own_left = own_both_ref[:, :B]
    mixed_rows(own_left, cube_ref, mixed_cells)
    gain, bias = wide(gain_ref), wide(bias_ref)
    clear(front_sum, gain_sum, bias_sum, outer_bias_sum, right_total)

    def step(i, _):
        mask_row = mask_ref[pl.ds(i, 1), :]
        grad_first = back_in(
            grad_second_ref[i].astype(F32),
            gate_grad_ref[i],
            get_row(left_cells, i),
            get_row(right_cells, i),
            first_ref[i].astype(F32),
            mask_row,
            gain,
            bias,
            front_ref,
            back_ref,
            (front_sum, gain_sum, bias_sum),
        ).astype(F32)
        pair_grad_ref[i] = grad_first.T.astype(BF16)
        outer_grad = grad_first * mask_row
        outer_bias_sum[...] += outer_grad
        outer_grad = outer_grad.astype(BF16)
        outer_cells[pl.ds(i, B, stride=I), :] = nt(right_rows, outer_grad)
        mixed_left = mixed_cells[pl.ds(i, B, stride=I), :].astype(BF16)
        right_total[:B, :] += nn(mixed_left, outer_grad)
        return 0

    lax.fori_loop(0, I, step, 0)
    small_ref[...] = columns(gain_sum, bias_sum, outer_bias_sum)
    left_single = jnp.zeros((I, B), F32)
    for b in range(B):
        rows = outer_cells[b * I : (b + 1) * I, :].astype(BF16)
        cube_sum_ref[b * B : (b + 1) * B, :] = tn(own_left, rows)
        left_single += nt(rows, cube_ref[:, b * C : (b + 1) * C])
    left_single_ref[...] = jnp.concatenate([left_single, jnp.zeros((I, C - B), F32)], axis=1)
    right_total_ref[...] = right_total[...].T


class Place:
    def __init__(self):
        self.me = lax.axis_index("axial")
        self.dp = lax.axis_index("dp")
        self.half = lax.rem(self.me // 2, 2)
        self.group = (self.me // 4) * 2 + lax.rem(self.me, 2)
        self.other = self.me + 2 - 4 * self.half

    def axial(self, group):
        return (group // 2) * 4 + self.half * 2 + lax.rem(group, 2)

    def peer(self, t):
        return lax.rem(self.group + t, 8)

    def greet(self):
        barrier = pltpu.get_barrier_semaphore()

        def signal(t, _):
            pl.semaphore_signal(
                barrier,
                inc=1,
                device_id=(self.dp, self.axial(self.peer(t))),
                device_id_type=MESH,
            )
            return 0

        lax.fori_loop(1, 8, signal, 0)
        pl.semaphore_signal(barrier, inc=1, device_id=(self.dp, self.other), device_id_type=MESH)
        pl.semaphore_wait(barrier, 8)

    def to_group(self, source, target, send_sem, recv_sem, t):
        group = self.peer(t)
        return pltpu.make_async_remote_copy(
            src_ref=source(group),
            dst_ref=target,
            send_sem=send_sem.at[t],
            recv_sem=recv_sem.at[t],
            device_id=(self.dp, self.axial(group)),
            device_id_type=MESH,
        )

    def to_half(self, source, target, send_sem, recv_sem):
        return pltpu.make_async_remote_copy(
            src_ref=source,
            dst_ref=target,
            send_sem=send_sem,
            recv_sem=recv_sem,
            device_id=(self.dp, self.other),
            device_id_type=MESH,
        )


def each_peer(do):
    def step(t, _):
        do(t)
        return 0

    lax.fori_loop(1, 8, step, 0)


def each_piece(do):
    def step(q, _):
        do(q)
        return 0

    lax.fori_loop(0, Q, step, 0)


def each_channel(q, do):
    def step(n, _):
        do(q * CQ + n)
        return 0

    lax.fori_loop(0, CQ, step, 0)


def rows_of(at, count=I):
    return pl.ds(pl.multiple_of(at, 16), count)


class Spread:
    def __init__(self, place, source, target, row, sems, at):
        self.place, self.source, self.target, self.row = place, source, target, row
        self.send_sem, self.recv_sem, self.local_sem = sems
        self.at = at

    def copy(self, q, t):
        return self.place.to_group(
            lambda group: self.source.at[pl.ds(group * 16 + q * CQ, CQ)],
            self.target.at[pl.ds(q * CQ, CQ), rows_of(self.row)],
            self.send_sem.at[self.at, q],
            self.recv_sem.at[self.at, q],
            t,
        )

    def local(self):
        return pltpu.make_async_copy(
            self.source.at[pl.ds(self.place.group * 16, 16)],
            self.target.at[:, rows_of(self.row)],
            self.local_sem.at[self.at],
        )

    def send(self, q):
        each_peer(lambda t: self.copy(q, t).start())

    def arrive(self, q):
        each_peer(lambda t: self.copy(q, t).wait_recv())

    def sent(self):
        each_piece(lambda q: each_peer(lambda t: self.copy(q, t).wait_send()))


class Collect:
    def __init__(self, place, source, target, sems, at):
        self.place, self.source, self.target = place, source, target
        self.send_sem, self.recv_sem, self.local_sem = sems
        self.at = at

    def copy(self, q, t):
        return self.place.to_group(
            lambda group: self.source.at[pl.ds(q * CQ, CQ), rows_of(group * I)],
            self.target.at[pl.ds(self.place.group * 16 + q * CQ, CQ)],
            self.send_sem.at[self.at, q],
            self.recv_sem.at[self.at, q],
            t,
        )

    def local(self):
        return pltpu.make_async_copy(
            self.source.at[:, rows_of(self.place.group * I)],
            self.target.at[pl.ds(self.place.group * 16, 16)],
            self.local_sem.at[self.at],
        )

    def send(self, q):
        each_peer(lambda t: self.copy(q, t).start())

    def finish(self):
        each_piece(lambda q: each_peer(lambda t: self.copy(q, t).wait()))


def swap_rows(place, target, send_sem, recv_sem, q, x):
    rows = rows_of(x * 64 + place.half * 32, 32)
    block = target.at[pl.ds(q * CQ, CQ), rows]
    return place.to_half(block, block, send_sem.at[q, x], recv_sem.at[q, x])


def each_x(do):
    def step(x, _):
        do(x)
        return 0

    lax.fori_loop(0, 4, step, 0)


def split_halves(place, whole, kept, sent, channel):
    for x in range(4):
        kept[channel, x * 32 : (x + 1) * 32, :] = whole[
            pl.ds(pl.multiple_of(x * 64 + place.half * 32, 32), 32), :
        ]
        sent[channel, x * 32 : (x + 1) * 32, :] = whole[
            pl.ds(pl.multiple_of(x * 64 + 32 - place.half * 32, 32), 32), :
        ].astype(BF16)


def swap_sums(place, sent, received, send_sem, recv_sem, q):
    piece = pl.ds(q * CQ, CQ)
    return place.to_half(
        sent.at[piece], received.at[piece], send_sem.at[q, 0], recv_sem.at[q, 0]
    )


def outgoing_kernel(
    left_ref,
    right_ref,
    left_kept,
    right_kept,
    product_ref,
    staged,
    send_sem,
    recv_sem,
    local_sem,
    half_send,
    half_recv,
):
    place = Place()
    sems = (send_sem, recv_sem, local_sem)
    right = Spread(place, right_ref, right_kept, place.me * I, sems, 0)
    left = Spread(place, left_ref, left_kept, place.group * I, sems, 1)
    product = Collect(place, staged, product_ref, sems, 2)
    right.local().start()
    left.local().start()
    place.greet()
    each_piece(right.send)
    each_piece(left.send)
    right.local().wait()
    left.local().wait()

    def forward(q):
        right.arrive(q)
        each_x(lambda x: swap_rows(place, right_kept, half_send, half_recv, q, x).start())

    each_piece(forward)

    def multiply(q):
        left.arrive(q)
        each_x(lambda x: swap_rows(place, right_kept, half_send, half_recv, q, x).wait_recv())

        def one(c):
            staged[c] = nt(left_kept[c], right_kept[c]).astype(BF16)

        each_channel(q, one)
        product.send(q)

    each_piece(multiply)
    product.local().start()
    right.sent()
    left.sent()
    each_piece(
        lambda q: each_x(
            lambda x: swap_rows(place, right_kept, half_send, half_recv, q, x).wait_send()
        )
    )
    product.local().wait()
    product.finish()


def incoming_kernel(
    left_ref,
    right_ref,
    left_kept,
    right_kept,
    product_ref,
    staged,
    whole,
    kept_sum,
    sent_sum,
    received_sum,
    send_sem,
    recv_sem,
    local_sem,
    half_send,
    half_recv,
):
    place = Place()
    sems = (send_sem, recv_sem, local_sem)
    right = Spread(place, right_ref, right_kept, place.group * I, sems, 0)
    left = Spread(place, left_ref, left_kept, place.group * I, sems, 1)
    product = Collect(place, staged, product_ref, sems, 2)
    right.local().start()
    left.local().start()
    place.greet()

    def begin(q):
        left.send(q)
        right.send(q)

    each_piece(begin)
    right.local().wait()
    left.local().wait()

    def multiply(q):
        left.arrive(q)
        right.arrive(q)

        def one(c):
            whole[...] = tn(left_kept[c], right_kept[c])
            split_halves(place, whole, kept_sum, sent_sum, c)

        each_channel(q, one)
        swap_sums(place, sent_sum, received_sum, half_send, half_recv, q).start()

    each_piece(multiply)

    def add(q):
        swap_sums(place, sent_sum, received_sum, half_send, half_recv, q).wait_recv()

        def one(c):
            staged[c] = (kept_sum[c] + received_sum[c].astype(F32)).astype(BF16)

        each_channel(q, one)
        product.send(q)

    each_piece(add)
    product.local().start()
    right.sent()
    left.sent()
    each_piece(
        lambda q: swap_sums(place, sent_sum, received_sum, half_send, half_recv, q).wait_send()
    )
    product.local().wait()
    product.finish()


def incoming_back_kernel(
    grad_ref,
    left_kept,
    right_kept,
    left_ref,
    right_ref,
    grad_every,
    left_staged,
    right_staged,
    send_sem,
    recv_sem,
    local_sem,
    half_send,
    half_recv,
):
    place = Place()
    sems = (send_sem, recv_sem, local_sem)
    grad = Spread(place, grad_ref, grad_every, place.me * I, sems, 0)
    left = Collect(place, left_staged, left_ref, sems, 1)
    right = Collect(place, right_staged, right_ref, sems, 2)
    grad.local().start()
    place.greet()
    each_piece(grad.send)
    grad.local().wait()

    def forward(q):
        grad.arrive(q)
        each_x(lambda x: swap_rows(place, grad_every, half_send, half_recv, q, x).start())

    each_piece(forward)

    def multiply(q):
        each_x(lambda x: swap_rows(place, grad_every, half_send, half_recv, q, x).wait_recv())

        def one(c):
            left_staged[c] = nt(right_kept[c], grad_every[c]).astype(BF16)
            right_staged[c] = nn(left_kept[c], grad_every[c]).astype(BF16)

        each_channel(q, one)
        left.send(q)
        right.send(q)

    each_piece(multiply)
    left.local().start()
    right.local().start()
    grad.sent()
    each_piece(
        lambda q: each_x(
            lambda x: swap_rows(place, grad_every, half_send, half_recv, q, x).wait_send()
        )
    )
    left.local().wait()
    right.local().wait()
    left.finish()
    right.finish()


def outgoing_back_kernel(
    grad_ref,
    left_kept,
    right_kept,
    left_ref,
    right_ref,
    grad_half,
    left_staged,
    right_staged,
    whole,
    kept_sum,
    sent_sum,
    received_sum,
    send_sem,
    recv_sem,
    local_sem,
    half_send,
    half_recv,
):
    place = Place()
    sems = (send_sem, recv_sem, local_sem)
    grad = Spread(place, grad_ref, grad_half, place.group * I, sems, 0)
    left = Collect(place, left_staged, left_ref, sems, 1)
    right = Collect(place, right_staged, right_ref, sems, 2)
    grad.local().start()
    place.greet()
    each_piece(grad.send)
    grad.local().wait()

    def multiply(q):
        grad.arrive(q)

        def one(c):
            whole[...] = tn(grad_half[c], left_kept[c])
            split_halves(place, whole, kept_sum, sent_sum, c)
            left_staged[c] = nn(grad_half[c], right_kept[c]).astype(BF16)

        each_channel(q, one)
        swap_sums(place, sent_sum, received_sum, half_send, half_recv, q).start()
        left.send(q)

    each_piece(multiply)

    def add(q):
        swap_sums(place, sent_sum, received_sum, half_send, half_recv, q).wait_recv()

        def one(c):
            right_staged[c] = (kept_sum[c] + received_sum[c].astype(F32)).astype(BF16)

        each_channel(q, one)
        right.send(q)

    each_piece(add)
    left.local().start()
    right.local().start()
    grad.sent()
    each_piece(
        lambda q: swap_sums(place, sent_sum, received_sum, half_send, half_recv, q).wait_send()
    )
    left.local().wait()
    right.local().wait()
    left.finish()
    right.finish()


def total_kernel(
    scale,
    right_total_ref,
    left_single_ref,
    single_ref,
    gain_ref,
    bias_ref,
    weight_ref,
    own_ref,
    front0_sum,
    front1_sum,
    out0_sum,
    out1_sum,
    cube_sum,
    small_ref,
    single_grad_ref,
    total_ref,
    packed,
    right_parts,
    pair_part,
    chip_sum,
    chip_parts,
    dp_parts,
    right_send,
    right_recv,
    core_sem,
    chip_send,
    chip_recv,
    dp_send,
    dp_recv,
    back_send,
    back_recv,
    last_send,
    last_recv,
):
    me = lax.axis_index("axial")
    dp = lax.axis_index("dp")
    core = lax.rem(me, 2)
    chip = me // 2
    sibling = me + 1 - 2 * core
    barrier = pltpu.get_barrier_semaphore()

    def greet(t, _):
        pl.semaphore_signal(
            barrier, inc=1, device_id=(dp, lax.rem(me + t, 16)), device_id_type=MESH
        )
        return 0

    def greet_dp(t, _):
        pl.semaphore_signal(
            barrier, inc=1, device_id=(lax.rem(dp + t, 8), me), device_id_type=MESH
        )
        return 0

    lax.fori_loop(1, 16, greet, 0)
    lax.fori_loop(1, 8, greet_dp, 0)

    def put(at, value):
        count = value.shape[0]
        while count:
            room = min(count, PART - at % PART)
            packed[at // PART, at % PART : at % PART + room, :] = value[:room].astype(BF16)
            at, value, count = at + room, value[room:], count - room

    for n in range(5):
        put(n * C, front0_sum[:, n * C : (n + 1) * C])
        put((5 + n) * C, front1_sum[:, n * C : (n + 1) * C])
    put(10 * C, out0_sum[...])
    put(11 * C, out1_sum[...])
    put(12 * C, cube_sum[...])
    put(24 * C, small_ref[...])
    standard, inverse = norm(single_ref[...].astype(F32), axis=1)
    normed = (standard * gain_ref[...] + bias_ref[...]).astype(BF16)
    pl.semaphore_wait(barrier, 22)

    def right_copy(t):
        target = lax.rem(me + t, 16)
        return pltpu.make_async_remote_copy(
            src_ref=right_total_ref.at[rows_of(target * I)],
            dst_ref=right_parts.at[t],
            send_sem=right_send.at[t],
            recv_sem=right_recv.at[t],
            device_id=(dp, target),
            device_id_type=MESH,
        )

    def loop(first, last, do):
        def step(t, _):
            do(t)
            return 0

        lax.fori_loop(first, last, step, 0)

    loop(1, 16, lambda t: right_copy(t).start())
    loop(1, 16, lambda t: right_copy(t).wait_recv())
    right_single = right_total_ref[rows_of(me * I), :]
    for t in range(1, 16):
        right_single += right_parts[t]
    both = jnp.concatenate(
        [left_single_ref[:, :B], right_single[:, :B], jnp.zeros((I, C - 2 * B), F32)], axis=1
    )
    both = (both * own_ref[...]).astype(BF16)
    single_grad = nt(both, weight_ref[...])
    gain_sum = jnp.sum(single_grad * standard, axis=0, keepdims=True)
    bias_sum = jnp.sum(single_grad, axis=0, keepdims=True)
    single_grad_ref[...] = norm_back(
        single_grad * gain_ref[...], standard, inverse, axis=1
    ).astype(BF16)
    factor_sums = tn(both, normed)
    for n in range(8):
        put(20 * C + n * 64, factor_sums[:64, n * C : (n + 1) * C])
    tail = [gain_sum[:, n * C : (n + 1) * C] for n in range(8)]
    tail += [bias_sum[:, n * C : (n + 1) * C] for n in range(8)]
    put(25 * C, jnp.concatenate(tail + [jnp.zeros((C - 16, C), F32)], axis=0))

    pair_copy = pltpu.make_async_remote_copy(
        src_ref=packed.at[pl.ds(8 - 8 * core, 8)],
        dst_ref=pair_part,
        send_sem=core_sem.at[0],
        recv_sem=core_sem.at[1],
        device_id=(dp, sibling),
        device_id_type=MESH,
    )
    pair_copy.start()
    pair_copy.wait()

    def chip_copy(t):
        target = lax.rem(chip + t, 8)
        return pltpu.make_async_remote_copy(
            src_ref=chip_sum.at[target],
            dst_ref=chip_parts.at[t],
            send_sem=chip_send.at[t],
            recv_sem=chip_recv.at[t],
            device_id=(dp, target * 2 + core),
            device_id_type=MESH,
        )

    def add_pair(t):
        n = lax.rem(chip + t, 8)
        chip_sum[n] = (packed[core * 8 + n].astype(F32) + pair_part[n].astype(F32)).astype(BF16)

    def add_and_send(t):
        add_pair(t)
        chip_copy(t).start()

    loop(1, 8, add_and_send)
    add_pair(0)
    loop(1, 8, lambda t: chip_copy(t).wait_recv())
    total = chip_sum[chip].astype(F32)
    for t in range(1, 8):
        total += chip_parts[t].astype(F32)
    dp_parts[dp] = total.astype(BF16)

    def dp_copy(t):
        return pltpu.make_async_remote_copy(
            src_ref=dp_parts.at[dp],
            dst_ref=dp_parts.at[dp],
            send_sem=dp_send.at[t],
            recv_sem=dp_recv.at[t],
            device_id=(lax.rem(dp + t, 8), me),
            device_id_type=MESH,
        )

    loop(1, 8, lambda t: dp_copy(t).start())
    loop(1, 8, lambda t: dp_copy(t).wait_recv())
    total = dp_parts[0].astype(F32)
    for n in range(1, 8):
        total += dp_parts[n].astype(F32)
    total_ref[core * 8 + chip] = (total * scale).astype(BF16)

    def back_copy(t):
        block = total_ref.at[core * 8 + chip]
        return pltpu.make_async_remote_copy(
            src_ref=block,
            dst_ref=block,
            send_sem=back_send.at[t],
            recv_sem=back_recv.at[t],
            device_id=(dp, lax.rem(chip + t, 8) * 2 + core),
            device_id_type=MESH,
        )

    def last_copy(t):
        block = total_ref.at[core * 8 + lax.rem(chip + 8 - t, 8)]
        return pltpu.make_async_remote_copy(
            src_ref=block,
            dst_ref=block,
            send_sem=last_send.at[t],
            recv_sem=last_recv.at[t],
            device_id=(dp, sibling),
            device_id_type=MESH,
        )

    loop(1, 8, lambda t: back_copy(t).start())
    last_copy(0).start()

    def pass_on(t):
        back_copy(t).wait_recv()
        last_copy(t).start()

    loop(1, 8, pass_on)
    loop(0, 8, lambda t: last_copy(t).wait())
    loop(1, 8, lambda t: back_copy(t).wait_send())
    loop(1, 8, lambda t: dp_copy(t).wait_send())
    loop(1, 8, lambda t: chip_copy(t).wait_send())
    loop(1, 16, lambda t: right_copy(t).wait_send())


def unpack_kernel(
    total_ref,
    outer_gain_ref,
    outer_bias_ref,
    outer_left_ref,
    outer_right_ref,
    cube_ref,
    pair_bias_ref,
    norm_gain_ref,
    norm_bias_ref,
    proj_ref,
    gate_ref,
    out_gain_ref,
    out_bias_ref,
    out_ref,
):
    for t in range(2):
        for n in range(4):
            at = (5 * t + n) * C
            proj_ref[t, :, n * C : (n + 1) * C] = total_ref[at : at + C, :].astype(F32)
        at = (5 * t + 4) * C
        gate_ref[t] = total_ref[at : at + C, :].astype(F32)
        out_ref[t] = total_ref[(10 + t) * C : (11 + t) * C, :].astype(F32)
    cube = total_ref[12 * C : 20 * C, :].astype(F32).reshape(B, B, C)
    cube_ref[...] = jnp.swapaxes(cube, 0, 1).reshape(B * B, C)
    for n in range(8):
        at = 20 * C + n * 64
        block = jnp.concatenate(
            [total_ref[at : at + 64, :].astype(F32), jnp.zeros((64, C), F32)], axis=0
        ).T
        outer_left_ref[n * C : (n + 1) * C, :] = block[:, :B]
        outer_right_ref[n * C : (n + 1) * C, :] = block[:, B : 2 * B]
    small = total_ref[24 * C : 25 * C, :].astype(F32).T
    for t in range(2):
        norm_gain_ref[t : t + 1, :] = small[4 * t : 4 * t + 1]
        norm_bias_ref[t : t + 1, :] = small[4 * t + 1 : 4 * t + 2]
        out_gain_ref[t : t + 1, :] = small[4 * t + 2 : 4 * t + 3]
        out_bias_ref[t : t + 1, :] = small[4 * t + 3 : 4 * t + 4]
    pair_bias_ref[...] = small[8:9]
    rows = total_ref[25 * C : 25 * C + 16, :].astype(F32)
    outer_gain_ref[...] = rows[:8]
    outer_bias_ref[...] = rows[8:16]


def call(kernel, outs, scratch, args, name, collective=None, flops=0):
    return pl.pallas_call(
        kernel,
        out_shape=[jax.ShapeDtypeStruct(shape, dtype) for shape, dtype in outs],
        in_specs=[pl.BlockSpec(memory_space=pltpu.VMEM)] * len(args),
        out_specs=[pl.BlockSpec(memory_space=pltpu.VMEM)] * len(outs),
        scratch_shapes=scratch,
        name=name,
        compiler_params=pltpu.CompilerParams(
            collective_id=collective,
            has_side_effects=collective is not None,
            vmem_limit_bytes=VMEM_LIMIT,
        ),
    )(*args)


CELLS = pltpu.VMEM((2, C * I, C), F32)
SUMS = pltpu.VMEM((C, J), F32)
DMA = pltpu.SemaphoreType.DMA
EXCHANGE_SEMS = [DMA((3, Q, 8)), DMA((3, Q, 8)), DMA((3,)), DMA((Q, 4)), DMA((Q, 4))]
BY_CHANNEL = ((C, I, J), BF16)
BY_ROW = ((I, C, J), BF16)
HALF = (16, C, J)
EVERY = (16, J, J)


def local(
    single_state,
    pair_state,
    residue_mask,
    pair_cotangent,
    outer_norm_gain,
    outer_norm_bias,
    outer_left,
    outer_right,
    outer_proj,
    outer_bias,
    triangle_norm_gain,
    triangle_norm_bias,
    triangle_proj,
    triangle_gate,
    triangle_out_gain,
    triangle_out_bias,
    triangle_out,
):
    me = lax.axis_index("axial")
    weight = residue_mask[0].astype(F32)
    own = lax.dynamic_slice_in_dim(weight, me * I, I)[:, None]
    mask = own * weight[None, :]
    own_wide = jnp.broadcast_to(own, (I, C))
    factor_weight = jnp.concatenate(
        [outer_left, outer_right, jnp.zeros((outer_left.shape[0], C - 2 * B), BF16)], axis=1
    )
    single = single_state[0]
    single_gain, single_bias = outer_norm_gain[None, :], outer_norm_bias[None, :]
    cube = outer_proj.reshape(B, B * C)
    back_weight = jnp.concatenate([triangle_proj, triangle_gate], axis=2)
    front_weight = jnp.swapaxes(back_weight, 1, 2)
    gains = [triangle_norm_gain[t][:, None] for t in range(2)]
    biases = [triangle_norm_bias[t][:, None] for t in range(2)]
    out_gains = [triangle_out_gain[t][:, None] for t in range(2)]
    out_biases = [triangle_out_bias[t][:, None] for t in range(2)]
    fronts = [front_weight[t] for t in range(2)]
    backs = [back_weight[t] for t in range(2)]
    outs = [triangle_out[t] for t in range(2)]

    (every,) = call(
        head_kernel,
        [((J, C), BF16)],
        [DMA((16,)), DMA((16,))],
        (single, single_gain, single_bias, factor_weight, own_wide),
        "head",
        collective=0,
    )
    own_both = lax.dynamic_slice_in_dim(every, me * I, I)
    mixed_scratch = pltpu.VMEM((B * I, C), F32)
    first, left0, right0 = call(
        front_first_kernel,
        [BY_ROW, BY_CHANNEL, BY_CHANNEL],
        [CELLS, CELLS, mixed_scratch],
        (
            pair_state[0],
            every,
            own_both,
            cube,
            mask,
            outer_bias[:, None],
            gains[0],
            biases[0],
            fronts[0],
        ),
        "front_first",
    )
    left0_kept, right0_kept, product0 = call(
        outgoing_kernel,
        [(HALF, BF16), (EVERY, BF16), BY_CHANNEL],
        [pltpu.VMEM(HALF, BF16)] + EXCHANGE_SEMS,
        (left0, right0),
        "outgoing",
        collective=1,
    )
    second, left1, right1 = call(
        middle_kernel,
        [BY_ROW, BY_CHANNEL, BY_CHANNEL],
        [CELLS, CELLS, CELLS],
        (
            product0,
            first,
            mask,
            gains[0],
            biases[0],
            fronts[0],
            out_gains[0],
            out_biases[0],
            outs[0],
            gains[1],
            biases[1],
            fronts[1],
        ),
        "middle",
    )
    sum_scratch = [
        pltpu.VMEM((J, J), F32),
        pltpu.VMEM(HALF, F32),
        pltpu.VMEM(HALF, BF16),
        pltpu.VMEM(HALF, BF16),
    ]
    left1_kept, right1_kept, product1 = call(
        incoming_kernel,
        [(HALF, BF16), (HALF, BF16), BY_CHANNEL],
        [pltpu.VMEM(HALF, BF16)] + sum_scratch + EXCHANGE_SEMS,
        (left1, right1),
        "incoming",
        collective=2,
    )
    cotangent = pair_cotangent[0]
    product_grad1, gate_grad1, out1_sum, small1 = call(
        back_second_kernel,
        [BY_CHANNEL, BY_ROW, ((C, C), F32), ((C, C), F32)],
        [CELLS, CELLS, SUMS, SUMS],
        (
            product1,
            second,
            cotangent,
            gains[1],
            biases[1],
            fronts[1],
            out_gains[1],
            out_biases[1],
            outs[1],
        ),
        "back_second",
    )
    left_grad1, right_grad1 = call(
        incoming_back_kernel,
        [BY_CHANNEL, BY_CHANNEL],
        [pltpu.VMEM(EVERY, BF16), pltpu.VMEM(HALF, BF16), pltpu.VMEM(HALF, BF16)] + EXCHANGE_SEMS,
        (product_grad1, left1_kept, right1_kept),
        "incoming_back",
        collective=3,
    )
    grad_second, product_grad0, gate_grad0, front1_sum, out0_sum, small_middle = call(
        back_middle_kernel,
        [
            BY_ROW,
            BY_CHANNEL,
            BY_ROW,
            ((C, 5 * C), F32),
            ((C, C), F32),
            ((C, C), F32),
        ],
        [CELLS, CELLS, CELLS, CELLS, SUMS, SUMS, SUMS, SUMS],
        (
            left_grad1,
            right_grad1,
            second,
            cotangent,
            gate_grad1,
            product0,
            first,
            mask,
            gains[1],
            biases[1],
            fronts[1],
            backs[1],
            gains[0],
            biases[0],
            fronts[0],
            out_gains[0],
            out_biases[0],
            outs[0],
        ),
        "back_middle",
    )
    left_grad0, right_grad0 = call(
        outgoing_back_kernel,
        [BY_CHANNEL, BY_CHANNEL],
        [pltpu.VMEM(HALF, BF16), pltpu.VMEM(HALF, BF16), pltpu.VMEM(HALF, BF16)]
        + sum_scratch
        + EXCHANGE_SEMS,
        (product_grad0, left0_kept, right0_kept),
        "outgoing_back",
        collective=4,
    )
    pair_gradient, front0_sum, small0, cube_sum, left_single, right_total = call(
        back_first_kernel,
        [
            ((I, J, C), BF16),
            ((C, 5 * C), F32),
            ((C, C), F32),
            ((B * B, C), F32),
            ((I, C), F32),
            ((J, C), F32),
        ],
        [
            CELLS,
            CELLS,
            mixed_scratch,
            mixed_scratch,
            SUMS,
            SUMS,
            SUMS,
            pltpu.VMEM((C, J), F32),
        ],
        (
            left_grad0,
            right_grad0,
            first,
            grad_second,
            gate_grad0,
            mask,
            every,
            own_both,
            cube,
            gains[0],
            biases[0],
            fronts[0],
            backs[0],
        ),
        "back_first",
    )
    small = jnp.concatenate(
        [
            small0[:, :2],
            small_middle[:, 2:4],
            small_middle[:, :2],
            small1[:, :2],
            small0[:, 2:3],
            jnp.zeros((C, C - 9), F32),
        ],
        axis=1,
    )
    scale = 1.0 / float(lax.axis_size("dp") * J)
    part = (PART, C)
    single_gradient, total = call(
        functools.partial(total_kernel, scale),
        [((I, single.shape[1]), BF16), ((16,) + part, BF16)],
        [
            pltpu.VMEM((16,) + part, BF16),
            pltpu.VMEM((16, I, C), F32),
            pltpu.VMEM((8,) + part, BF16),
            pltpu.VMEM((8,) + part, BF16),
            pltpu.VMEM((8,) + part, BF16),
            pltpu.VMEM((8,) + part, BF16),
            DMA((16,)),
            DMA((16,)),
            DMA((2,)),
        ]
        + [DMA((8,))] * 8,
        (
            right_total,
            left_single,
            single,
            single_gain,
            single_bias,
            factor_weight,
            own_wide,
            front0_sum,
            front1_sum,
            out0_sum,
            out1_sum,
            cube_sum,
            small,
        ),
        "total",
        collective=5,
    )
    unpacked = call(
        unpack_kernel,
        [
            ((8, C), F32),
            ((8, C), F32),
            (outer_left.shape, F32),
            (outer_right.shape, F32),
            (outer_proj.shape, F32),
            ((1, C), F32),
            ((2, C), F32),
            ((2, C), F32),
            (triangle_proj.shape, F32),
            (triangle_gate.shape, F32),
            ((2, C), F32),
            ((2, C), F32),
            (triangle_out.shape, F32),
        ],
        [],
        (total.reshape(16 * PART, C),),
        "unpack",
    )
    unpacked = list(unpacked)
    unpacked[0] = unpacked[0].reshape(-1)
    unpacked[1] = unpacked[1].reshape(-1)
    unpacked[5] = unpacked[5].reshape(-1)
    return (single_gradient[None], pair_gradient[None]) + tuple(unpacked)


def solution(mesh):
    whole = P()
    rows = P("dp", "axial", None)
    cells = P("dp", "axial", None, None)
    return jax.shard_map(
        local,
        mesh=mesh,
        in_specs=(rows, cells, P("dp", None), cells) + (whole,) * 13,
        out_specs=(rows, cells) + (whole,) * 13,
        check_vma=False,
    )
```

```python
import functools

import jax
import jax.numpy as jnp
from jax import lax
from jax.experimental import pallas as pl
from jax.experimental.pallas import tpu as pltpu
from jax.sharding import PartitionSpec as P

EPSILON = 1e-05
F32 = jnp.float32
BF16 = jnp.bfloat16
MESH = pl.DeviceIdType.MESH
C = 128
I = 16
J = 256
B = 32
Q = 2
CQ = 8
PART = 208
VMEM_LIMIT = 60 * 2**20


def nn(a, b):
    return lax.dot_general(a, b, (((1,), (0,)), ((), ())), preferred_element_type=F32)


def nt(a, b):
    return lax.dot_general(a, b, (((1,), (1,)), ((), ())), preferred_element_type=F32)


def tn(a, b):
    return lax.dot_general(a, b, (((0,), (0,)), ((), ())), preferred_element_type=F32)


def sigmoid(x):
    return 0.5 * jnp.tanh(0.5 * x) + 0.5


def norm(x, axis=0):
    centred = x - jnp.mean(x, axis=axis, keepdims=True)
    variance = jnp.mean(centred * centred, axis=axis, keepdims=True)
    inverse = lax.rsqrt(variance + EPSILON)
    return centred * inverse, inverse


def norm_back(scaled, standard, inverse, axis=0):
    first = jnp.mean(scaled, axis=axis, keepdims=True)
    second = jnp.mean(scaled * standard, axis=axis, keepdims=True)
    return inverse * (scaled - first - standard * second)


def put_pair(cells, p, value):
    cells[pl.ds(2 * p, C, stride=I), :] = value[:, :C]
    cells[pl.ds(2 * p + 1, C, stride=I), :] = value[:, C:]


def get_pair(cells, p):
    return side_by_side(cells[pl.ds(2 * p, C, stride=I), :], cells[pl.ds(2 * p + 1, C, stride=I), :])


def side_by_side(a, b):
    return jnp.concatenate([a, b], axis=1)


def lanes(h):
    return slice(h * C, (h + 1) * C)


def cells_out(cells, out_ref, h):
    def step(n, _):
        part = cells[pl.ds(pl.multiple_of(n * 256, 256), 256), :]
        out_ref[pl.ds(n * 16, 16), :, lanes(h)] = part.reshape(16, I, C).astype(BF16)
        return 0

    lax.fori_loop(0, 8, step, 0)


def cells_in(in_ref, cells, h):
    def step(n, _):
        part = in_ref[pl.ds(n * 16, 16), :, lanes(h)]
        cells[pl.ds(pl.multiple_of(n * 256, 256), 256), :] = part.astype(F32).reshape(256, C)
        return 0

    lax.fori_loop(0, 8, step, 0)


def rows_in(ref, p, h):
    return side_by_side(
        ref[2 * p, lanes(h), :].astype(F32).T, ref[2 * p + 1, lanes(h), :].astype(F32).T
    )


def mask_pair(mask_ref, p, h):
    return side_by_side(
        mask_ref[h, pl.ds(2 * p, 1), :], mask_ref[h, pl.ds(2 * p + 1, 1), :]
    )


def wide(ref):
    return side_by_side(ref[...], ref[...])


def send_factors(pair_in, mask_row, gain, bias, front_ref, left_cells, right_cells, p):
    standard, _ = norm(pair_in)
    normed = (standard * gain + bias).astype(BF16)
    projected = nn(front_ref[: 4 * C, :], normed)
    put_pair(left_cells, p, mask_row * sigmoid(projected[:C]) * projected[C : 2 * C])
    put_pair(right_cells, p, mask_row * sigmoid(projected[2 * C : 3 * C]) * projected[3 * C :])


def over_pairs(body, hook=None, at=4):
    def step(p, _):
        if hook is not None:
            pl.when(p == at)(hook)
        body(p)
        return 0

    lax.fori_loop(0, I // 2, step, 0)


def head_kernel(single_ref, gain_ref, bias_ref, weight_ref, own_ref, every_ref, send_sem, recv_sem):
    me = lax.axis_index("axial")
    dp = lax.axis_index("dp")
    barrier = pltpu.get_barrier_semaphore()

    def greet(t, _):
        pl.semaphore_signal(
            barrier, inc=1, device_id=(dp, lax.rem(me + t, 16)), device_id_type=MESH
        )
        return 0

    lax.fori_loop(1, 16, greet, 0)
    standard, _ = norm(single_ref[...].astype(F32), axis=1)
    normed = (standard * gain_ref[...] + bias_ref[...]).astype(BF16)
    both = nn(normed, weight_ref[...]) * own_ref[...]
    mine = pl.ds(pl.multiple_of(me * I, I), I)
    every_ref[mine, :] = both.astype(BF16)
    pl.semaphore_wait(barrier, 15)

    def copy(t):
        return pltpu.make_async_remote_copy(
            src_ref=every_ref.at[mine],
            dst_ref=every_ref.at[mine],
            send_sem=send_sem.at[t],
            recv_sem=recv_sem.at[t],
            device_id=(dp, lax.rem(me + t, 16)),
            device_id_type=MESH,
        )

    def begin(t, _):
        copy(t).start()
        return 0

    def finish(t, _):
        copy(t).wait()
        return 0

    lax.fori_loop(1, 16, begin, 0)
    lax.fori_loop(1, 16, finish, 0)


def mixed_rows(own_left, cube_ref, mixed_cells):
    for b in range(B):
        mixed_cells[b * I : (b + 1) * I, :] = nn(own_left, cube_ref[:, b * C : (b + 1) * C])


def back_out(cotangent, product, pair_in, gain, bias, front_ref, out_gain, out_bias, out_ref, sums):
    out_sum, out_gain_sum, out_bias_sum = sums
    product_standard, product_inverse = norm(product)
    product_norm = (product_standard * out_gain + out_bias).astype(BF16)
    linear = tn(out_ref[...], product_norm)
    standard, _ = norm(pair_in)
    normed = (standard * gain + bias).astype(BF16)
    gate = sigmoid(nn(front_ref[4 * C :, :], normed))
    linear_grad = (cotangent * gate).astype(BF16)
    gate_grad = (cotangent * linear * gate * (1.0 - gate)).astype(BF16)
    out_sum[...] += nt(product_norm, linear_grad)
    norm_grad = nn(out_ref[...], linear_grad)
    out_gain_sum[...] += norm_grad * product_standard
    out_bias_sum[...] += norm_grad
    return gate_grad, norm_back(norm_grad * out_gain, product_standard, product_inverse)


def back_in(
    cotangent,
    gate_grad,
    left_grad,
    right_grad,
    pair_in,
    mask_row,
    gain,
    bias,
    front_ref,
    back_ref,
    sums,
):
    front_sum, gain_sum, bias_sum = sums
    standard, inverse = norm(pair_in)
    normed = (standard * gain + bias).astype(BF16)
    projected = nn(front_ref[: 4 * C, :], normed)
    grads = []
    for at, side in ((0, left_grad), (2 * C, right_grad)):
        gate = sigmoid(projected[at : at + C])
        masked = side * mask_row * gate
        grads.append((masked * projected[at + C : at + 2 * C] * (1.0 - gate)).astype(BF16))
        grads.append(masked.astype(BF16))
    grads = jnp.concatenate(grads + [gate_grad], axis=0)
    front_sum[...] += nt(normed, grads)
    normed_grad = nn(back_ref[...], grads)
    gain_sum[...] += normed_grad * standard
    bias_sum[...] += normed_grad
    return (cotangent + norm_back(normed_grad * gain, standard, inverse)).astype(BF16)


def clear(*refs):
    for ref in refs:
        ref[...] = jnp.zeros(ref.shape, ref.dtype)


def columns(*refs):
    made = [jnp.sum(ref[...], axis=1, keepdims=True) for ref in refs]
    lane = lax.broadcasted_iota(jnp.int32, (C, C), 1)
    total = jnp.zeros((C, C), F32)
    for n, column in enumerate(made):
        total = jnp.where(lane == n, column, total)
    return total


class Place:
    def __init__(self):
        self.me = lax.axis_index("axial")
        self.dp = lax.axis_index("dp")
        self.half = lax.rem(self.me // 2, 2)
        self.group = (self.me // 4) * 2 + lax.rem(self.me, 2)
        self.other = self.me + 2 - 4 * self.half

    def axial(self, group):
        return (group // 2) * 4 + self.half * 2 + lax.rem(group, 2)

    def peer(self, t):
        return lax.rem(self.group + t, 8)

    def greet(self):
        barrier = pltpu.get_barrier_semaphore()

        def signal(t, _):
            pl.semaphore_signal(
                barrier,
                inc=1,
                device_id=(self.dp, self.axial(self.peer(t))),
                device_id_type=MESH,
            )
            return 0

        lax.fori_loop(1, 8, signal, 0)
        pl.semaphore_signal(barrier, inc=1, device_id=(self.dp, self.other), device_id_type=MESH)
        pl.semaphore_wait(barrier, 8)

    def copy(self, source, target, send_sem, recv_sem, axial):
        return pltpu.make_async_remote_copy(
            src_ref=source,
            dst_ref=target,
            send_sem=send_sem,
            recv_sem=recv_sem,
            device_id=(self.dp, axial),
            device_id_type=MESH,
        )


def loop(first, last, do):
    def step(n, _):
        do(n)
        return 0

    lax.fori_loop(first, last, step, 0)


def rows_of(at, count=I):
    return pl.ds(pl.multiple_of(at, 16), count)


def piece(q):
    return pl.ds(q * CQ, CQ)


def wait_bytes(ref, sem):
    pltpu.make_async_copy(ref, ref, sem).wait()


class Travel:
    def __init__(self, place, source, target, sems, at):
        self.place, self.source, self.target = place, source, target
        self.send_sem, self.recv_sem, self.local_sem = (sem.at[at] for sem in sems)

    def send(self, h):
        pltpu.make_async_copy(*self.ends(h, self.place.group, slice(None)), self.local_sem.at[h]).start()
        for q in range(Q):
            self.send_piece(h, q)

    def send_piece(self, h, q):
        def start(t):
            group = self.place.peer(t)
            self.place.copy(
                *self.ends(h, group, q),
                self.send_sem,
                self.recv_sem.at[h, q],
                self.place.axial(group),
            ).start()

        loop(1, 8, start)

    def local(self, h):
        pltpu.make_async_copy(*self.ends(h, self.place.group, slice(None)), self.local_sem.at[h]).start()

    def here(self, h):
        pltpu.make_async_copy(*self.ends(h, self.place.group, slice(None)), self.local_sem.at[h]).wait()

    def arrive(self, h, q):
        wait_bytes(self.by_channel().at[: 7 * CQ, :, lanes(h)], self.recv_sem.at[h, q])

    def arrive_half(self, h):
        self.here(h)
        for q in range(Q):
            self.arrive(h, q)

    def sent(self):
        wait_bytes(self.by_channel().at[: 7 * 16], self.send_sem)


class Spread(Travel):
    def __init__(self, place, source, target, row, sems, at):
        super().__init__(place, source, target, sems, at)
        self.row = row

    def by_channel(self):
        return self.source

    def ends(self, h, group, q):
        if isinstance(q, slice):
            channels, kept = pl.ds(group * 16, 16), q
        else:
            channels, kept = pl.ds(group * 16 + q * CQ, CQ), piece(q)
        return (
            self.source.at[channels, :, lanes(h)],
            self.target.at[kept, rows_of(self.row), lanes(h)],
        )


class Collect(Travel):
    def by_channel(self):
        return self.target

    def ends(self, h, group, q):
        mine = self.place.group * 16
        if isinstance(q, slice):
            channels, kept = pl.ds(mine, 16), q
        else:
            channels, kept = pl.ds(mine + q * CQ, CQ), piece(q)
        return (
            self.source.at[kept, rows_of(group * I), lanes(h)],
            self.target.at[channels, :, lanes(h)],
        )


class Swap:
    def __init__(self, place, sems, at):
        self.place = place
        self.send_sem, self.recv_sem = (sem.at[at] for sem in sems)

    def rows(self, ref, h, q, r):
        for x in (2 * r, 2 * r + 1):
            block = ref.at[piece(q), rows_of(x * 64 + self.place.half * 32, 32), lanes(h)]
            self.place.copy(
                block, block, self.send_sem, self.recv_sem.at[h, q, r], self.place.other
            ).start()

    def sums(self, sent, received, h, q, r):
        where = (piece(q), slice(64 * r, 64 * r + 64), lanes(h))
        self.place.copy(
            sent.at[where],
            received.at[where],
            self.send_sem,
            self.recv_sem.at[h, q, r],
            self.place.other,
        ).start()

    def arrive(self, ref, h, q, r):
        wait_bytes(ref.at[piece(q), :64, lanes(h)], self.recv_sem.at[h, q, r])

    def sent(self, ref):
        wait_bytes(ref, self.send_sem)


def split_rows(place, whole, kept, sent, channel, r):
    for n in range(2):
        to = slice(64 * r + 32 * n, 64 * r + 32 * n + 32)
        kept[channel, to, :] = whole[rows_of(n * 64 + place.half * 32, 32), :]
        sent[channel, to, :] = whole[rows_of(n * 64 + 32 - place.half * 32, 32), :].astype(BF16)


def trunk_kernel(
    pair_ref,
    cotangent_ref,
    every_ref,
    cube_ref,
    mask_ref,
    outer_bias_ref,
    norm_gain_ref,
    norm_bias_ref,
    out_gain_ref,
    out_bias_ref,
    front_ref,
    back_ref,
    out_ref,
    pair_grad_ref,
    front0_sum,
    front1_sum,
    out0_sum,
    out1_sum,
    small_ref,
    cube_sum_ref,
    left_single_ref,
    right_total_ref,
    first,
    second,
    gate_grad0,
    gate_grad1,
    grad_second,
    sends,
    arrived,
    staged,
    left0,
    right0,
    left1,
    right1,
    grad1,
    grad0,
    kept_sum,
    sent_sum,
    received_sum,
    cells,
    mixed_cells,
    outer_cells,
    wides,
    sums,
    right_total,
    whole,
    send_sem,
    recv_sem,
    local_sem,
    half_send,
    half_recv,
):
    place = Place()
    place.greet()
    for t in range(2):
        for n, ref in enumerate((norm_gain_ref, norm_bias_ref, out_gain_ref, out_bias_ref)):
            wides[4 * t + n] = jnp.broadcast_to(ref[t : t + 1, :], (C, C)).T
    wides[8] = jnp.broadcast_to(outer_bias_ref[...], (C, C)).T
    clear(sums, front0_sum, front1_sum, out0_sum, out1_sum, right_total, outer_cells)
    right_rows = every_ref[...].astype(F32).T[B : 2 * B].astype(BF16)
    own_left = every_ref[rows_of(place.me * I), :][:, :B]
    mixed_rows(own_left, cube_ref, mixed_cells)

    sems = (send_sem, recv_sem, local_sem)
    swap_sems = (half_send, half_recv)
    me_row, group_row = place.me * I, place.group * I
    travel = [
        Spread(place, sends.at[0], left0, group_row, sems, 0),
        Spread(place, sends.at[1], right0, me_row, sems, 1),
        Collect(place, staged.at[0], arrived.at[0], sems, 2),
        Spread(place, sends.at[2], left1, group_row, sems, 3),
        Spread(place, sends.at[3], right1, group_row, sems, 4),
        Collect(place, staged.at[1], arrived.at[1], sems, 5),
        Spread(place, sends.at[4], grad1, me_row, sems, 6),
        Collect(place, staged.at[2], arrived.at[2], sems, 7),
        Collect(place, staged.at[3], arrived.at[3], sems, 8),
        Spread(place, sends.at[5], grad0, group_row, sems, 9),
        Collect(place, staged.at[4], arrived.at[4], sems, 10),
        Collect(place, staged.at[5], arrived.at[5], sems, 11),
    ]
    (
        send_left0,
        send_right0,
        send_product0,
        send_left1,
        send_right1,
        send_product1,
        send_grad1,
        send_left_grad1,
        send_right_grad1,
        send_grad0,
        send_left_grad0,
        send_right_grad0,
    ) = travel
    swaps = [Swap(place, swap_sems, n) for n in range(4)]

    def over_channels(q, do):
        loop(q * CQ, (q + 1) * CQ, do)

    def front_first(h, hook=None):
        gain, bias, outer_bias = wide(wides.at[0]), wide(wides.at[1]), wide(wides.at[8])

        def body(p):
            mask_row = mask_pair(mask_ref, p, h)
            mixed = [mixed_cells[pl.ds(2 * p + n, B, stride=I), :].astype(BF16) for n in range(2)]
            term = side_by_side(*[tn(m, right_rows[:, lanes(h)]) for m in mixed]) + outer_bias
            value = (rows_in(pair_ref, p, h) + mask_row * term).astype(BF16)
            first[h, p] = value
            send_factors(
                value.astype(F32), mask_row, gain, bias, front_ref.at[0], cells.at[0], cells.at[1], p
            )

        over_pairs(body, hook)
        cells_out(cells.at[1], sends.at[1], h)
        send_right0.send(h)
        cells_out(cells.at[0], sends.at[0], h)
        send_left0.send(h)

    def forward(travelling, ref, swap, h):
        travelling.here(h)
        if h == 0:
            for q in range(Q):
                travelling.arrive(h, q)
                for r in range(2):
                    swap.rows(ref, h, q, r)
        else:
            for q in range(Q):
                travelling.arrive(h, q)
                swap.rows(ref, h, q, 0)
            for q in range(Q):
                swap.rows(ref, h, q, 1)

    front_first(0)
    front_first(1, lambda: forward(send_right0, right0, swaps[0], 0))
    forward(send_right0, right0, swaps[0], 1)
    send_left0.arrive_half(0)
    send_left0.arrive_half(1)
    for h in range(2):
        for q in range(Q):
            for n in range(2):
                swaps[0].arrive(right0, n, q, h)

            def multiply(c):
                staged[0, c, :, lanes(h)] = nt(left0[c], right0[c, lanes(h), :]).astype(BF16)

            over_channels(q, multiply)
            send_product0.send_piece(h, q)
        send_product0.local(h)

    def middle(h):
        send_product0.arrive_half(h)
        cells_in(arrived.at[0], cells.at[2], h)
        gain0, bias0 = wide(wides.at[0]), wide(wides.at[1])
        out_gain0, out_bias0 = wide(wides.at[2]), wide(wides.at[3])
        gain1, bias1 = wide(wides.at[4]), wide(wides.at[5])

        def body(p):
            product_standard, _ = norm(get_pair(cells.at[2], p))
            product_norm = (product_standard * out_gain0 + out_bias0).astype(BF16)
            linear = tn(out_ref[0], product_norm)
            value = first[h, p].astype(F32)
            standard, _ = norm(value)
            normed = (standard * gain0 + bias0).astype(BF16)
            gate = sigmoid(nn(front_ref[0, 4 * C :, :], normed))
            value = (value + gate * linear).astype(BF16)
            second[h, p] = value
            send_factors(
                value.astype(F32),
                mask_pair(mask_ref, p, h),
                gain1,
                bias1,
                front_ref.at[1],
                cells.at[0],
                cells.at[1],
                p,
            )

        over_pairs(body)
        for n, way in ((0, send_left1), (1, send_right1)):
            cells_out(cells.at[n], sends.at[2 + n], h)
            way.local(h)
        for q in range(Q):
            send_left1.send_piece(h, q)
            send_right1.send_piece(h, q)

    middle(0)
    middle(1)
    for way in (send_left1, send_right1):
        way.here(0)
        way.here(1)
    for q in range(Q):
        for way in (send_left1, send_right1):
            for h in range(2):
                way.arrive(h, q)

        def multiply_sums(c):
            for r in range(2):
                whole[...] = tn(left1[c, :, lanes(r)], right1[c])
                split_rows(place, whole, kept_sum, sent_sum.at[0], c, r)

        over_channels(q, multiply_sums)
        for r in range(2):
            swaps[1].sums(sent_sum.at[0], received_sum.at[0], 0, q, r)
    for q in range(Q):
        for r in range(2):
            swaps[1].sums(sent_sum.at[0], received_sum.at[0], 1, q, r)

    def add_halves(swap, received, target, way, h):
        for q in range(Q):
            for r in range(2):
                swap.arrive(received, h, q, r)

            def add(c):
                target[c, :, lanes(h)] = (
                    kept_sum[c, :, lanes(h)] + received[c, :, lanes(h)].astype(F32)
                ).astype(BF16)

            over_channels(q, add)
            way.send_piece(h, q)
        way.local(h)

    def back_second(h, hook=None):
        send_product1.arrive_half(h)
        cells_in(arrived.at[1], cells.at[2], h)
        gain, bias = wide(wides.at[4]), wide(wides.at[5])
        out_gain, out_bias = wide(wides.at[6]), wide(wides.at[7])

        def body(p):
            gate_grad, product_grad = back_out(
                rows_in(cotangent_ref, p, h),
                get_pair(cells.at[2], p),
                second[h, p].astype(F32),
                gain,
                bias,
                front_ref.at[1],
                out_gain,
                out_bias,
                out_ref.at[1],
                (out1_sum, sums.at[6], sums.at[7]),
            )
            gate_grad1[h, p] = gate_grad
            put_pair(cells.at[3], p, product_grad)

        over_pairs(body, hook)
        cells_out(cells.at[3], sends.at[4], h)
        send_grad1.send(h)

    add_halves(swaps[1], received_sum.at[0], staged.at[1], send_product1, 0)
    back_second(0)
    add_halves(swaps[1], received_sum.at[0], staged.at[1], send_product1, 1)
    forward(send_grad1, grad1, swaps[2], 0)
    back_second(1)
    forward(send_grad1, grad1, swaps[2], 1)
    for h in range(2):
        for q in range(Q):
            for r in range(2):
                if h == 0 or r == 1:
                    swaps[2].arrive(grad1, h, q, r)

            def right_back(c):
                staged[3, c, :, lanes(h)] = nn(left1[c], grad1[c, :, lanes(h)]).astype(BF16)

            over_channels(q, right_back)
            send_right_grad1.send_piece(h, q)
        send_right_grad1.local(h)
        for q in range(Q):
            if h == 0:
                swaps[2].arrive(grad1, 1, q, 0)

            def left_back(c):
                staged[2, c, :, lanes(h)] = nt(right1[c], grad1[c, lanes(h), :]).astype(BF16)

            over_channels(q, left_back)
            send_left_grad1.send_piece(h, q)
        send_left_grad1.local(h)

    def back_middle(h, hook=None):
        send_left_grad1.arrive_half(h)
        send_right_grad1.arrive_half(h)
        cells_in(arrived.at[2], cells.at[0], h)
        cells_in(arrived.at[3], cells.at[1], h)
        cells_in(arrived.at[0], cells.at[2], h)
        gain1, bias1, gain0, bias0 = (wide(wides.at[n]) for n in (4, 5, 0, 1))
        out_gain0, out_bias0 = wide(wides.at[2]), wide(wides.at[3])

        def body(p):
            value = back_in(
                rows_in(cotangent_ref, p, h),
                gate_grad1[h, p],
                get_pair(cells.at[0], p),
                get_pair(cells.at[1], p),
                second[h, p].astype(F32),
                mask_pair(mask_ref, p, h),
                gain1,
                bias1,
                front_ref.at[1],
                back_ref.at[1],
                (front1_sum, sums.at[4], sums.at[5]),
            )
            grad_second[h, p] = value
            gate_grad, product_grad = back_out(
                value.astype(F32),
                get_pair(cells.at[2], p),
                first[h, p].astype(F32),
                gain0,
                bias0,
                front_ref.at[0],
                out_gain0,
                out_bias0,
                out_ref.at[0],
                (out0_sum, sums.at[2], sums.at[3]),
            )
            gate_grad0[h, p] = gate_grad
            put_pair(cells.at[3], p, product_grad)

        over_pairs(body, hook)
        cells_out(cells.at[3], sends.at[5], h)
        send_grad0.send(h)

    def right_sums(r):
        send_grad0.here(r)
        for q in range(Q):
            send_grad0.arrive(r, q)

            def multiply_back(c):
                whole[...] = tn(grad0[c, :, lanes(r)], left0[c])
                split_rows(place, whole, kept_sum, sent_sum.at[1], c, r)

            over_channels(q, multiply_back)
            swaps[3].sums(sent_sum.at[1], received_sum.at[1], 0, q, r)
            if r == 0:
                swaps[3].sums(sent_sum.at[1], received_sum.at[1], 1, q, r)
        if r == 1:
            for q in range(Q):
                swaps[3].sums(sent_sum.at[1], received_sum.at[1], 1, q, r)

    back_middle(0)
    back_middle(1, lambda: right_sums(0))
    right_sums(1)
    for h in range(2):
        for q in range(Q):

            def left_back_out(c):
                staged[4, c, :, lanes(h)] = nn(grad0[c], right0[c, :, lanes(h)]).astype(BF16)

            over_channels(q, left_back_out)
            send_left_grad0.send_piece(h, q)
        send_left_grad0.local(h)

    def back_first(h):
        send_left_grad0.arrive_half(h)
        send_right_grad0.arrive_half(h)
        cells_in(arrived.at[4], cells.at[0], h)
        cells_in(arrived.at[5], cells.at[1], h)
        gain, bias = wide(wides.at[0]), wide(wides.at[1])

        def body(p):
            mask_row = mask_pair(mask_ref, p, h)
            value = back_in(
                grad_second[h, p].astype(F32),
                gate_grad0[h, p],
                get_pair(cells.at[0], p),
                get_pair(cells.at[1], p),
                first[h, p].astype(F32),
                mask_row,
                gain,
                bias,
                front_ref.at[0],
                back_ref.at[0],
                (front0_sum, sums.at[0], sums.at[1]),
            ).astype(F32)
            outer_grad = value * mask_row
            sums[8] += outer_grad
            outer_grad = outer_grad.astype(BF16)
            for n in range(2):
                pair_grad_ref[2 * p + n, lanes(h), :] = value[:, lanes(n)].T.astype(BF16)
                grad_row = outer_grad[:, lanes(n)]
                rows = pl.ds(2 * p + n, B, stride=I)
                outer_cells[rows, :] += nt(right_rows[:, lanes(h)], grad_row)
                mixed_left = mixed_cells[rows, :].astype(BF16)
                right_total[:B, lanes(h)] += nn(mixed_left, grad_row)

        over_pairs(body)

    add_halves(swaps[3], received_sum.at[1], staged.at[5], send_right_grad0, 0)
    back_first(0)
    add_halves(swaps[3], received_sum.at[1], staged.at[5], send_right_grad0, 1)
    back_first(1)

    small_ref[...] = columns(*[sums.at[n] for n in range(9)])
    left_single = jnp.zeros((I, B), F32)
    for b in range(B):
        rows = outer_cells[b * I : (b + 1) * I, :].astype(BF16)
        cube_sum_ref[b * B : (b + 1) * B, :] = tn(own_left, rows)
        left_single += nt(rows, cube_ref[:, b * C : (b + 1) * C])
    left_single_ref[...] = side_by_side(left_single, jnp.zeros((I, C - B), F32))
    right_total_ref[...] = right_total[...].T
    for way in travel:
        way.sent()
    swaps[0].sent(left0)
    swaps[1].sent(left0)
    swaps[2].sent(left0)
    swaps[3].sent(left0)


def total_kernel(
    scale,
    right_total_ref,
    left_single_ref,
    single_ref,
    gain_ref,
    bias_ref,
    weight_ref,
    own_ref,
    front0_sum,
    front1_sum,
    out0_sum,
    out1_sum,
    cube_sum,
    small_ref,
    single_grad_ref,
    total_ref,
    packed,
    right_parts,
    pair_part,
    chip_sum,
    chip_parts,
    dp_parts,
    right_send,
    right_recv,
    core_sem,
    chip_send,
    chip_recv,
    dp_send,
    dp_recv,
    back_send,
    back_recv,
    last_send,
    last_recv,
):
    me = lax.axis_index("axial")
    dp = lax.axis_index("dp")
    core = lax.rem(me, 2)
    chip = me // 2
    sibling = me + 1 - 2 * core
    barrier = pltpu.get_barrier_semaphore()

    def greet(t, _):
        pl.semaphore_signal(
            barrier, inc=1, device_id=(dp, lax.rem(me + t, 16)), device_id_type=MESH
        )
        return 0

    def greet_dp(t, _):
        pl.semaphore_signal(
            barrier, inc=1, device_id=(lax.rem(dp + t, 8), me), device_id_type=MESH
        )
        return 0

    lax.fori_loop(1, 16, greet, 0)
    lax.fori_loop(1, 8, greet_dp, 0)

    def put(at, value):
        count = value.shape[0]
        while count:
            room = min(count, PART - at % PART)
            packed[at // PART, at % PART : at % PART + room, :] = value[:room].astype(BF16)
            at, value, count = at + room, value[room:], count - room

    for n in range(5):
        put(n * C, front0_sum[:, n * C : (n + 1) * C])
        put((5 + n) * C, front1_sum[:, n * C : (n + 1) * C])
    put(10 * C, out0_sum[...])
    put(11 * C, out1_sum[...])
    put(12 * C, cube_sum[...])
    put(24 * C, small_ref[...])
    standard, inverse = norm(single_ref[...].astype(F32), axis=1)
    normed = (standard * gain_ref[...] + bias_ref[...]).astype(BF16)
    pl.semaphore_wait(barrier, 22)

    def right_copy(t):
        target = lax.rem(me + t, 16)
        return pltpu.make_async_remote_copy(
            src_ref=right_total_ref.at[rows_of(target * I)],
            dst_ref=right_parts.at[t],
            send_sem=right_send.at[t],
            recv_sem=right_recv.at[t],
            device_id=(dp, target),
            device_id_type=MESH,
        )

    loop(1, 16, lambda t: right_copy(t).start())
    loop(1, 16, lambda t: right_copy(t).wait_recv())
    right_single = right_total_ref[rows_of(me * I), :]
    for t in range(1, 16):
        right_single += right_parts[t]
    both = jnp.concatenate(
        [left_single_ref[:, :B], right_single[:, :B], jnp.zeros((I, C - 2 * B), F32)], axis=1
    )
    both = (both * own_ref[...]).astype(BF16)
    single_grad = nt(both, weight_ref[...])
    gain_sum = jnp.sum(single_grad * standard, axis=0, keepdims=True)
    bias_sum = jnp.sum(single_grad, axis=0, keepdims=True)
    single_grad_ref[...] = norm_back(
        single_grad * gain_ref[...], standard, inverse, axis=1
    ).astype(BF16)
    factor_sums = tn(both, normed)
    for n in range(8):
        put(20 * C + n * 64, factor_sums[:64, n * C : (n + 1) * C])
    tail = [gain_sum[:, n * C : (n + 1) * C] for n in range(8)]
    tail += [bias_sum[:, n * C : (n + 1) * C] for n in range(8)]
    put(25 * C, jnp.concatenate(tail + [jnp.zeros((C - 16, C), F32)], axis=0))

    pair_copy = pltpu.make_async_remote_copy(
        src_ref=packed.at[pl.ds(8 - 8 * core, 8)],
        dst_ref=pair_part,
        send_sem=core_sem.at[0],
        recv_sem=core_sem.at[1],
        device_id=(dp, sibling),
        device_id_type=MESH,
    )
    pair_copy.start()
    pair_copy.wait()

    def chip_copy(t):
        target = lax.rem(chip + t, 8)
        return pltpu.make_async_remote_copy(
            src_ref=chip_sum.at[target],
            dst_ref=chip_parts.at[t],
            send_sem=chip_send.at[t],
            recv_sem=chip_recv.at[t],
            device_id=(dp, target * 2 + core),
            device_id_type=MESH,
        )

    def add_pair(t):
        n = lax.rem(chip + t, 8)
        chip_sum[n] = (packed[core * 8 + n].astype(F32) + pair_part[n].astype(F32)).astype(BF16)

    def add_and_send(t):
        add_pair(t)
        chip_copy(t).start()

    loop(1, 8, add_and_send)
    add_pair(0)
    loop(1, 8, lambda t: chip_copy(t).wait_recv())
    total = chip_sum[chip].astype(F32)
    for t in range(1, 8):
        total += chip_parts[t].astype(F32)
    dp_parts[dp] = total.astype(BF16)

    def dp_copy(t):
        return pltpu.make_async_remote_copy(
            src_ref=dp_parts.at[dp],
            dst_ref=dp_parts.at[dp],
            send_sem=dp_send.at[t],
            recv_sem=dp_recv.at[t],
            device_id=(lax.rem(dp + t, 8), me),
            device_id_type=MESH,
        )

    loop(1, 8, lambda t: dp_copy(t).start())
    loop(1, 8, lambda t: dp_copy(t).wait_recv())
    total = dp_parts[0].astype(F32)
    for n in range(1, 8):
        total += dp_parts[n].astype(F32)
    total_ref[core * 8 + chip] = (total * scale).astype(BF16)

    def back_copy(t):
        block = total_ref.at[core * 8 + chip]
        return pltpu.make_async_remote_copy(
            src_ref=block,
            dst_ref=block,
            send_sem=back_send.at[t],
            recv_sem=back_recv.at[t],
            device_id=(dp, lax.rem(chip + t, 8) * 2 + core),
            device_id_type=MESH,
        )

    def last_copy(t):
        block = total_ref.at[core * 8 + lax.rem(chip + 8 - t, 8)]
        return pltpu.make_async_remote_copy(
            src_ref=block,
            dst_ref=block,
            send_sem=last_send.at[t],
            recv_sem=last_recv.at[t],
            device_id=(dp, sibling),
            device_id_type=MESH,
        )

    loop(1, 8, lambda t: back_copy(t).start())
    last_copy(0).start()

    def pass_on(t):
        back_copy(t).wait_recv()
        last_copy(t).start()

    loop(1, 8, pass_on)
    loop(0, 8, lambda t: last_copy(t).wait())
    loop(1, 8, lambda t: back_copy(t).wait_send())
    loop(1, 8, lambda t: dp_copy(t).wait_send())
    loop(1, 8, lambda t: chip_copy(t).wait_send())
    loop(1, 16, lambda t: right_copy(t).wait_send())


def unpack_kernel(
    total_ref,
    outer_gain_ref,
    outer_bias_ref,
    outer_left_ref,
    outer_right_ref,
    cube_ref,
    pair_bias_ref,
    norm_gain_ref,
    norm_bias_ref,
    proj_ref,
    gate_ref,
    out_gain_ref,
    out_bias_ref,
    out_ref,
):
    for t in range(2):
        for n in range(4):
            at = (5 * t + n) * C
            proj_ref[t, :, n * C : (n + 1) * C] = total_ref[at : at + C, :].astype(F32)
        at = (5 * t + 4) * C
        gate_ref[t] = total_ref[at : at + C, :].astype(F32)
        out_ref[t] = total_ref[(10 + t) * C : (11 + t) * C, :].astype(F32)
    cube = total_ref[12 * C : 20 * C, :].astype(F32).reshape(B, B, C)
    cube_ref[...] = jnp.swapaxes(cube, 0, 1).reshape(B * B, C)
    for n in range(8):
        at = 20 * C + n * 64
        block = jnp.concatenate(
            [total_ref[at : at + 64, :].astype(F32), jnp.zeros((64, C), F32)], axis=0
        ).T
        outer_left_ref[n * C : (n + 1) * C, :] = block[:, :B]
        outer_right_ref[n * C : (n + 1) * C, :] = block[:, B : 2 * B]
    small = total_ref[24 * C : 25 * C, :].astype(F32).T
    for t in range(2):
        norm_gain_ref[t : t + 1, :] = small[4 * t : 4 * t + 1]
        norm_bias_ref[t : t + 1, :] = small[4 * t + 1 : 4 * t + 2]
        out_gain_ref[t : t + 1, :] = small[4 * t + 2 : 4 * t + 3]
        out_bias_ref[t : t + 1, :] = small[4 * t + 3 : 4 * t + 4]
    pair_bias_ref[...] = small[8:9]
    rows = total_ref[25 * C : 25 * C + 16, :].astype(F32)
    outer_gain_ref[...] = rows[:8]
    outer_bias_ref[...] = rows[8:16]


def call(kernel, outs, scratch, args, name, collective=None, flops=0):
    return pl.pallas_call(
        kernel,
        out_shape=[jax.ShapeDtypeStruct(shape, dtype) for shape, dtype in outs],
        in_specs=[pl.BlockSpec(memory_space=pltpu.VMEM)] * len(args),
        out_specs=[pl.BlockSpec(memory_space=pltpu.VMEM)] * len(outs),
        scratch_shapes=scratch,
        name=name,
        compiler_params=pltpu.CompilerParams(
            collective_id=collective,
            has_side_effects=collective is not None,
            vmem_limit_bytes=VMEM_LIMIT,
        ),
    )(*args)


DMA = pltpu.SemaphoreType.DMA
BY_CHANNEL = (C, I, J)
BY_PAIR = (2, I // 2, C, J)
HALF = (16, C, J)
EVERY = (16, J, J)


def local(
    single_state,
    pair_state,
    residue_mask,
    pair_cotangent,
    outer_norm_gain,
    outer_norm_bias,
    outer_left,
    outer_right,
    outer_proj,
    outer_bias,
    triangle_norm_gain,
    triangle_norm_bias,
    triangle_proj,
    triangle_gate,
    triangle_out_gain,
    triangle_out_bias,
    triangle_out,
):
    me = lax.axis_index("axial")
    weight = residue_mask[0].astype(F32)
    own = lax.dynamic_slice_in_dim(weight, me * I, I)[:, None]
    mask = own[None] * weight.reshape(2, 1, C)
    own_wide = jnp.broadcast_to(own, (I, C))
    factor_weight = jnp.concatenate(
        [outer_left, outer_right, jnp.zeros((outer_left.shape[0], C - 2 * B), BF16)], axis=1
    )
    single = single_state[0]
    single_gain, single_bias = outer_norm_gain[None, :], outer_norm_bias[None, :]
    cube = outer_proj.reshape(B, B * C)
    back_weight = jnp.concatenate([triangle_proj, triangle_gate], axis=2)
    front_weight = jnp.swapaxes(back_weight, 1, 2)

    (every,) = call(
        head_kernel,
        [((J, C), BF16)],
        [DMA((16,)), DMA((16,))],
        (single, single_gain, single_bias, factor_weight, own_wide),
        "head",
        collective=0,
    )
    (
        pair_gradient,
        front0_sum,
        front1_sum,
        out0_sum,
        out1_sum,
        small,
        cube_sum,
        left_single,
        right_total,
    ) = call(
        trunk_kernel,
        [
            ((I, J, C), BF16),
            ((C, 5 * C), F32),
            ((C, 5 * C), F32),
            ((C, C), F32),
            ((C, C), F32),
            ((C, C), F32),
            ((B * B, C), F32),
            ((I, C), F32),
            ((J, C), F32),
        ],
        [pltpu.VMEM(BY_PAIR, BF16)] * 5
        + [pltpu.VMEM((6,) + BY_CHANNEL, BF16)] * 2
        + [pltpu.VMEM((6,) + HALF, BF16)]
        + [pltpu.VMEM(shape, BF16) for shape in (HALF, EVERY, HALF, HALF, EVERY, HALF)]
        + [
            pltpu.VMEM(HALF, F32),
            pltpu.VMEM((2,) + HALF, BF16),
            pltpu.VMEM((2,) + HALF, BF16),
            pltpu.VMEM((4, C * I, C), F32),
            pltpu.VMEM((B * I, C), F32),
            pltpu.VMEM((B * I, C), F32),
            pltpu.VMEM((9, C, C), F32),
            pltpu.VMEM((9, C, J), F32),
            pltpu.VMEM((C, J), F32),
            pltpu.VMEM((C, J), F32),
            DMA((12,)),
            DMA((12, 2, Q)),
            DMA((12, 2)),
            DMA((4,)),
            DMA((4, 2, Q, 2)),
        ],
        (
            pair_state[0],
            pair_cotangent[0],
            every,
            cube,
            mask,
            outer_bias[None, :],
            triangle_norm_gain,
            triangle_norm_bias,
            triangle_out_gain,
            triangle_out_bias,
            front_weight,
            back_weight,
            triangle_out,
        ),
        "trunk",
        collective=1,
    )
    scale = 1.0 / float(lax.axis_size("dp") * J)
    part = (PART, C)
    single_gradient, total = call(
        functools.partial(total_kernel, scale),
        [((I, single.shape[1]), BF16), ((16,) + part, BF16)],
        [
            pltpu.VMEM((16,) + part, BF16),
            pltpu.VMEM((16, I, C), F32),
            pltpu.VMEM((8,) + part, BF16),
            pltpu.VMEM((8,) + part, BF16),
            pltpu.VMEM((8,) + part, BF16),
            pltpu.VMEM((8,) + part, BF16),
            DMA((16,)),
            DMA((16,)),
            DMA((2,)),
        ]
        + [DMA((8,))] * 8,
        (
            right_total,
            left_single,
            single,
            single_gain,
            single_bias,
            factor_weight,
            own_wide,
            front0_sum,
            front1_sum,
            out0_sum,
            out1_sum,
            cube_sum,
            small,
        ),
        "total",
        collective=2,
    )
    unpacked = call(
        unpack_kernel,
        [
            ((8, C), F32),
            ((8, C), F32),
            (outer_left.shape, F32),
            (outer_right.shape, F32),
            (outer_proj.shape, F32),
            ((1, C), F32),
            ((2, C), F32),
            ((2, C), F32),
            (triangle_proj.shape, F32),
            (triangle_gate.shape, F32),
            ((2, C), F32),
            ((2, C), F32),
            (triangle_out.shape, F32),
        ],
        [],
        (total.reshape(16 * PART, C),),
        "unpack",
    )
    unpacked = list(unpacked)
    unpacked[0] = unpacked[0].reshape(-1)
    unpacked[1] = unpacked[1].reshape(-1)
    unpacked[5] = unpacked[5].reshape(-1)
    return (single_gradient[None], pair_gradient[None]) + tuple(unpacked)


def solution(mesh):
    whole = P()
    rows = P("dp", "axial", None)
    cells = P("dp", "axial", None, None)
    return jax.shard_map(
        local,
        mesh=mesh,
        in_specs=(rows, cells, P("dp", None), cells) + (whole,) * 13,
        out_specs=(rows, cells) + (whole,) * 13,
        check_vma=False,
    )
```

```python
import functools

import jax
import jax.numpy as jnp
from jax import lax
from jax.experimental import pallas as pl
from jax.experimental.pallas import tpu as pltpu
from jax.sharding import PartitionSpec as P

EPSILON = 1e-05
F32 = jnp.float32
BF16 = jnp.bfloat16
MESH = pl.DeviceIdType.MESH
C = 128
I = 16
J = 256
B = 32
Q = 2
CQ = 8
UNROLL = 4
VMEM_LIMIT = 60 * 2**20


def nn(a, b):
    return lax.dot_general(a, b, (((1,), (0,)), ((), ())), preferred_element_type=F32)


def nt(a, b):
    return lax.dot_general(a, b, (((1,), (1,)), ((), ())), preferred_element_type=F32)


def tn(a, b):
    return lax.dot_general(a, b, (((0,), (0,)), ((), ())), preferred_element_type=F32)


def sigmoid(x):
    return 0.5 * jnp.tanh(0.5 * x) + 0.5


def norm(x, axis=0):
    centred = x - jnp.mean(x, axis=axis, keepdims=True)
    variance = jnp.mean(centred * centred, axis=axis, keepdims=True)
    inverse = lax.rsqrt(variance + EPSILON)
    return centred * inverse, inverse


def norm_back(scaled, standard, inverse, axis=0):
    first = jnp.mean(scaled, axis=axis, keepdims=True)
    second = jnp.mean(scaled * standard, axis=axis, keepdims=True)
    return inverse * (scaled - first - standard * second)


def put_pair(cells, p, value):
    cells[pl.ds(2 * p, C, stride=I), :] = value[:, :C]
    cells[pl.ds(2 * p + 1, C, stride=I), :] = value[:, C:]


def get_pair(cells, p):
    return side_by_side(cells[pl.ds(2 * p, C, stride=I), :], cells[pl.ds(2 * p + 1, C, stride=I), :])


def side_by_side(a, b):
    return jnp.concatenate([a, b], axis=1)


def lanes(h):
    return slice(h * C, (h + 1) * C)


def cells_out(cells, out_ref, h):
    def step(n, _):
        part = cells[pl.ds(pl.multiple_of(n * 256, 256), 256), :]
        out_ref[pl.ds(n * 16, 16), :, lanes(h)] = part.reshape(16, I, C).astype(BF16)
        return 0

    lax.fori_loop(0, 8, step, 0)


def cells_in(in_ref, cells, h):
    def step(n, _):
        part = in_ref[pl.ds(n * 16, 16), :, lanes(h)]
        cells[pl.ds(pl.multiple_of(n * 256, 256), 256), :] = part.astype(F32).reshape(256, C)
        return 0

    lax.fori_loop(0, 8, step, 0)


def rows_in(ref, p, h):
    return side_by_side(
        ref[2 * p, lanes(h), :].astype(F32).T, ref[2 * p + 1, lanes(h), :].astype(F32).T
    )


def weight_rows(residue_ref):
    return residue_ref[...].astype(F32)


def own_weights(residue_ref, me):
    weights = weight_rows(residue_ref)
    flat = side_by_side(weights[0:1], weights[1:2])
    lane = lax.broadcasted_iota(jnp.int32, (I, J), 1)
    row = lax.broadcasted_iota(jnp.int32, (I, J), 0) + me * I
    return jnp.sum(jnp.where(lane == row, flat, 0.0), axis=1, keepdims=True)


def mask_pair(mask_ref, p, h):
    return side_by_side(
        mask_ref[h, pl.ds(2 * p, 1), :], mask_ref[h, pl.ds(2 * p + 1, 1), :]
    )


def wide(ref):
    return side_by_side(ref[...], ref[...])


def send_factors(pair_in, mask_row, gain, bias, front_ref, left_cells, right_cells, p):
    standard, _ = norm(pair_in)
    normed = (standard * gain + bias).astype(BF16)
    projected = nn(front_ref[: 4 * C, :], normed)
    put_pair(left_cells, p, mask_row * sigmoid(projected[:C]) * projected[C : 2 * C])
    put_pair(right_cells, p, mask_row * sigmoid(projected[2 * C : 3 * C]) * projected[3 * C :])


def over_pairs(body, hook=None, at=4):
    def step(n, _):
        if hook is not None:
            pl.when(2 * n == at)(hook)
        body(2 * n)
        body(2 * n + 1)
        return 0

    lax.fori_loop(0, I // 4, step, 0)


def factor_weights(left_ref, right_ref):
    empty = jnp.zeros((C - 2 * B, left_ref.shape[1]), BF16)
    return jnp.concatenate([left_ref[...], right_ref[...], empty], axis=0)


def mixed_rows(own_left, cube_ref, mixed_cells):
    for b in range(B):
        mixed_cells[b * I : (b + 1) * I, :] = nn(own_left, cube_ref[:, b * C : (b + 1) * C])


def back_out(cotangent, product, pair_in, gain, bias, front_ref, out_gain, out_bias, out_ref, sums):
    out_sum, out_gain_sum, out_bias_sum = sums
    product_standard, product_inverse = norm(product)
    product_norm = (product_standard * out_gain + out_bias).astype(BF16)
    linear = tn(out_ref[...], product_norm)
    standard, _ = norm(pair_in)
    normed = (standard * gain + bias).astype(BF16)
    gate = sigmoid(nn(front_ref[4 * C :, :], normed))
    linear_grad = (cotangent * gate).astype(BF16)
    gate_grad = (cotangent * linear * gate * (1.0 - gate)).astype(BF16)
    out_sum[...] += nt(product_norm, linear_grad)
    norm_grad = nn(out_ref[...], linear_grad)
    out_gain_sum[...] += norm_grad * product_standard
    out_bias_sum[...] += norm_grad
    return gate_grad, norm_back(norm_grad * out_gain, product_standard, product_inverse)


def back_in(
    cotangent,
    gate_grad,
    left_grad,
    right_grad,
    pair_in,
    mask_row,
    gain,
    bias,
    front_ref,
    back_ref,
    sums,
):
    front_sum, gain_sum, bias_sum = sums
    standard, inverse = norm(pair_in)
    normed = (standard * gain + bias).astype(BF16)
    projected = nn(front_ref[: 4 * C, :], normed)
    grads = []
    for at, side in ((0, left_grad), (2 * C, right_grad)):
        gate = sigmoid(projected[at : at + C])
        masked = side * mask_row * gate
        grads.append((masked * projected[at + C : at + 2 * C] * (1.0 - gate)).astype(BF16))
        grads.append(masked.astype(BF16))
    grads = jnp.concatenate(grads + [gate_grad], axis=0)
    front_sum[...] += nt(normed, grads)
    normed_grad = nn(back_ref[...], grads)
    gain_sum[...] += normed_grad * standard
    bias_sum[...] += normed_grad
    return (cotangent + norm_back(normed_grad * gain, standard, inverse)).astype(BF16)


def clear(*refs):
    for ref in refs:
        ref[...] = jnp.zeros(ref.shape, ref.dtype)


def columns(*refs):
    made = [jnp.sum(ref[...], axis=1, keepdims=True) for ref in refs]
    lane = lax.broadcasted_iota(jnp.int32, (C, C), 1)
    total = jnp.zeros((C, C), F32)
    for n, column in enumerate(made):
        total = jnp.where(lane == n, column, total)
    return total


class Place:
    def __init__(self):
        self.me = lax.axis_index("axial")
        self.dp = lax.axis_index("dp")
        self.half = lax.rem(self.me // 2, 2)
        self.group = (self.me // 4) * 2 + lax.rem(self.me, 2)
        self.other = self.me + 2 - 4 * self.half

    def axial(self, group):
        return (group // 2) * 4 + self.half * 2 + lax.rem(group, 2)

    def peer(self, t):
        return lax.rem(self.group + t, 8)

    def greet(self):
        barrier = pltpu.get_barrier_semaphore()

        def signal(t):
            pl.semaphore_signal(
                barrier,
                inc=1,
                device_id=(self.dp, lax.rem(self.me + t, 16)),
                device_id_type=MESH,
            )

        def signal_dp(t):
            pl.semaphore_signal(
                barrier,
                inc=1,
                device_id=(lax.rem(self.dp + t, 8), self.me),
                device_id_type=MESH,
            )

        loop(1, 16, signal)
        loop(1, 8, signal_dp)

    def met(self):
        pl.semaphore_wait(pltpu.get_barrier_semaphore(), 22)

    def copy(self, source, target, send_sem, recv_sem, axial):
        return pltpu.make_async_remote_copy(
            src_ref=source,
            dst_ref=target,
            send_sem=send_sem,
            recv_sem=recv_sem,
            device_id=(self.dp, axial),
            device_id_type=MESH,
        )

    def copy_dp(self, block, send_sem, recv_sem, t):
        return pltpu.make_async_remote_copy(
            src_ref=block,
            dst_ref=block,
            send_sem=send_sem,
            recv_sem=recv_sem,
            device_id=(lax.rem(self.dp + t, 8), self.me),
            device_id_type=MESH,
        )


def loop(first, last, do):
    def step(n, _):
        do(n)
        return 0

    lax.fori_loop(first, last, step, 0)


def rows_of(at, count=I):
    return pl.ds(pl.multiple_of(at, 16), count)


def piece(q):
    return pl.ds(q * CQ, CQ)


def wait_bytes(ref, sem):
    pltpu.make_async_copy(ref, ref, sem).wait()


class Travel:
    def __init__(self, place, source, target, sems, at):
        self.place, self.source, self.target = place, source, target
        self.send_sem, self.recv_sem, self.local_sem = (sem.at[at] for sem in sems)

    def send(self, h):
        pltpu.make_async_copy(*self.ends(h, self.place.group, slice(None)), self.local_sem.at[h]).start()
        for q in range(Q):
            self.send_piece(h, q)

    def send_piece(self, h, q):
        def start(t):
            group = self.place.peer(t)
            self.place.copy(
                *self.ends(h, group, q),
                self.send_sem,
                self.recv_sem.at[h, q],
                self.place.axial(group),
            ).start()

        loop(1, 8, start)

    def local(self, h):
        pltpu.make_async_copy(*self.ends(h, self.place.group, slice(None)), self.local_sem.at[h]).start()

    def here(self, h):
        pltpu.make_async_copy(*self.ends(h, self.place.group, slice(None)), self.local_sem.at[h]).wait()

    def arrive(self, h, q):
        wait_bytes(self.by_channel().at[: 7 * CQ, :, lanes(h)], self.recv_sem.at[h, q])

    def arrive_half(self, h):
        self.here(h)
        for q in range(Q):
            self.arrive(h, q)

    def sent(self):
        wait_bytes(self.by_channel().at[: 7 * 16], self.send_sem)


class Spread(Travel):
    def __init__(self, place, source, target, row, sems, at):
        super().__init__(place, source, target, sems, at)
        self.row = row

    def by_channel(self):
        return self.source

    def ends(self, h, group, q):
        if isinstance(q, slice):
            channels, kept = pl.ds(group * 16, 16), q
        else:
            channels, kept = pl.ds(group * 16 + q * CQ, CQ), piece(q)
        return (
            self.source.at[channels, :, lanes(h)],
            self.target.at[kept, rows_of(self.row), lanes(h)],
        )


class Collect(Travel):
    def by_channel(self):
        return self.target

    def ends(self, h, group, q):
        mine = self.place.group * 16
        if isinstance(q, slice):
            channels, kept = pl.ds(mine, 16), q
        else:
            channels, kept = pl.ds(mine + q * CQ, CQ), piece(q)
        return (
            self.source.at[kept, rows_of(group * I), lanes(h)],
            self.target.at[channels, :, lanes(h)],
        )


class Swap:
    def __init__(self, place, sems, at):
        self.place = place
        self.send_sem, self.recv_sem = (sem.at[at] for sem in sems)

    def rows(self, ref, h, q, r):
        for x in (2 * r, 2 * r + 1):
            block = ref.at[piece(q), rows_of(x * 64 + self.place.half * 32, 32), lanes(h)]
            self.place.copy(
                block, block, self.send_sem, self.recv_sem.at[h, q, r], self.place.other
            ).start()

    def sums(self, sent, received, h, q, r):
        where = (piece(q), slice(64 * r, 64 * r + 64), lanes(h))
        self.place.copy(
            sent.at[where],
            received.at[where],
            self.send_sem,
            self.recv_sem.at[h, q, r],
            self.place.other,
        ).start()

    def arrive(self, ref, h, q, r):
        wait_bytes(ref.at[piece(q), :64, lanes(h)], self.recv_sem.at[h, q, r])

    def sent(self, ref):
        wait_bytes(ref, self.send_sem)


def split_rows(place, whole, kept, sent, channel, r, to_lanes, of_lanes):
    for n in range(2):
        to = slice(64 * r + 32 * n, 64 * r + 32 * n + 32)
        kept[channel, to, to_lanes] = whole[rows_of(n * 64 + place.half * 32, 32), of_lanes]
        sent[channel, to, to_lanes] = whole[
            rows_of(n * 64 + 32 - place.half * 32, 32), of_lanes
        ].astype(BF16)


class Total:
    def __init__(self, place, scale, total, first_part, refs, sems):
        self.place, self.scale, self.total, self.first = place, scale, total, first_part
        self.packed, self.pair_part, self.chip_sum, self.chip_parts, self.dp_parts = refs
        self.sem, self.back_recv = sems
        self.part = self.packed.shape[1]
        self.core = lax.rem(place.me, 2)
        self.chip = place.me // 2
        self.sibling = place.me + 1 - 2 * self.core

    def put(self, at, value):
        count, part = value.shape[0], self.part
        while count:
            room = min(count, part - at % part)
            self.packed[at // part, at % part : at % part + room, :] = value[:room].astype(BF16)
            at, value, count = at + room, value[room:], count - room

    def pair_copy(self):
        return self.place.copy(
            self.packed.at[pl.ds(8 - 8 * self.core, 8)],
            self.pair_part,
            self.sem.at[0],
            self.sem.at[1],
            self.sibling,
        )

    def start(self):
        self.pair_copy().start()

    def to_chips(self):
        self.pair_copy().wait()

        def add(t):
            n = lax.rem(self.chip + t, 8)
            self.chip_sum[n] = (
                self.packed[self.core * 8 + n].astype(F32) + self.pair_part[n].astype(F32)
            ).astype(BF16)

        def add_and_send(t):
            add(t)
            n = lax.rem(self.chip + t, 8)
            self.place.copy(
                self.chip_sum.at[n],
                self.chip_parts.at[t],
                self.sem.at[2],
                self.sem.at[3],
                n * 2 + self.core,
            ).start()

        loop(1, 8, add_and_send)
        add(0)

    def to_dp(self):
        wait_bytes(self.chip_parts.at[1:8], self.sem.at[3])
        total = self.chip_sum[self.chip].astype(F32)
        for t in range(1, 8):
            total += self.chip_parts[t].astype(F32)
        dp = self.place.dp
        self.dp_parts[dp] = total.astype(BF16)
        loop(
            1,
            8,
            lambda t: self.place.copy_dp(
                self.dp_parts.at[dp], self.sem.at[4], self.sem.at[5], t
            ).start(),
        )

    def block(self, chip):
        at = self.first + (self.core * 8 + chip) * self.part
        return self.total.at[rows_of(at, self.part)]

    def back_copy(self, t):
        block = self.block(self.chip)
        return self.place.copy(
            block,
            block,
            self.sem.at[6],
            self.back_recv.at[t],
            lax.rem(self.chip + t, 8) * 2 + self.core,
        )

    def pass_copy(self, t):
        block = self.block(lax.rem(self.chip + 8 - t, 8))
        return self.place.copy(block, block, self.sem.at[7], self.sem.at[8], self.sibling)

    def to_all(self):
        wait_bytes(self.dp_parts.at[1:8], self.sem.at[5])
        total = self.dp_parts[0].astype(F32)
        for n in range(1, 8):
            total += self.dp_parts[n].astype(F32)
        self.block(self.chip)[...] = (total * self.scale).astype(BF16)
        loop(1, 8, lambda t: self.back_copy(t).start())
        self.pass_copy(0).start()

    def to_sibling(self):
        def pass_on(t):
            self.back_copy(t).wait_recv()
            self.pass_copy(t).start()

        loop(1, 8, pass_on)

    def finish(self):
        half = self.total.at[pl.ds(self.first, 8 * self.part)]
        wait_bytes(half, self.sem.at[7])
        wait_bytes(half, self.sem.at[8])
        for n in (2, 4, 6):
            wait_bytes(self.chip_parts.at[1:8], self.sem.at[n])


def trunk_kernel(
    scale,
    single_ref,
    single_gain_ref,
    single_bias_ref,
    left_weight_ref,
    right_weight_ref,
    pair_ref,
    cotangent_ref,
    cube_ref,
    residue_ref,
    outer_bias_ref,
    norm_gain_ref,
    norm_bias_ref,
    out_gain_ref,
    out_bias_ref,
    front_ref,
    back_ref,
    out_ref,
    pair_grad_ref,
    single_grad_ref,
    total_ref,
    every_ref,
    right_total_ref,
    right_parts,
    single_standard,
    front0_sum,
    front1_sum,
    out0_sum,
    out1_sum,
    first,
    second,
    gate_grad0,
    gate_grad1,
    grad_second,
    sends,
    arrived,
    staged,
    left0,
    right0,
    left1,
    right1,
    grad1,
    grad0,
    kept_sum,
    sent_sum,
    received_sum,
    cells,
    mixed_cells,
    outer_cells,
    wides,
    sums,
    right_total,
    whole,
    mask_ref,
    send_sem,
    recv_sem,
    local_sem,
    half_send,
    half_recv,
    few_sem,
    total_sem,
    total_back,
    *total_refs,
):
    place = Place()
    place.greet()
    me, dp = place.me, place.dp
    own = own_weights(residue_ref, me)
    totals = [
        Total(
            place,
            scale,
            total_ref,
            first_part,
            total_refs[5 * n : 5 * n + 5],
            (total_sem.at[n], total_back.at[n]),
        )
        for n, first_part in enumerate((0, 1024, 2816))
    ]
    standard, single_inverse = norm(single_ref[...].astype(F32), axis=1)
    single_standard[...] = standard
    normed_single = (standard * single_gain_ref[...] + single_bias_ref[...]).astype(BF16)
    factors = nt(normed_single, factor_weights(left_weight_ref, right_weight_ref))
    mine = rows_of(me * I)
    every_ref[mine, :] = (factors * own).astype(BF16)
    place.met()

    def factor_copy(t):
        block = every_ref.at[mine]
        return place.copy(block, block, few_sem.at[0], few_sem.at[1], lax.rem(me + t, 16))

    loop(1, 16, lambda t: factor_copy(t).start())
    for h in range(2):
        mask_ref[h] = own * weight_rows(residue_ref)[h : h + 1]
    for t in range(2):
        for n, ref in enumerate((norm_gain_ref, norm_bias_ref, out_gain_ref, out_bias_ref)):
            wides[4 * t + n] = jnp.broadcast_to(ref[t : t + 1, :], (C, C)).T
    wides[8] = jnp.broadcast_to(outer_bias_ref[...], (C, C)).T
    clear(sums, front0_sum, front1_sum, out0_sum, out1_sum, right_total, outer_cells)
    own_left = every_ref[mine, :][:, :B]
    mixed_rows(own_left, cube_ref, mixed_cells)
    wait_bytes(every_ref.at[: 15 * I], few_sem.at[1])
    right_rows = every_ref[...].astype(F32).T[B : 2 * B].astype(BF16)

    sems = (send_sem, recv_sem, local_sem)
    swap_sems = (half_send, half_recv)
    me_row, group_row = place.me * I, place.group * I
    travel = [
        Spread(place, sends.at[0], left0, group_row, sems, 0),
        Spread(place, sends.at[1], right0, me_row, sems, 1),
        Collect(place, staged.at[0], arrived.at[0], sems, 2),
        Spread(place, sends.at[2], left1, group_row, sems, 3),
        Spread(place, sends.at[3], right1, group_row, sems, 4),
        Collect(place, staged.at[1], arrived.at[1], sems, 5),
        Spread(place, sends.at[4], grad1, me_row, sems, 6),
        Collect(place, staged.at[2], arrived.at[2], sems, 7),
        Collect(place, staged.at[3], arrived.at[3], sems, 8),
        Spread(place, sends.at[5], grad0, group_row, sems, 9),
        Collect(place, staged.at[4], arrived.at[4], sems, 10),
        Collect(place, staged.at[5], arrived.at[5], sems, 11),
    ]
    (
        send_left0,
        send_right0,
        send_product0,
        send_left1,
        send_right1,
        send_product1,
        send_grad1,
        send_left_grad1,
        send_right_grad1,
        send_grad0,
        send_left_grad0,
        send_right_grad0,
    ) = travel
    swaps = [Swap(place, swap_sems, n) for n in range(4)]

    def over_channels(q, do):
        def step(n):
            for m in range(UNROLL):
                do(q * CQ + n * UNROLL + m, m)

        loop(0, CQ // UNROLL, step)

    def front_first(h, hook=None):
        gain, bias, outer_bias = wide(wides.at[0]), wide(wides.at[1]), wide(wides.at[8])

        def body(p):
            mask_row = mask_pair(mask_ref, p, h)
            mixed = [mixed_cells[pl.ds(2 * p + n, B, stride=I), :].astype(BF16) for n in range(2)]
            term = side_by_side(*[tn(m, right_rows[:, lanes(h)]) for m in mixed]) + outer_bias
            value = (rows_in(pair_ref, p, h) + mask_row * term).astype(BF16)
            first[h, p] = value
            send_factors(
                value.astype(F32), mask_row, gain, bias, front_ref.at[0], cells.at[0], cells.at[1], p
            )

        over_pairs(body, hook)
        cells_out(cells.at[1], sends.at[1], h)
        send_right0.send(h)
        cells_out(cells.at[0], sends.at[0], h)
        send_left0.send(h)

    def forward_right(h):
        send_right0.here(h)
        order = ((0, 0, 0), (0, 1, 0), (0, 0, 1)) if h == 0 else (
            (1, 0, 0), (1, 1, 0), (0, 1, 1), (1, 0, 1), (1, 1, 1)
        )
        for half, q, r in order:
            if half == h and r == 0:
                send_right0.arrive(h, q)
            swaps[0].rows(right0, half, q, r)

    def forward_grad(h):
        send_grad1.here(h)
        for q in range(Q):
            send_grad1.arrive(h, q)
            swaps[2].rows(grad1, h, q, 0)
        for q in range(Q):
            swaps[2].rows(grad1, h, q, 1)

    front_first(0)
    front_first(1, lambda: forward_right(0))
    forward_right(1)
    send_left0.arrive_half(0)
    send_left0.arrive_half(1)
    for h in range(2):
        for q in range(Q):
            for n in range(2):
                swaps[0].arrive(right0, n, q, h)

            def multiply(c, m):
                staged[0, c, :, lanes(h)] = nt(left0[c], right0[c, lanes(h), :]).astype(BF16)

            over_channels(q, multiply)
            send_product0.send_piece(h, q)
        send_product0.local(h)

    def middle(h):
        send_product0.arrive_half(h)
        cells_in(arrived.at[0], cells.at[2], h)
        gain0, bias0 = wide(wides.at[0]), wide(wides.at[1])
        out_gain0, out_bias0 = wide(wides.at[2]), wide(wides.at[3])
        gain1, bias1 = wide(wides.at[4]), wide(wides.at[5])

        def body(p):
            product_standard, _ = norm(get_pair(cells.at[2], p))
            product_norm = (product_standard * out_gain0 + out_bias0).astype(BF16)
            linear = tn(out_ref[0], product_norm)
            value = first[h, p].astype(F32)
            standard, _ = norm(value)
            normed = (standard * gain0 + bias0).astype(BF16)
            gate = sigmoid(nn(front_ref[0, 4 * C :, :], normed))
            value = (value + gate * linear).astype(BF16)
            second[h, p] = value
            send_factors(
                value.astype(F32),
                mask_pair(mask_ref, p, h),
                gain1,
                bias1,
                front_ref.at[1],
                cells.at[0],
                cells.at[1],
                p,
            )

        over_pairs(body)
        for n, way in ((0, send_left1), (1, send_right1)):
            cells_out(cells.at[n], sends.at[2 + n], h)
            way.local(h)
        for q in range(Q):
            send_left1.send_piece(h, q)
            send_right1.send_piece(h, q)

    middle(0)
    middle(1)
    def incoming_sums(q, h, r):
        def multiply_sums(c, m):
            whole[m, :, :C] = tn(left1[c, :, lanes(r)], right1[c, :, lanes(h)])
            split_rows(
                place, whole.at[m], kept_sum, sent_sum.at[0], c, r, lanes(h), slice(0, C)
            )

        over_channels(q, multiply_sums)
        swaps[1].sums(sent_sum.at[0], received_sum.at[0], h, q, r)

    for n in range(2):
        for way in (send_left1, send_right1):
            way.here(n)
        for q in range(Q):
            for way in (send_left1, send_right1):
                way.arrive(n, q)
            incoming_sums(q, 0, n)
    for r in range(2):
        for q in range(Q):
            incoming_sums(q, 1, r)

    def add_halves(swap, received, target, way, h):
        for q in range(Q):
            for r in range(2):
                swap.arrive(received, h, q, r)

            def add(c, m):
                target[c, :, lanes(h)] = (
                    kept_sum[c, :, lanes(h)] + received[c, :, lanes(h)].astype(F32)
                ).astype(BF16)

            over_channels(q, add)
            way.send_piece(h, q)
        way.local(h)

    def back_second(h, hook=None):
        send_product1.arrive_half(h)
        cells_in(arrived.at[1], cells.at[2], h)
        gain, bias = wide(wides.at[4]), wide(wides.at[5])
        out_gain, out_bias = wide(wides.at[6]), wide(wides.at[7])

        def body(p):
            gate_grad, product_grad = back_out(
                rows_in(cotangent_ref, p, h),
                get_pair(cells.at[2], p),
                second[h, p].astype(F32),
                gain,
                bias,
                front_ref.at[1],
                out_gain,
                out_bias,
                out_ref.at[1],
                (out1_sum, sums.at[6], sums.at[7]),
            )
            gate_grad1[h, p] = gate_grad
            put_pair(cells.at[3], p, product_grad)

        over_pairs(body, hook)
        cells_out(cells.at[3], sends.at[4], h)
        send_grad1.send(h)

    add_halves(swaps[1], received_sum.at[0], staged.at[1], send_product1, 0)
    back_second(0)
    add_halves(swaps[1], received_sum.at[0], staged.at[1], send_product1, 1)
    forward_grad(0)
    back_second(1)
    forward_grad(1)
    for h in range(2):
        for q in range(Q):
            for r in range(2):
                if h == 0 or r == 1:
                    swaps[2].arrive(grad1, h, q, r)

            def right_back(c, m):
                staged[3, c, :, lanes(h)] = nn(left1[c], grad1[c, :, lanes(h)]).astype(BF16)

            over_channels(q, right_back)
            send_right_grad1.send_piece(h, q)
        send_right_grad1.local(h)
        for q in range(Q):
            if h == 0:
                swaps[2].arrive(grad1, 1, q, 0)

            def left_back(c, m):
                staged[2, c, :, lanes(h)] = nt(right1[c], grad1[c, lanes(h), :]).astype(BF16)

            over_channels(q, left_back)
            send_left_grad1.send_piece(h, q)
        send_left_grad1.local(h)

    def back_middle(h, hook=None):
        send_left_grad1.arrive_half(h)
        send_right_grad1.arrive_half(h)
        cells_in(arrived.at[2], cells.at[0], h)
        cells_in(arrived.at[3], cells.at[1], h)
        cells_in(arrived.at[0], cells.at[2], h)
        gain1, bias1, gain0, bias0 = (wide(wides.at[n]) for n in (4, 5, 0, 1))
        out_gain0, out_bias0 = wide(wides.at[2]), wide(wides.at[3])

        def body(p):
            value = back_in(
                rows_in(cotangent_ref, p, h),
                gate_grad1[h, p],
                get_pair(cells.at[0], p),
                get_pair(cells.at[1], p),
                second[h, p].astype(F32),
                mask_pair(mask_ref, p, h),
                gain1,
                bias1,
                front_ref.at[1],
                back_ref.at[1],
                (front1_sum, sums.at[4], sums.at[5]),
            )
            grad_second[h, p] = value
            gate_grad, product_grad = back_out(
                value.astype(F32),
                get_pair(cells.at[2], p),
                first[h, p].astype(F32),
                gain0,
                bias0,
                front_ref.at[0],
                out_gain0,
                out_bias0,
                out_ref.at[0],
                (out0_sum, sums.at[2], sums.at[3]),
            )
            gate_grad0[h, p] = gate_grad
            put_pair(cells.at[3], p, product_grad)

        over_pairs(body, hook)
        cells_out(cells.at[3], sends.at[5], h)
        send_grad0.send(h)

    def right_sums(r):
        send_grad0.here(r)
        for q in range(Q):
            send_grad0.arrive(r, q)

            def multiply_back(c, m):
                whole[m] = tn(grad0[c, :, lanes(r)], left0[c])
                split_rows(
                    place, whole.at[m], kept_sum, sent_sum.at[1], c, r, slice(None), slice(None)
                )

            over_channels(q, multiply_back)
            swaps[3].sums(sent_sum.at[1], received_sum.at[1], 0, q, r)
            if r == 0:
                swaps[3].sums(sent_sum.at[1], received_sum.at[1], 1, q, r)
        if r == 1:
            for q in range(Q):
                swaps[3].sums(sent_sum.at[1], received_sum.at[1], 1, q, r)

    back_middle(0)
    back_middle(1, lambda: right_sums(0))
    for n in range(5):
        totals[0].put(n * C, front1_sum[:, n * C : (n + 1) * C])
    totals[0].put(5 * C, out0_sum[...])
    totals[0].put(6 * C, out1_sum[...])
    totals[0].put(7 * C, jnp.zeros((C, C), F32))
    totals[0].start()
    right_sums(1)
    totals[0].to_chips()
    for h in range(2):
        for q in range(Q):

            def left_back_out(c, m):
                staged[4, c, :, lanes(h)] = nn(grad0[c], right0[c, :, lanes(h)]).astype(BF16)

            over_channels(q, left_back_out)
            send_left_grad0.send_piece(h, q)
        send_left_grad0.local(h)

    def back_first(h):
        send_left_grad0.arrive_half(h)
        send_right_grad0.arrive_half(h)
        cells_in(arrived.at[4], cells.at[0], h)
        cells_in(arrived.at[5], cells.at[1], h)
        gain, bias = wide(wides.at[0]), wide(wides.at[1])

        def body(p):
            mask_row = mask_pair(mask_ref, p, h)
            value = back_in(
                grad_second[h, p].astype(F32),
                gate_grad0[h, p],
                get_pair(cells.at[0], p),
                get_pair(cells.at[1], p),
                first[h, p].astype(F32),
                mask_row,
                gain,
                bias,
                front_ref.at[0],
                back_ref.at[0],
                (front0_sum, sums.at[0], sums.at[1]),
            ).astype(F32)
            outer_grad = value * mask_row
            sums[8] += outer_grad
            outer_grad = outer_grad.astype(BF16)
            for n in range(2):
                pair_grad_ref[2 * p + n, lanes(h), :] = value[:, lanes(n)].T.astype(BF16)
                grad_row = outer_grad[:, lanes(n)]
                rows = pl.ds(2 * p + n, B, stride=I)
                outer_cells[rows, :] += nt(right_rows[:, lanes(h)], grad_row)
                mixed_left = mixed_cells[rows, :].astype(BF16)
                right_total[:B, lanes(h)] += nn(mixed_left, grad_row)

        over_pairs(body)

    add_halves(swaps[3], received_sum.at[1], staged.at[5], send_right_grad0, 0)
    totals[0].to_dp()
    back_first(0)
    add_halves(swaps[3], received_sum.at[1], staged.at[5], send_right_grad0, 1)
    totals[0].to_all()
    back_first(1)

    right_total_ref[...] = right_total[...].T

    def right_copy(t):
        target = lax.rem(me + t, 16)
        return place.copy(
            right_total_ref.at[rows_of(target * I)],
            right_parts.at[t],
            few_sem.at[2],
            few_sem.at[3],
            target,
        )

    loop(1, 16, lambda t: right_copy(t).start())
    for n in range(5):
        totals[1].put(n * C, front0_sum[:, n * C : (n + 1) * C])
    left_single = jnp.zeros((I, B), F32)
    for b in range(B):
        rows = outer_cells[b * I : (b + 1) * I, :].astype(BF16)
        totals[1].put(5 * C + b * B, tn(own_left, rows))
        left_single += nt(rows, cube_ref[:, b * C : (b + 1) * C])
    totals[1].put(13 * C, columns(*[sums.at[n] for n in range(9)]))
    totals[1].start()

    wait_bytes(right_parts.at[1:16], few_sem.at[3])
    right_single = right_total_ref[mine, :]
    for t in range(1, 16):
        right_single += right_parts[t]
    both = jnp.concatenate(
        [left_single, right_single[:, :B], jnp.zeros((I, C - 2 * B), F32)], axis=1
    )
    both = (both * own).astype(BF16)
    single_grad = nn(both, factor_weights(left_weight_ref, right_weight_ref))
    standard = single_standard[...]
    normed_single = (standard * single_gain_ref[...] + single_bias_ref[...]).astype(BF16)
    factor_sums = tn(both, normed_single)
    totals[1].to_chips()
    for n in range(8):
        totals[2].put(n * 64, factor_sums[:64, lanes(n)])
    gain_sum = jnp.sum(single_grad * standard, axis=0, keepdims=True)
    bias_sum = jnp.sum(single_grad, axis=0, keepdims=True)
    tail = [gain_sum[:, lanes(n)] for n in range(8)] + [bias_sum[:, lanes(n)] for n in range(8)]
    totals[2].put(4 * C, jnp.concatenate(tail + [jnp.zeros((2 * C - 16, C), F32)], axis=0))
    totals[2].start()
    single_grad_ref[...] = norm_back(
        single_grad * single_gain_ref[...], standard, single_inverse, axis=1
    ).astype(BF16)
    totals[0].to_sibling()
    totals[2].to_chips()
    totals[1].to_dp()
    totals[2].to_dp()
    totals[1].to_all()
    totals[2].to_all()
    totals[1].to_sibling()
    totals[2].to_sibling()
    for batch in totals:
        batch.finish()
    wait_bytes(every_ref.at[: 15 * I], few_sem.at[0])
    wait_bytes(right_parts.at[1:16], few_sem.at[2])
    for way in travel:
        way.sent()
    swaps[0].sent(left0)
    swaps[1].sent(left0)
    swaps[2].sent(left0)
    swaps[3].sent(left0)


def unpack_kernel(
    total_ref,
    outer_gain_ref,
    outer_bias_ref,
    outer_left_ref,
    outer_right_ref,
    cube_ref,
    pair_bias_ref,
    norm_gain_ref,
    norm_bias_ref,
    proj_ref,
    gate_ref,
    out_gain_ref,
    out_bias_ref,
    out_ref,
):
    for t in range(2):
        front = 8 - 8 * t
        for n in range(4):
            at = (front + n) * C
            proj_ref[t, :, n * C : (n + 1) * C] = total_ref[at : at + C, :].astype(F32)
        at = (front + 4) * C
        gate_ref[t] = total_ref[at : at + C, :].astype(F32)
        out_ref[t] = total_ref[(5 + t) * C : (6 + t) * C, :].astype(F32)
    cube = total_ref[13 * C : 21 * C, :].astype(F32).reshape(B, B, C)
    cube_ref[...] = jnp.swapaxes(cube, 0, 1).reshape(B * B, C)
    for n in range(8):
        at = 22 * C + n * 64
        outer_left_ref[:, n * C : (n + 1) * C] = total_ref[at : at + B, :].astype(F32)
        outer_right_ref[:, n * C : (n + 1) * C] = total_ref[at + B : at + 2 * B, :].astype(F32)
    small = total_ref[21 * C : 22 * C, :].astype(F32).T
    for t in range(2):
        norm_gain_ref[t : t + 1, :] = small[4 * t : 4 * t + 1]
        norm_bias_ref[t : t + 1, :] = small[4 * t + 1 : 4 * t + 2]
        out_gain_ref[t : t + 1, :] = small[4 * t + 2 : 4 * t + 3]
        out_bias_ref[t : t + 1, :] = small[4 * t + 3 : 4 * t + 4]
    pair_bias_ref[...] = small[8:9]
    rows = total_ref[26 * C : 26 * C + 16, :].astype(F32)
    outer_gain_ref[...] = rows[:8]
    outer_bias_ref[...] = rows[8:16]


def call(kernel, outs, scratch, args, name, collective=None, flops=0):
    return pl.pallas_call(
        kernel,
        out_shape=[jax.ShapeDtypeStruct(shape, dtype) for shape, dtype in outs],
        in_specs=[pl.BlockSpec(memory_space=pltpu.VMEM)] * len(args),
        out_specs=[pl.BlockSpec(memory_space=pltpu.VMEM)] * len(outs),
        scratch_shapes=scratch,
        name=name,
        compiler_params=pltpu.CompilerParams(
            collective_id=collective,
            has_side_effects=collective is not None,
            vmem_limit_bytes=VMEM_LIMIT,
        ),
    )(*args)


DMA = pltpu.SemaphoreType.DMA
BY_CHANNEL = (C, I, J)
BY_PAIR = (2, I // 2, C, J)
HALF = (16, C, J)
EVERY = (16, J, J)


def local(
    single_state,
    pair_state,
    residue_mask,
    pair_cotangent,
    outer_norm_gain,
    outer_norm_bias,
    outer_left,
    outer_right,
    outer_proj,
    outer_bias,
    triangle_norm_gain,
    triangle_norm_bias,
    triangle_proj,
    triangle_gate,
    triangle_out_gain,
    triangle_out_bias,
    triangle_out,
):
    residues = residue_mask.reshape(2, C)
    left_weight, right_weight = outer_left.T, outer_right.T
    single = single_state[0]
    single_gain, single_bias = outer_norm_gain[None, :], outer_norm_bias[None, :]
    cube = outer_proj.reshape(B, B * C)
    back_weight = jnp.concatenate([triangle_proj, triangle_gate], axis=2)
    front_weight = jnp.swapaxes(back_weight, 1, 2)

    scale = 1.0 / float(lax.axis_size("dp") * J)
    pair_gradient, single_gradient, total = call(
        functools.partial(trunk_kernel, scale),
        [((I, J, C), BF16), ((I, single.shape[1]), BF16), ((28 * C, C), BF16)],
        [
            pltpu.VMEM((J, C), BF16),
            pltpu.VMEM((J, C), F32),
            pltpu.VMEM((16, I, C), F32),
            pltpu.VMEM((I, single.shape[1]), F32),
            pltpu.VMEM((C, 5 * C), F32),
            pltpu.VMEM((C, 5 * C), F32),
            pltpu.VMEM((C, C), F32),
            pltpu.VMEM((C, C), F32),
        ]
        + [pltpu.VMEM(BY_PAIR, BF16)] * 5
        + [pltpu.VMEM((6,) + BY_CHANNEL, BF16)] * 2
        + [pltpu.VMEM((6,) + HALF, BF16)]
        + [pltpu.VMEM(shape, BF16) for shape in (HALF, EVERY, HALF, HALF, EVERY, HALF)]
        + [
            pltpu.VMEM(HALF, F32),
            pltpu.VMEM((2,) + HALF, BF16),
            pltpu.VMEM((2,) + HALF, BF16),
            pltpu.VMEM((4, C * I, C), F32),
            pltpu.VMEM((B * I, C), F32),
            pltpu.VMEM((B * I, C), F32),
            pltpu.VMEM((9, C, C), F32),
            pltpu.VMEM((9, C, J), F32),
            pltpu.VMEM((C, J), F32),
            pltpu.VMEM((UNROLL, C, J), F32),
            pltpu.VMEM((2, I, C), F32),
            DMA((12,)),
            DMA((12, 2, Q)),
            DMA((12, 2)),
            DMA((4,)),
            DMA((4, 2, Q, 2)),
            DMA((4,)),
            DMA((3, 9)),
            DMA((3, 8)),
        ]
        + [
            pltpu.VMEM((count, part, C), BF16)
            for part in (64, 112, 48)
            for count in (16, 8, 8, 8, 8)
        ],
        (
            single,
            single_gain,
            single_bias,
            left_weight,
            right_weight,
            pair_state[0],
            pair_cotangent[0],
            cube,
            residues,
            outer_bias[None, :],
            triangle_norm_gain,
            triangle_norm_bias,
            triangle_out_gain,
            triangle_out_bias,
            front_weight,
            back_weight,
            triangle_out,
        ),
        "trunk",
        collective=0,
    )
    unpacked = call(
        unpack_kernel,
        [
            ((8, C), F32),
            ((8, C), F32),
            (left_weight.shape, F32),
            (right_weight.shape, F32),
            (outer_proj.shape, F32),
            ((1, C), F32),
            ((2, C), F32),
            ((2, C), F32),
            (triangle_proj.shape, F32),
            (triangle_gate.shape, F32),
            ((2, C), F32),
            ((2, C), F32),
            (triangle_out.shape, F32),
        ],
        [],
        (total,),
        "unpack",
    )
    unpacked = list(unpacked)
    unpacked[0] = unpacked[0].reshape(-1)
    unpacked[1] = unpacked[1].reshape(-1)
    unpacked[5] = unpacked[5].reshape(-1)
    unpacked[2] = unpacked[2].T
    unpacked[3] = unpacked[3].T
    return (single_gradient[None], pair_gradient[None]) + tuple(unpacked)


def solution(mesh):
    whole = P()
    rows = P("dp", "axial", None)
    cells = P("dp", "axial", None, None)
    return jax.shard_map(
        local,
        mesh=mesh,
        in_specs=(rows, cells, P("dp", None), cells) + (whole,) * 13,
        out_specs=(rows, cells) + (whole,) * 13,
        check_vma=False,
    )
```

```python
import functools

import jax
import jax.numpy as jnp
from jax import lax
from jax.experimental import pallas as pl
from jax.experimental.pallas import tpu as pltpu
from jax.sharding import PartitionSpec as P

EPSILON = 1e-05
F32 = jnp.float32
BF16 = jnp.bfloat16
MESH = pl.DeviceIdType.MESH
C = 128
I = 16
J = 256
B = 32
Q = 4
CQ = 4
UNROLL = 4
VMEM_LIMIT = 60 * 2**20


def nn(a, b):
    return lax.dot_general(a, b, (((1,), (0,)), ((), ())), preferred_element_type=F32)


def nt(a, b):
    return lax.dot_general(a, b, (((1,), (1,)), ((), ())), preferred_element_type=F32)


def tn(a, b):
    return lax.dot_general(a, b, (((0,), (0,)), ((), ())), preferred_element_type=F32)


def sigmoid(x):
    return 0.5 * jnp.tanh(0.5 * x) + 0.5


def norm(x, axis=0):
    centred = x - jnp.mean(x, axis=axis, keepdims=True)
    variance = jnp.mean(centred * centred, axis=axis, keepdims=True)
    inverse = lax.rsqrt(variance + EPSILON)
    return centred * inverse, inverse


def norm_back(scaled, standard, inverse, axis=0):
    first = jnp.mean(scaled, axis=axis, keepdims=True)
    second = jnp.mean(scaled * standard, axis=axis, keepdims=True)
    return inverse * (scaled - first - standard * second)


def put_pair(cells, p, value):
    cells[pl.ds(2 * p, C, stride=I), :] = value[:, :C]
    cells[pl.ds(2 * p + 1, C, stride=I), :] = value[:, C:]


def get_pair(cells, p):
    return side_by_side(cells[pl.ds(2 * p, C, stride=I), :], cells[pl.ds(2 * p + 1, C, stride=I), :])


def side_by_side(a, b):
    return jnp.concatenate([a, b], axis=1)


def lanes(h):
    return slice(h * C, (h + 1) * C)


def cells_out(cells, out_ref, h):
    def step(n, _):
        part = cells[pl.ds(pl.multiple_of(n * 256, 256), 256), :]
        out_ref[pl.ds(n * 16, 16), :, lanes(h)] = part.reshape(16, I, C).astype(BF16)
        return 0

    lax.fori_loop(0, 8, step, 0)


def cells_in(in_ref, cells, h):
    def step(n, _):
        part = in_ref[pl.ds(n * 16, 16), :, lanes(h)]
        cells[pl.ds(pl.multiple_of(n * 256, 256), 256), :] = part.astype(F32).reshape(256, C)
        return 0

    lax.fori_loop(0, 8, step, 0)


def rows_in(ref, p, h):
    return side_by_side(
        ref[2 * p, lanes(h), :].astype(F32).T, ref[2 * p + 1, lanes(h), :].astype(F32).T
    )


def weight_rows(residue_ref):
    return residue_ref[...].astype(F32)


def own_weights(residue_ref, me):
    weights = weight_rows(residue_ref)
    flat = side_by_side(weights[0:1], weights[1:2])
    lane = lax.broadcasted_iota(jnp.int32, (I, J), 1)
    row = lax.broadcasted_iota(jnp.int32, (I, J), 0) + me * I
    return jnp.sum(jnp.where(lane == row, flat, 0.0), axis=1, keepdims=True)


def mask_pair(mask_ref, p, h):
    return side_by_side(
        mask_ref[h, pl.ds(2 * p, 1), :], mask_ref[h, pl.ds(2 * p + 1, 1), :]
    )


def wide(ref):
    return side_by_side(ref[...], ref[...])


def send_factors(pair_in, mask_row, gain, bias, front_ref, left_cells, right_cells, p):
    standard, _ = norm(pair_in)
    normed = (standard * gain + bias).astype(BF16)
    projected = nn(front_ref[: 4 * C, :], normed)
    put_pair(left_cells, p, mask_row * sigmoid(projected[:C]) * projected[C : 2 * C])
    put_pair(right_cells, p, mask_row * sigmoid(projected[2 * C : 3 * C]) * projected[3 * C :])


def over_pairs(body, hook=None, at=4):
    def step(n, _):
        if hook is not None:
            pl.when(2 * n == at)(hook)
        body(2 * n)
        body(2 * n + 1)
        return 0

    lax.fori_loop(0, I // 4, step, 0)


def factor_weights(left_ref, right_ref):
    empty = jnp.zeros((C - 2 * B, left_ref.shape[1]), BF16)
    return jnp.concatenate([left_ref[...], right_ref[...], empty], axis=0)


def mixed_rows(own_left, outer_proj_ref, rows, cube_ref, mixed_cells):
    rows[: B * B, :] = outer_proj_ref[...].astype(F32)
    for b in range(B):
        cube_ref[b] = rows[pl.ds(b, B, stride=B), :].astype(BF16)
        mixed_cells[b * I : (b + 1) * I, :] = nn(own_left, cube_ref[b])


def back_out(cotangent, product, pair_in, gain, bias, front_ref, out_gain, out_bias, out_ref, sums):
    out_sum, out_gain_sum, out_bias_sum = sums
    product_standard, product_inverse = norm(product)
    product_norm = (product_standard * out_gain + out_bias).astype(BF16)
    linear = tn(out_ref[...], product_norm)
    standard, _ = norm(pair_in)
    normed = (standard * gain + bias).astype(BF16)
    gate = sigmoid(nn(front_ref[4 * C :, :], normed))
    linear_grad = (cotangent * gate).astype(BF16)
    gate_grad = (cotangent * linear * gate * (1.0 - gate)).astype(BF16)
    out_sum[...] += nt(product_norm, linear_grad)
    norm_grad = nn(out_ref[...], linear_grad)
    out_gain_sum[...] += norm_grad * product_standard
    out_bias_sum[...] += norm_grad
    return gate_grad, norm_back(norm_grad * out_gain, product_standard, product_inverse)


def back_in(
    cotangent,
    gate_grad,
    left_grad,
    right_grad,
    pair_in,
    mask_row,
    gain,
    bias,
    front_ref,
    back_ref,
    sums,
):
    front_sum, gain_sum, bias_sum = sums
    standard, inverse = norm(pair_in)
    normed = (standard * gain + bias).astype(BF16)
    projected = nn(front_ref[: 4 * C, :], normed)
    grads = []
    for at, side in ((0, left_grad), (2 * C, right_grad)):
        gate = sigmoid(projected[at : at + C])
        masked = side * mask_row * gate
        grads.append((masked * projected[at + C : at + 2 * C] * (1.0 - gate)).astype(BF16))
        grads.append(masked.astype(BF16))
    grads = jnp.concatenate(grads + [gate_grad], axis=0)
    front_sum[...] += nt(normed, grads)
    normed_grad = nn(back_ref[...], grads)
    gain_sum[...] += normed_grad * standard
    bias_sum[...] += normed_grad
    return (cotangent + norm_back(normed_grad * gain, standard, inverse)).astype(BF16)


def clear(*refs):
    for ref in refs:
        ref[...] = jnp.zeros(ref.shape, ref.dtype)


def columns(*refs):
    made = [jnp.sum(ref[...], axis=1, keepdims=True) for ref in refs]
    lane = lax.broadcasted_iota(jnp.int32, (C, C), 1)
    total = jnp.zeros((C, C), F32)
    for n, column in enumerate(made):
        total = jnp.where(lane == n, column, total)
    return total


class Place:
    def __init__(self):
        self.me = lax.axis_index("axial")
        self.dp = lax.axis_index("dp")
        self.half = lax.rem(self.me // 2, 2)
        self.group = (self.me // 4) * 2 + lax.rem(self.me, 2)
        self.other = self.me + 2 - 4 * self.half

    def axial(self, group):
        return (group // 2) * 4 + self.half * 2 + lax.rem(group, 2)

    def peer(self, t):
        n = t - 1
        turn = lax.rem(n, 3)
        step = (2 * turn + 1 - 3 * (turn // 2)) * (1 - n // 6)
        core = lax.rem(self.me + n // 3 + n // 6, 2)
        return lax.rem(self.group // 2 + step, 4) * 2 + core

    def greet(self):
        barrier = pltpu.get_barrier_semaphore()

        def signal(t):
            pl.semaphore_signal(
                barrier,
                inc=1,
                device_id=(self.dp, lax.rem(self.me + t, 16)),
                device_id_type=MESH,
            )

        def signal_dp(t):
            pl.semaphore_signal(
                barrier,
                inc=1,
                device_id=(lax.rem(self.dp + t, 8), self.me),
                device_id_type=MESH,
            )

        loop(1, 16, signal)
        loop(1, 8, signal_dp)

    def met(self):
        pl.semaphore_wait(pltpu.get_barrier_semaphore(), 22)

    def copy(self, source, target, send_sem, recv_sem, axial):
        return pltpu.make_async_remote_copy(
            src_ref=source,
            dst_ref=target,
            send_sem=send_sem,
            recv_sem=recv_sem,
            device_id=(self.dp, axial),
            device_id_type=MESH,
        )

    def copy_dp(self, block, send_sem, recv_sem, t):
        return pltpu.make_async_remote_copy(
            src_ref=block,
            dst_ref=block,
            send_sem=send_sem,
            recv_sem=recv_sem,
            device_id=(lax.rem(self.dp + t, 8), self.me),
            device_id_type=MESH,
        )


def loop(first, last, do):
    def step(n, _):
        do(n)
        return 0

    lax.fori_loop(first, last, step, 0)


def rows_of(at, count=I):
    return pl.ds(pl.multiple_of(at, 16), count)


def piece(q):
    return pl.ds(q * CQ, CQ)


def wait_bytes(ref, sem):
    pltpu.make_async_copy(ref, ref, sem).wait()


class Travel:
    def __init__(self, place, source, target, sems, at):
        self.place, self.source, self.target = place, source, target
        self.send_sem, self.recv_sem, self.local_sem = (sem.at[at] for sem in sems)

    def send(self, h):
        pltpu.make_async_copy(*self.ends(h, self.place.group, slice(None)), self.local_sem.at[h]).start()
        for q in range(Q):
            self.send_piece(h, q)

    def send_piece(self, h, q):
        def start(t):
            group = self.place.peer(t)
            self.place.copy(
                *self.ends(h, group, q),
                self.send_sem,
                self.recv_sem.at[h, q],
                self.place.axial(group),
            ).start()

        loop(1, 8, start)

    def local(self, h):
        pltpu.make_async_copy(*self.ends(h, self.place.group, slice(None)), self.local_sem.at[h]).start()

    def here(self, h):
        pltpu.make_async_copy(*self.ends(h, self.place.group, slice(None)), self.local_sem.at[h]).wait()

    def arrive(self, h, q):
        wait_bytes(self.by_channel().at[: 7 * CQ, :, lanes(h)], self.recv_sem.at[h, q])

    def arrive_half(self, h):
        self.here(h)
        for q in range(Q):
            self.arrive(h, q)

    def sent(self):
        wait_bytes(self.by_channel().at[: 7 * 16], self.send_sem)


class Spread(Travel):
    def __init__(self, place, source, target, row, sems, at):
        super().__init__(place, source, target, sems, at)
        self.row = row

    def by_channel(self):
        return self.source

    def ends(self, h, group, q):
        if isinstance(q, slice):
            channels, kept = pl.ds(group * 16, 16), q
        else:
            channels, kept = pl.ds(group * 16 + q * CQ, CQ), piece(q)
        return (
            self.source.at[channels, :, lanes(h)],
            self.target.at[kept, rows_of(self.row), lanes(h)],
        )


class Collect(Travel):
    def by_channel(self):
        return self.target

    def ends(self, h, group, q):
        mine = self.place.group * 16
        if isinstance(q, slice):
            channels, kept = pl.ds(mine, 16), q
        else:
            channels, kept = pl.ds(mine + q * CQ, CQ), piece(q)
        return (
            self.source.at[kept, rows_of(group * I), lanes(h)],
            self.target.at[channels, :, lanes(h)],
        )


class Swap:
    def __init__(self, place, sems, at):
        self.place = place
        self.send_sem, self.recv_sem = (sem.at[at] for sem in sems)

    def rows(self, ref, h, q, r):
        for x in (2 * r, 2 * r + 1):
            block = ref.at[piece(q), rows_of(x * 64 + self.place.half * 32, 32), lanes(h)]
            self.place.copy(
                block, block, self.send_sem, self.recv_sem.at[h, q, r], self.place.other
            ).start()

    def sums(self, sent, received, h, q, r):
        where = (piece(q), slice(64 * r, 64 * r + 64), lanes(h))
        self.place.copy(
            sent.at[where],
            received.at[where],
            self.send_sem,
            self.recv_sem.at[h, q, r],
            self.place.other,
        ).start()

    def arrive(self, ref, h, q, r):
        wait_bytes(ref.at[piece(q), :64, lanes(h)], self.recv_sem.at[h, q, r])

    def sent(self, ref):
        wait_bytes(ref, self.send_sem)


def split_rows(place, whole, kept, sent, channel, r, to_lanes, of_lanes):
    for n in range(2):
        to = slice(64 * r + 32 * n, 64 * r + 32 * n + 32)
        kept[channel, to, to_lanes] = whole[rows_of(n * 64 + place.half * 32, 32), of_lanes]
        sent[channel, to, to_lanes] = whole[
            rows_of(n * 64 + 32 - place.half * 32, 32), of_lanes
        ].astype(BF16)


class Total:
    def __init__(self, place, scale, total, first_part, refs, sems):
        self.place, self.scale, self.total, self.first = place, scale, total, first_part
        self.packed, self.pair_part, self.chip_sum, self.chip_parts, self.dp_parts = refs
        self.sem, self.back_recv = sems
        self.part = self.packed.shape[1]
        self.core = lax.rem(place.me, 2)
        self.chip = place.me // 2
        self.sibling = place.me + 1 - 2 * self.core

    def put(self, at, value):
        count, part = value.shape[0], self.part
        while count:
            room = min(count, part - at % part)
            self.packed[at // part, at % part : at % part + room, :] = value[:room].astype(BF16)
            at, value, count = at + room, value[room:], count - room

    def pair_copy(self):
        return self.place.copy(
            self.packed.at[pl.ds(8 - 8 * self.core, 8)],
            self.pair_part,
            self.sem.at[0],
            self.sem.at[1],
            self.sibling,
        )

    def start(self):
        self.pair_copy().start()

    def to_chips(self):
        self.pair_copy().wait()

        def add(t):
            n = lax.rem(self.chip + t, 8)
            self.chip_sum[n] = (
                self.packed[self.core * 8 + n].astype(F32) + self.pair_part[n].astype(F32)
            ).astype(BF16)

        def add_and_send(t):
            add(t)
            n = lax.rem(self.chip + t, 8)
            self.place.copy(
                self.chip_sum.at[n],
                self.chip_parts.at[t],
                self.sem.at[2],
                self.sem.at[3],
                n * 2 + self.core,
            ).start()

        loop(1, 8, add_and_send)
        add(0)

    def to_dp(self):
        wait_bytes(self.chip_parts.at[1:8], self.sem.at[3])
        total = self.chip_sum[self.chip].astype(F32)
        for t in range(1, 8):
            total += self.chip_parts[t].astype(F32)
        self.send_dp(total)

    def send_dp(self, total):
        dp = self.place.dp
        self.dp_parts[dp] = total.astype(BF16)
        loop(
            1,
            8,
            lambda t: self.place.copy_dp(
                self.dp_parts.at[dp], self.sem.at[4], self.sem.at[5], t
            ).start(),
        )

    def block(self, chip):
        at = self.first + (self.core * 8 + chip) * self.part
        return self.total.at[rows_of(at, self.part)]

    def back_copy(self, t):
        block = self.block(self.chip)
        return self.place.copy(
            block,
            block,
            self.sem.at[6],
            self.back_recv.at[t],
            lax.rem(self.chip + t, 8) * 2 + self.core,
        )

    def pass_copy(self, t):
        block = self.block(lax.rem(self.chip + 8 - t, 8))
        return self.place.copy(block, block, self.sem.at[7], self.sem.at[8], self.sibling)

    def dp_total(self):
        wait_bytes(self.dp_parts.at[1:8], self.sem.at[5])
        total = self.dp_parts[0].astype(F32)
        for n in range(1, 8):
            total += self.dp_parts[n].astype(F32)
        return (total * self.scale).astype(BF16)

    def to_all(self):
        self.block(self.chip)[...] = self.dp_total()
        loop(1, 8, lambda t: self.back_copy(t).start())
        self.pass_copy(0).start()

    def to_sibling(self):
        def pass_on(t):
            self.back_copy(t).wait_recv()
            self.pass_copy(t).start()

        loop(1, 8, pass_on)

    def finish(self):
        half = self.total.at[pl.ds(self.first, 8 * self.part)]
        wait_bytes(half, self.sem.at[7])
        wait_bytes(half, self.sem.at[8])
        for n in (2, 4, 6):
            wait_bytes(self.chip_parts.at[1:8], self.sem.at[n])


class Direct(Total):
    def start(self):
        def send(t):
            n = lax.rem(self.place.me + t, 16)
            self.place.copy(
                self.packed.at[n], self.chip_parts.at[t], self.sem.at[2], self.sem.at[3], n
            ).start()

        loop(1, 16, send)

    def block(self, me):
        return self.total.at[rows_of(self.first + me * self.part, self.part)]

    def to_dp(self):
        wait_bytes(self.chip_parts.at[1:16], self.sem.at[3])
        total = self.packed[self.place.me].astype(F32)
        for t in range(1, 16):
            total += self.chip_parts[t].astype(F32)
        self.send_dp(total)

    def to_all(self):
        block = self.block(self.place.me)
        block[...] = self.dp_total()

        def send(t):
            self.place.copy(
                block, block, self.sem.at[6], self.sem.at[7], lax.rem(self.place.me + t, 16)
            ).start()

        loop(1, 16, send)

    def finish(self):
        for n in (2, 6, 7):
            wait_bytes(self.chip_parts.at[1:16], self.sem.at[n])
        wait_bytes(self.dp_parts.at[1:8], self.sem.at[4])


def trunk_kernel(
    scale,
    single_ref,
    single_gain_ref,
    single_bias_ref,
    left_weight_ref,
    right_weight_ref,
    pair_ref,
    cotangent_ref,
    outer_proj_ref,
    residue_ref,
    outer_bias_ref,
    norm_gain_ref,
    norm_bias_ref,
    out_gain_ref,
    out_bias_ref,
    front_ref,
    back_ref,
    out_ref,
    pair_grad_ref,
    single_grad_ref,
    total_ref,
    every_ref,
    cube_ref,
    right_total_ref,
    right_parts,
    single_standard,
    front0_sum,
    front1_sum,
    out0_sum,
    out1_sum,
    first,
    second,
    gate_grad0,
    gate_grad1,
    grad_second,
    sends,
    arrived,
    staged,
    left0,
    right0,
    left1,
    right1,
    grad1,
    grad0,
    kept_sum,
    sent_sum,
    received_sum,
    cells,
    mixed_cells,
    outer_cells,
    wides,
    sums,
    right_total,
    whole,
    mask_ref,
    send_sem,
    recv_sem,
    local_sem,
    half_send,
    half_recv,
    few_sem,
    total_sem,
    total_back,
    *total_refs,
):
    place = Place()
    place.greet()
    me, dp = place.me, place.dp
    own = own_weights(residue_ref, me)
    totals = [
        (Direct if n == 2 else Total)(
            place,
            scale,
            total_ref,
            first_part,
            total_refs[5 * n : 5 * n + 5],
            (total_sem.at[n], total_back.at[n]),
        )
        for n, first_part in enumerate((0, 1024, 2816))
    ]
    standard, single_inverse = norm(single_ref[...].astype(F32), axis=1)
    single_standard[...] = standard
    normed_single = (standard * single_gain_ref[...] + single_bias_ref[...]).astype(BF16)
    factors = nt(normed_single, factor_weights(left_weight_ref, right_weight_ref))
    mine = rows_of(me * I)
    every_ref[mine, :] = (factors * own).astype(BF16)
    place.met()

    def factor_copy(t):
        block = every_ref.at[mine]
        return place.copy(block, block, few_sem.at[0], few_sem.at[1], lax.rem(me + t, 16))

    loop(1, 16, lambda t: factor_copy(t).start())
    for h in range(2):
        mask_ref[h] = own * weight_rows(residue_ref)[h : h + 1]
    for t in range(2):
        for n, ref in enumerate((norm_gain_ref, norm_bias_ref, out_gain_ref, out_bias_ref)):
            wides[4 * t + n] = jnp.broadcast_to(ref[t : t + 1, :], (C, C)).T
    wides[8] = jnp.broadcast_to(outer_bias_ref[...], (C, C)).T
    clear(sums, front0_sum, front1_sum, out0_sum, out1_sum, right_total, outer_cells)
    own_left = every_ref[mine, :][:, :B]
    mixed_rows(own_left, outer_proj_ref, cells.at[0], cube_ref, mixed_cells)
    wait_bytes(every_ref.at[: 15 * I], few_sem.at[1])
    right_rows = every_ref[...].astype(F32).T[B : 2 * B].astype(BF16)

    sems = (send_sem, recv_sem, local_sem)
    swap_sems = (half_send, half_recv)
    me_row, group_row = place.me * I, place.group * I
    travel = [
        Spread(place, sends.at[0], left0, group_row, sems, 0),
        Spread(place, sends.at[1], right0, me_row, sems, 1),
        Collect(place, staged.at[0], arrived.at[0], sems, 2),
        Spread(place, sends.at[2], left1, group_row, sems, 3),
        Spread(place, sends.at[3], right1, group_row, sems, 4),
        Collect(place, staged.at[1], arrived.at[1], sems, 5),
        Spread(place, sends.at[4], grad1, me_row, sems, 6),
        Collect(place, staged.at[2], arrived.at[2], sems, 7),
        Collect(place, staged.at[3], arrived.at[3], sems, 8),
        Spread(place, sends.at[5], grad0, group_row, sems, 9),
        Collect(place, staged.at[4], arrived.at[4], sems, 10),
        Collect(place, staged.at[5], arrived.at[5], sems, 11),
    ]
    (
        send_left0,
        send_right0,
        send_product0,
        send_left1,
        send_right1,
        send_product1,
        send_grad1,
        send_left_grad1,
        send_right_grad1,
        send_grad0,
        send_left_grad0,
        send_right_grad0,
    ) = travel
    swaps = [Swap(place, swap_sems, n) for n in range(4)]

    def over_channels(q, do):
        def step(n):
            for m in range(UNROLL):
                do(q * CQ + n * UNROLL + m, m)

        loop(0, CQ // UNROLL, step)

    def front_first(h, hook=None):
        gain, bias, outer_bias = wide(wides.at[0]), wide(wides.at[1]), wide(wides.at[8])

        def body(p):
            mask_row = mask_pair(mask_ref, p, h)
            mixed = [mixed_cells[pl.ds(2 * p + n, B, stride=I), :].astype(BF16) for n in range(2)]
            term = side_by_side(*[tn(m, right_rows[:, lanes(h)]) for m in mixed]) + outer_bias
            value = (rows_in(pair_ref, p, h) + mask_row * term).astype(BF16)
            first[h, p] = value
            send_factors(
                value.astype(F32), mask_row, gain, bias, front_ref.at[0], cells.at[0], cells.at[1], p
            )

        over_pairs(body, hook)
        cells_out(cells.at[1], sends.at[1], h)
        send_right0.send(h)
        cells_out(cells.at[0], sends.at[0], h)
        send_left0.send(h)

    def forward_right(h):
        send_right0.here(h)
        pieces = range(Q)
        order = [(h, q, 0) for q in pieces] + [(0, q, 1) for q in pieces[h * Q // 2 : (h + 1) * Q // 2]]
        if h == 1:
            order += [(1, q, 1) for q in pieces]
        for half, q, r in order:
            if half == h and r == 0:
                send_right0.arrive(h, q)
            swaps[0].rows(right0, half, q, r)

    def forward_grad(h):
        send_grad1.here(h)
        order = [(q, r) for q in range(Q) for r in range(2)]
        for q, r in order if h == 0 else sorted(order, key=lambda at: at[1]):
            if r == 0:
                send_grad1.arrive(h, q)
            swaps[2].rows(grad1, h, q, r)

    front_first(0)
    front_first(1, lambda: forward_right(0))
    forward_right(1)
    send_left0.arrive_half(0)
    send_left0.arrive_half(1)
    for h in range(2):
        for q in range(Q):
            for n in range(2):
                swaps[0].arrive(right0, n, q, h)

            def multiply(c, m):
                staged[0, c, :, lanes(h)] = nt(left0[c], right0[c, lanes(h), :]).astype(BF16)

            over_channels(q, multiply)
            send_product0.send_piece(h, q)
        send_product0.local(h)

    def middle(h):
        send_product0.arrive_half(h)
        cells_in(arrived.at[0], cells.at[2], h)
        gain0, bias0 = wide(wides.at[0]), wide(wides.at[1])
        out_gain0, out_bias0 = wide(wides.at[2]), wide(wides.at[3])
        gain1, bias1 = wide(wides.at[4]), wide(wides.at[5])

        def body(p):
            product_standard, _ = norm(get_pair(cells.at[2], p))
            product_norm = (product_standard * out_gain0 + out_bias0).astype(BF16)
            linear = tn(out_ref[0], product_norm)
            value = first[h, p].astype(F32)
            standard, _ = norm(value)
            normed = (standard * gain0 + bias0).astype(BF16)
            gate = sigmoid(nn(front_ref[0, 4 * C :, :], normed))
            value = (value + gate * linear).astype(BF16)
            second[h, p] = value
            send_factors(
                value.astype(F32),
                mask_pair(mask_ref, p, h),
                gain1,
                bias1,
                front_ref.at[1],
                cells.at[0],
                cells.at[1],
                p,
            )

        over_pairs(body)
        for n, way in ((0, send_left1), (1, send_right1)):
            cells_out(cells.at[n], sends.at[2 + n], h)
            way.local(h)
        for q in range(Q):
            send_left1.send_piece(h, q)
            send_right1.send_piece(h, q)

    middle(0)
    middle(1)
    def incoming_sums(q, h, r):
        def multiply_sums(c, m):
            whole[m, :, :C] = tn(left1[c, :, lanes(r)], right1[c, :, lanes(h)])
            split_rows(
                place, whole.at[m], kept_sum, sent_sum.at[0], c, r, lanes(h), slice(0, C)
            )

        over_channels(q, multiply_sums)
        swaps[1].sums(sent_sum.at[0], received_sum.at[0], h, q, r)

    for n in range(2):
        for way in (send_left1, send_right1):
            way.here(n)
        for q in range(Q):
            for way in (send_left1, send_right1):
                way.arrive(n, q)
            incoming_sums(q, 0, n)
    for r in range(2):
        for q in range(Q):
            incoming_sums(q, 1, r)

    def add_halves(swap, received, target, way, h):
        for q in range(Q):
            for r in range(2):
                swap.arrive(received, h, q, r)

            def add(c, m):
                target[c, :, lanes(h)] = (
                    kept_sum[c, :, lanes(h)] + received[c, :, lanes(h)].astype(F32)
                ).astype(BF16)

            over_channels(q, add)
            way.send_piece(h, q)
        way.local(h)

    def back_second(h, hook=None):
        send_product1.arrive_half(h)
        cells_in(arrived.at[1], cells.at[2], h)
        gain, bias = wide(wides.at[4]), wide(wides.at[5])
        out_gain, out_bias = wide(wides.at[6]), wide(wides.at[7])

        def body(p):
            gate_grad, product_grad = back_out(
                rows_in(cotangent_ref, p, h),
                get_pair(cells.at[2], p),
                second[h, p].astype(F32),
                gain,
                bias,
                front_ref.at[1],
                out_gain,
                out_bias,
                out_ref.at[1],
                (out1_sum, sums.at[6], sums.at[7]),
            )
            gate_grad1[h, p] = gate_grad
            put_pair(cells.at[3], p, product_grad)

        over_pairs(body, hook)
        cells_out(cells.at[3], sends.at[4], h)
        send_grad1.send(h)

    add_halves(swaps[1], received_sum.at[0], staged.at[1], send_product1, 0)
    back_second(0)
    add_halves(swaps[1], received_sum.at[0], staged.at[1], send_product1, 1)
    forward_grad(0)
    back_second(1)

    def send_right_back(h, q):
        for r in range(2):
            if h == 0 or r == 1:
                swaps[2].arrive(grad1, h, q, r)

        def right_back(c, m):
            staged[3, c, :, lanes(h)] = nn(left1[c], grad1[c, :, lanes(h)]).astype(BF16)

        over_channels(q, right_back)
        send_right_grad1.send_piece(h, q)

    def send_left_back(h, q):
        if h == 0:
            swaps[2].arrive(grad1, 1, q, 0)

        def left_back(c, m):
            staged[2, c, :, lanes(h)] = nt(right1[c], grad1[c, lanes(h), :]).astype(BF16)

        over_channels(q, left_back)
        send_left_grad1.send_piece(h, q)

    for q in range(Q // 2):
        send_right_back(0, q)
    forward_grad(1)
    for q in range(Q // 2, Q):
        send_right_back(0, q)
    send_right_grad1.local(0)
    for q in range(Q):
        send_left_back(0, q)
    send_left_grad1.local(0)
    for q in range(Q):
        send_right_back(1, q)
    send_right_grad1.local(1)
    for q in range(Q):
        send_left_back(1, q)
    send_left_grad1.local(1)

    def back_middle(h, hook=None):
        send_left_grad1.arrive_half(h)
        send_right_grad1.arrive_half(h)
        cells_in(arrived.at[2], cells.at[0], h)
        cells_in(arrived.at[3], cells.at[1], h)
        cells_in(arrived.at[0], cells.at[2], h)
        gain1, bias1, gain0, bias0 = (wide(wides.at[n]) for n in (4, 5, 0, 1))
        out_gain0, out_bias0 = wide(wides.at[2]), wide(wides.at[3])

        def body(p):
            value = back_in(
                rows_in(cotangent_ref, p, h),
                gate_grad1[h, p],
                get_pair(cells.at[0], p),
                get_pair(cells.at[1], p),
                second[h, p].astype(F32),
                mask_pair(mask_ref, p, h),
                gain1,
                bias1,
                front_ref.at[1],
                back_ref.at[1],
                (front1_sum, sums.at[4], sums.at[5]),
            )
            grad_second[h, p] = value
            gate_grad, product_grad = back_out(
                value.astype(F32),
                get_pair(cells.at[2], p),
                first[h, p].astype(F32),
                gain0,
                bias0,
                front_ref.at[0],
                out_gain0,
                out_bias0,
                out_ref.at[0],
                (out0_sum, sums.at[2], sums.at[3]),
            )
            gate_grad0[h, p] = gate_grad
            put_pair(cells.at[3], p, product_grad)

        over_pairs(body, hook)
        cells_out(cells.at[3], sends.at[5], h)
        send_grad0.send(h)

    def right_sums(r):
        send_grad0.here(r)
        for q in range(Q):
            send_grad0.arrive(r, q)

            def multiply_back(c, m):
                whole[m] = tn(grad0[c, :, lanes(r)], left0[c])
                split_rows(
                    place, whole.at[m], kept_sum, sent_sum.at[1], c, r, slice(None), slice(None)
                )

            over_channels(q, multiply_back)
            swaps[3].sums(sent_sum.at[1], received_sum.at[1], 0, q, r)
            if r == 0:
                swaps[3].sums(sent_sum.at[1], received_sum.at[1], 1, q, r)
        if r == 1:
            for q in range(Q):
                swaps[3].sums(sent_sum.at[1], received_sum.at[1], 1, q, r)

    back_middle(0)
    back_middle(1, lambda: right_sums(0))
    for n in range(5):
        totals[0].put(n * C, front1_sum[:, n * C : (n + 1) * C])
    totals[0].put(5 * C, out0_sum[...])
    totals[0].put(6 * C, out1_sum[...])
    totals[0].put(7 * C, jnp.zeros((C, C), F32))
    totals[0].start()
    right_sums(1)
    totals[0].to_chips()
    for h in range(2):
        for q in range(Q):

            def left_back_out(c, m):
                staged[4, c, :, lanes(h)] = nn(grad0[c], right0[c, :, lanes(h)]).astype(BF16)

            over_channels(q, left_back_out)
            send_left_grad0.send_piece(h, q)
        send_left_grad0.local(h)

    def back_first(h):
        send_left_grad0.arrive_half(h)
        send_right_grad0.arrive_half(h)
        cells_in(arrived.at[4], cells.at[0], h)
        cells_in(arrived.at[5], cells.at[1], h)
        gain, bias = wide(wides.at[0]), wide(wides.at[1])

        def body(p):
            mask_row = mask_pair(mask_ref, p, h)
            value = back_in(
                grad_second[h, p].astype(F32),
                gate_grad0[h, p],
                get_pair(cells.at[0], p),
                get_pair(cells.at[1], p),
                first[h, p].astype(F32),
                mask_row,
                gain,
                bias,
                front_ref.at[0],
                back_ref.at[0],
                (front0_sum, sums.at[0], sums.at[1]),
            ).astype(F32)
            outer_grad = value * mask_row
            sums[8] += outer_grad
            outer_grad = outer_grad.astype(BF16)
            for n in range(2):
                pair_grad_ref[2 * p + n, lanes(h), :] = value[:, lanes(n)].T.astype(BF16)
                grad_row = outer_grad[:, lanes(n)]
                rows = pl.ds(2 * p + n, B, stride=I)
                outer_cells[rows, :] += nt(right_rows[:, lanes(h)], grad_row)
                mixed_left = mixed_cells[rows, :].astype(BF16)
                right_total[:B, lanes(h)] += nn(mixed_left, grad_row)

        over_pairs(body)

    add_halves(swaps[3], received_sum.at[1], staged.at[5], send_right_grad0, 0)
    totals[0].to_dp()
    back_first(0)
    add_halves(swaps[3], received_sum.at[1], staged.at[5], send_right_grad0, 1)
    totals[0].to_all()
    back_first(1)

    right_total_ref[...] = right_total[...].T

    def right_copy(t):
        target = lax.rem(me + t, 16)
        return place.copy(
            right_total_ref.at[rows_of(target * I)],
            right_parts.at[t],
            few_sem.at[2],
            few_sem.at[3],
            target,
        )

    loop(1, 16, lambda t: right_copy(t).start())
    for n in range(5):
        totals[1].put(n * C, front0_sum[:, n * C : (n + 1) * C])
    left_single = jnp.zeros((I, B), F32)
    for b in range(B):
        rows = outer_cells[b * I : (b + 1) * I, :].astype(BF16)
        totals[1].put(5 * C + b * B, tn(own_left, rows))
        left_single += nt(rows, cube_ref[b])
    totals[1].put(13 * C, columns(*[sums.at[n] for n in range(9)]))
    totals[1].start()

    wait_bytes(right_parts.at[1:16], few_sem.at[3])
    right_single = right_total_ref[mine, :]
    for t in range(1, 16):
        right_single += right_parts[t]
    both = jnp.concatenate(
        [left_single, right_single[:, :B], jnp.zeros((I, C - 2 * B), F32)], axis=1
    )
    both = (both * own).astype(BF16)
    single_grad = nn(both, factor_weights(left_weight_ref, right_weight_ref))
    standard = single_standard[...]
    normed_single = (standard * single_gain_ref[...] + single_bias_ref[...]).astype(BF16)
    factor_sums = tn(both, normed_single)
    totals[1].to_chips()
    for n in range(8):
        totals[2].put(n * 64, factor_sums[:64, lanes(n)])
    gain_sum = jnp.sum(single_grad * standard, axis=0, keepdims=True)
    bias_sum = jnp.sum(single_grad, axis=0, keepdims=True)
    tail = [gain_sum[:, lanes(n)] for n in range(8)] + [bias_sum[:, lanes(n)] for n in range(8)]
    totals[2].put(4 * C, jnp.concatenate(tail + [jnp.zeros((2 * C - 16, C), F32)], axis=0))
    totals[2].start()
    single_grad_ref[...] = norm_back(
        single_grad * single_gain_ref[...], standard, single_inverse, axis=1
    ).astype(BF16)
    totals[0].to_sibling()
    totals[1].to_dp()
    totals[2].to_dp()
    totals[1].to_all()
    totals[2].to_all()
    totals[1].to_sibling()
    for batch in totals:
        batch.finish()
    wait_bytes(every_ref.at[: 15 * I], few_sem.at[0])
    wait_bytes(right_parts.at[1:16], few_sem.at[2])
    for way in travel:
        way.sent()
    swaps[0].sent(left0)
    swaps[1].sent(left0)
    swaps[2].sent(left0)
    swaps[3].sent(left0)


def unpack_kernel(
    total_ref,
    outer_gain_ref,
    outer_bias_ref,
    outer_left_ref,
    outer_right_ref,
    cube_ref,
    pair_bias_ref,
    norm_gain_ref,
    norm_bias_ref,
    proj_ref,
    gate_ref,
    out_gain_ref,
    out_bias_ref,
    out_ref,
):
    for t in range(2):
        front = 8 - 8 * t
        for n in range(4):
            at = (front + n) * C
            proj_ref[t, :, n * C : (n + 1) * C] = total_ref[at : at + C, :].astype(F32)
        at = (front + 4) * C
        gate_ref[t] = total_ref[at : at + C, :].astype(F32)
        out_ref[t] = total_ref[(5 + t) * C : (6 + t) * C, :].astype(F32)
    cube = total_ref[13 * C : 21 * C, :].astype(F32).reshape(B, B, C)
    cube_ref[...] = jnp.swapaxes(cube, 0, 1).reshape(B * B, C)
    for n in range(8):
        at = 22 * C + n * 64
        outer_left_ref[:, n * C : (n + 1) * C] = total_ref[at : at + B, :].astype(F32)
        outer_right_ref[:, n * C : (n + 1) * C] = total_ref[at + B : at + 2 * B, :].astype(F32)
    small = total_ref[21 * C : 22 * C, :].astype(F32).T
    for t in range(2):
        norm_gain_ref[t : t + 1, :] = small[4 * t : 4 * t + 1]
        norm_bias_ref[t : t + 1, :] = small[4 * t + 1 : 4 * t + 2]
        out_gain_ref[t : t + 1, :] = small[4 * t + 2 : 4 * t + 3]
        out_bias_ref[t : t + 1, :] = small[4 * t + 3 : 4 * t + 4]
    pair_bias_ref[...] = small[8:9]
    rows = total_ref[26 * C : 26 * C + 16, :].astype(F32)
    outer_gain_ref[...] = rows[:8]
    outer_bias_ref[...] = rows[8:16]


def call(kernel, outs, scratch, args, name, collective=None, flops=0):
    return pl.pallas_call(
        kernel,
        out_shape=[jax.ShapeDtypeStruct(shape, dtype) for shape, dtype in outs],
        in_specs=[pl.BlockSpec(memory_space=pltpu.VMEM)] * len(args),
        out_specs=[pl.BlockSpec(memory_space=pltpu.VMEM)] * len(outs),
        scratch_shapes=scratch,
        name=name,
        compiler_params=pltpu.CompilerParams(
            collective_id=collective,
            has_side_effects=collective is not None,
            vmem_limit_bytes=VMEM_LIMIT,
        ),
    )(*args)


DMA = pltpu.SemaphoreType.DMA
BY_CHANNEL = (C, I, J)
BY_PAIR = (2, I // 2, C, J)
HALF = (16, C, J)
EVERY = (16, J, J)


def local(
    single_state,
    pair_state,
    residue_mask,
    pair_cotangent,
    outer_norm_gain,
    outer_norm_bias,
    outer_left,
    outer_right,
    outer_proj,
    outer_bias,
    triangle_norm_gain,
    triangle_norm_bias,
    triangle_proj,
    triangle_gate,
    triangle_out_gain,
    triangle_out_bias,
    triangle_out,
):
    residues = residue_mask.reshape(2, C)
    left_weight, right_weight = outer_left.T, outer_right.T
    single = single_state[0]
    single_gain, single_bias = outer_norm_gain[None, :], outer_norm_bias[None, :]
    back_weight = jnp.concatenate([triangle_proj, triangle_gate], axis=2)
    front_weight = jnp.swapaxes(back_weight, 1, 2)

    scale = 1.0 / float(lax.axis_size("dp") * J)
    pair_gradient, single_gradient, total = call(
        functools.partial(trunk_kernel, scale),
        [((I, J, C), BF16), ((I, single.shape[1]), BF16), ((28 * C, C), BF16)],
        [
            pltpu.VMEM((J, C), BF16),
            pltpu.VMEM((B, B, C), BF16),
            pltpu.VMEM((J, C), F32),
            pltpu.VMEM((16, I, C), F32),
            pltpu.VMEM((I, single.shape[1]), F32),
            pltpu.VMEM((C, 5 * C), F32),
            pltpu.VMEM((C, 5 * C), F32),
            pltpu.VMEM((C, C), F32),
            pltpu.VMEM((C, C), F32),
        ]
        + [pltpu.VMEM(BY_PAIR, BF16)] * 5
        + [pltpu.VMEM((6,) + BY_CHANNEL, BF16)] * 2
        + [pltpu.VMEM((6,) + HALF, BF16)]
        + [pltpu.VMEM(shape, BF16) for shape in (HALF, EVERY, HALF, HALF, EVERY, HALF)]
        + [
            pltpu.VMEM(HALF, F32),
            pltpu.VMEM((2,) + HALF, BF16),
            pltpu.VMEM((2,) + HALF, BF16),
            pltpu.VMEM((4, C * I, C), F32),
            pltpu.VMEM((B * I, C), F32),
            pltpu.VMEM((B * I, C), F32),
            pltpu.VMEM((9, C, C), F32),
            pltpu.VMEM((9, C, J), F32),
            pltpu.VMEM((C, J), F32),
            pltpu.VMEM((UNROLL, C, J), F32),
            pltpu.VMEM((2, I, C), F32),
            DMA((12,)),
            DMA((12, 2, Q)),
            DMA((12, 2)),
            DMA((4,)),
            DMA((4, 2, Q, 2)),
            DMA((4,)),
            DMA((3, 9)),
            DMA((3, 8)),
        ]
        + [
            pltpu.VMEM((count, part, C), BF16)
            for part, parts in ((64, 8), (112, 8), (48, 16))
            for count in (16, 8, 8, parts, 8)
        ],
        (
            single,
            single_gain,
            single_bias,
            left_weight,
            right_weight,
            pair_state[0],
            pair_cotangent[0],
            outer_proj,
            residues,
            outer_bias[None, :],
            triangle_norm_gain,
            triangle_norm_bias,
            triangle_out_gain,
            triangle_out_bias,
            front_weight,
            back_weight,
            triangle_out,
        ),
        "trunk",
        collective=0,
    )
    unpacked = call(
        unpack_kernel,
        [
            ((8, C), F32),
            ((8, C), F32),
            (left_weight.shape, F32),
            (right_weight.shape, F32),
            (outer_proj.shape, F32),
            ((1, C), F32),
            ((2, C), F32),
            ((2, C), F32),
            (triangle_proj.shape, F32),
            (triangle_gate.shape, F32),
            ((2, C), F32),
            ((2, C), F32),
            (triangle_out.shape, F32),
        ],
        [],
        (total,),
        "unpack",
    )
    unpacked = list(unpacked)
    unpacked[0] = unpacked[0].reshape(-1)
    unpacked[1] = unpacked[1].reshape(-1)
    unpacked[5] = unpacked[5].reshape(-1)
    unpacked[2] = unpacked[2].T
    unpacked[3] = unpacked[3].T
    return (single_gradient[None], pair_gradient[None]) + tuple(unpacked)


def solution(mesh):
    whole = P()
    rows = P("dp", "axial", None)
    cells = P("dp", "axial", None, None)
    return jax.shard_map(
        local,
        mesh=mesh,
        in_specs=(rows, cells, P("dp", None), cells) + (whole,) * 13,
        out_specs=(rows, cells) + (whole,) * 13,
        check_vma=False,
    )
```

```python
import functools

import jax
import jax.numpy as jnp
from jax import lax
from jax.experimental import pallas as pl
from jax.experimental.pallas import tpu as pltpu
from jax.sharding import PartitionSpec as P

EPSILON = 1e-05
F32 = jnp.float32
BF16 = jnp.bfloat16
MESH = pl.DeviceIdType.MESH
C = 128
I = 16
J = 256
B = 32
Q = 4
CQ = 4
UNROLL = 4
VMEM_LIMIT = 60 * 2**20


def nn(a, b):
    return lax.dot_general(a, b, (((1,), (0,)), ((), ())), preferred_element_type=F32)


def nt(a, b):
    return lax.dot_general(a, b, (((1,), (1,)), ((), ())), preferred_element_type=F32)


def tn(a, b):
    return lax.dot_general(a, b, (((0,), (0,)), ((), ())), preferred_element_type=F32)


def sigmoid(x):
    return 0.5 * jnp.tanh(0.5 * x) + 0.5


def norm(x, axis=0):
    centred = x - jnp.mean(x, axis=axis, keepdims=True)
    variance = jnp.mean(centred * centred, axis=axis, keepdims=True)
    inverse = lax.rsqrt(variance + EPSILON)
    return centred * inverse, inverse


def norm_back(scaled, standard, inverse, axis=0):
    first = jnp.mean(scaled, axis=axis, keepdims=True)
    second = jnp.mean(scaled * standard, axis=axis, keepdims=True)
    return inverse * (scaled - first - standard * second)


def put_pair(cells, p, value):
    cells[pl.ds(2 * p, C, stride=I), :] = value[:, :C]
    cells[pl.ds(2 * p + 1, C, stride=I), :] = value[:, C:]


def get_pair(cells, p):
    return side_by_side(cells[pl.ds(2 * p, C, stride=I), :], cells[pl.ds(2 * p + 1, C, stride=I), :])


def side_by_side(a, b):
    return jnp.concatenate([a, b], axis=1)


def lanes(h):
    return slice(h * C, (h + 1) * C)


def cells_out(cells, out_ref, h):
    def step(n, _):
        part = cells[pl.ds(pl.multiple_of(n * 256, 256), 256), :]
        out_ref[pl.ds(n * 16, 16), :, lanes(h)] = part.reshape(16, I, C).astype(BF16)
        return 0

    lax.fori_loop(0, 8, step, 0)


def cells_in(in_ref, cells, h):
    def step(n, _):
        part = in_ref[pl.ds(n * 16, 16), :, lanes(h)]
        cells[pl.ds(pl.multiple_of(n * 256, 256), 256), :] = part.astype(F32).reshape(256, C)
        return 0

    lax.fori_loop(0, 8, step, 0)


def rows_in(ref, p, h):
    return side_by_side(
        ref[2 * p, lanes(h), :].astype(F32).T, ref[2 * p + 1, lanes(h), :].astype(F32).T
    )


def weight_rows(residue_ref):
    return residue_ref[...].astype(F32)


def own_weights(residue_ref, me):
    weights = weight_rows(residue_ref)
    flat = side_by_side(weights[0:1], weights[1:2])
    lane = lax.broadcasted_iota(jnp.int32, (I, J), 1)
    row = lax.broadcasted_iota(jnp.int32, (I, J), 0) + me * I
    return jnp.sum(jnp.where(lane == row, flat, 0.0), axis=1, keepdims=True)


def mask_pair(mask_ref, p, h):
    return side_by_side(
        mask_ref[h, pl.ds(2 * p, 1), :], mask_ref[h, pl.ds(2 * p + 1, 1), :]
    )


def wide(ref):
    return side_by_side(ref[...], ref[...])


def send_factors(pair_in, mask_row, gain, bias, front_ref, left_cells, right_cells, p):
    standard, _ = norm(pair_in)
    normed = (standard * gain + bias).astype(BF16)
    projected = nn(front_ref[: 4 * C, :], normed)
    put_pair(left_cells, p, mask_row * sigmoid(projected[:C]) * projected[C : 2 * C])
    put_pair(right_cells, p, mask_row * sigmoid(projected[2 * C : 3 * C]) * projected[3 * C :])


def over_pairs(body, hook=None, at=4):
    def step(n, _):
        if hook is not None:
            pl.when(4 * n == at)(hook)
        for m in range(4):
            body(4 * n + m)
        return 0

    lax.fori_loop(0, I // 8, step, 0)


def factor_weights(left_ref, right_ref):
    empty = jnp.zeros((C - 2 * B, left_ref.shape[1]), BF16)
    return jnp.concatenate([left_ref[...], right_ref[...], empty], axis=0)


def mixed_rows(own_left, outer_proj_ref, rows, cube_ref, mixed_cells):
    rows[: B * B, :] = outer_proj_ref[...].astype(F32)
    for b in range(B):
        cube_ref[b] = rows[pl.ds(b, B, stride=B), :].astype(BF16)
        mixed_cells[b * I : (b + 1) * I, :] = nn(own_left, cube_ref[b])


def back_out(cotangent, product, pair_in, gain, bias, front_ref, out_gain, out_bias, out_ref, sums):
    out_sum, out_gain_sum, out_bias_sum = sums
    product_standard, product_inverse = norm(product)
    product_norm = (product_standard * out_gain + out_bias).astype(BF16)
    linear = tn(out_ref[...], product_norm)
    standard, _ = norm(pair_in)
    normed = (standard * gain + bias).astype(BF16)
    gate = sigmoid(nn(front_ref[4 * C :, :], normed))
    linear_grad = (cotangent * gate).astype(BF16)
    gate_grad = (cotangent * linear * gate * (1.0 - gate)).astype(BF16)
    out_sum[...] += nt(product_norm, linear_grad)
    norm_grad = nn(out_ref[...], linear_grad)
    out_gain_sum[...] += norm_grad * product_standard
    out_bias_sum[...] += norm_grad
    return gate_grad, norm_back(norm_grad * out_gain, product_standard, product_inverse)


def back_in(
    cotangent,
    gate_grad,
    left_grad,
    right_grad,
    pair_in,
    mask_row,
    gain,
    bias,
    front_ref,
    back_ref,
    sums,
):
    front_sum, gain_sum, bias_sum = sums
    standard, inverse = norm(pair_in)
    normed = (standard * gain + bias).astype(BF16)
    projected = nn(front_ref[: 4 * C, :], normed)
    grads = []
    for at, side in ((0, left_grad), (2 * C, right_grad)):
        gate = sigmoid(projected[at : at + C])
        masked = side * mask_row * gate
        grads.append((masked * projected[at + C : at + 2 * C] * (1.0 - gate)).astype(BF16))
        grads.append(masked.astype(BF16))
    grads = jnp.concatenate(grads + [gate_grad], axis=0)
    front_sum[...] += nt(normed, grads)
    normed_grad = nn(back_ref[...], grads)
    gain_sum[...] += normed_grad * standard
    bias_sum[...] += normed_grad
    return (cotangent + norm_back(normed_grad * gain, standard, inverse)).astype(BF16)


def clear(*refs):
    for ref in refs:
        ref[...] = jnp.zeros(ref.shape, ref.dtype)


def columns(*refs):
    made = [jnp.sum(ref[...], axis=1, keepdims=True) for ref in refs]
    lane = lax.broadcasted_iota(jnp.int32, (C, C), 1)
    total = jnp.zeros((C, C), F32)
    for n, column in enumerate(made):
        total = jnp.where(lane == n, column, total)
    return total


class Place:
    def __init__(self):
        self.me = lax.axis_index("axial")
        self.dp = lax.axis_index("dp")
        self.half = lax.rem(self.me // 2, 2)
        self.group = (self.me // 4) * 2 + lax.rem(self.me, 2)
        self.other = self.me + 2 - 4 * self.half

    def axial(self, group):
        return (group // 2) * 4 + self.half * 2 + lax.rem(group, 2)

    def peer(self, t):
        n = t - 1
        turn = lax.rem(n, 3)
        step = (2 * turn + 1 - 3 * (turn // 2)) * (1 - n // 6)
        core = lax.rem(self.me + n // 3 + n // 6, 2)
        return lax.rem(self.group // 2 + step, 4) * 2 + core

    def greet(self):
        barrier = pltpu.get_barrier_semaphore()

        def signal(t):
            pl.semaphore_signal(
                barrier,
                inc=1,
                device_id=(self.dp, lax.rem(self.me + t, 16)),
                device_id_type=MESH,
            )

        def signal_dp(t):
            pl.semaphore_signal(
                barrier,
                inc=1,
                device_id=(lax.rem(self.dp + t, 8), self.me),
                device_id_type=MESH,
            )

        loop(1, 16, signal)
        loop(1, 8, signal_dp)

    def met(self):
        pl.semaphore_wait(pltpu.get_barrier_semaphore(), 22)

    def copy(self, source, target, send_sem, recv_sem, axial):
        return pltpu.make_async_remote_copy(
            src_ref=source,
            dst_ref=target,
            send_sem=send_sem,
            recv_sem=recv_sem,
            device_id=(self.dp, axial),
            device_id_type=MESH,
        )

    def copy_dp(self, block, send_sem, recv_sem, t):
        return pltpu.make_async_remote_copy(
            src_ref=block,
            dst_ref=block,
            send_sem=send_sem,
            recv_sem=recv_sem,
            device_id=(lax.rem(self.dp + t, 8), self.me),
            device_id_type=MESH,
        )


def loop(first, last, do):
    def step(n, _):
        do(n)
        return 0

    lax.fori_loop(first, last, step, 0)


def rows_of(at, count=I):
    return pl.ds(pl.multiple_of(at, 16), count)


def piece(q):
    return pl.ds(q * CQ, CQ)


def wait_bytes(ref, sem):
    pltpu.make_async_copy(ref, ref, sem).wait()


class Travel:
    def __init__(self, place, source, target, sems, at):
        self.place, self.source, self.target = place, source, target
        self.send_sem, self.recv_sem, self.local_sem = (sem.at[at] for sem in sems)

    def send(self, h):
        pltpu.make_async_copy(*self.ends(h, self.place.group, slice(None)), self.local_sem.at[h]).start()
        for q in range(Q):
            self.send_piece(h, q)

    def send_piece(self, h, q):
        def start(t):
            group = self.place.peer(t)
            self.place.copy(
                *self.ends(h, group, q),
                self.send_sem,
                self.recv_sem.at[h, q],
                self.place.axial(group),
            ).start()

        loop(1, 8, start)

    def local(self, h):
        pltpu.make_async_copy(*self.ends(h, self.place.group, slice(None)), self.local_sem.at[h]).start()

    def here(self, h):
        pltpu.make_async_copy(*self.ends(h, self.place.group, slice(None)), self.local_sem.at[h]).wait()

    def arrive(self, h, q):
        wait_bytes(self.by_channel().at[: 7 * CQ, :, lanes(h)], self.recv_sem.at[h, q])

    def arrive_half(self, h):
        self.here(h)
        for q in range(Q):
            self.arrive(h, q)

    def sent(self):
        wait_bytes(self.by_channel().at[: 7 * 16], self.send_sem)


class Spread(Travel):
    def __init__(self, place, source, target, row, sems, at):
        super().__init__(place, source, target, sems, at)
        self.row = row

    def by_channel(self):
        return self.source

    def ends(self, h, group, q):
        if isinstance(q, slice):
            channels, kept = pl.ds(group * 16, 16), q
        else:
            channels, kept = pl.ds(group * 16 + q * CQ, CQ), piece(q)
        return (
            self.source.at[channels, :, lanes(h)],
            self.target.at[kept, rows_of(self.row), lanes(h)],
        )


class Collect(Travel):
    def by_channel(self):
        return self.target

    def ends(self, h, group, q):
        mine = self.place.group * 16
        if isinstance(q, slice):
            channels, kept = pl.ds(mine, 16), q
        else:
            channels, kept = pl.ds(mine + q * CQ, CQ), piece(q)
        return (
            self.source.at[kept, rows_of(group * I), lanes(h)],
            self.target.at[channels, :, lanes(h)],
        )


class Swap:
    def __init__(self, place, sems, at):
        self.place = place
        self.send_sem, self.recv_sem = (sem.at[at] for sem in sems)

    def rows(self, ref, h, q, r):
        for x in (2 * r, 2 * r + 1):
            block = ref.at[piece(q), rows_of(x * 64 + self.place.half * 32, 32), lanes(h)]
            self.place.copy(
                block, block, self.send_sem, self.recv_sem.at[h, q, r], self.place.other
            ).start()

    def sums(self, sent, received, h, q, r):
        where = (piece(q), slice(64 * r, 64 * r + 64), lanes(h))
        self.place.copy(
            sent.at[where],
            received.at[where],
            self.send_sem,
            self.recv_sem.at[h, q, r],
            self.place.other,
        ).start()

    def arrive(self, ref, h, q, r):
        wait_bytes(ref.at[piece(q), :64, lanes(h)], self.recv_sem.at[h, q, r])

    def sent(self, ref):
        wait_bytes(ref, self.send_sem)


def split_rows(place, whole, kept, sent, channel, r, to_lanes, of_lanes):
    for n in range(2):
        to = slice(64 * r + 32 * n, 64 * r + 32 * n + 32)
        kept[channel, to, to_lanes] = whole[rows_of(n * 64 + place.half * 32, 32), of_lanes]
        sent[channel, to, to_lanes] = whole[
            rows_of(n * 64 + 32 - place.half * 32, 32), of_lanes
        ].astype(BF16)


class Total:
    def __init__(self, place, scale, total, first_part, refs, sems):
        self.place, self.scale, self.total, self.first = place, scale, total, first_part
        self.packed, self.pair_part, self.chip_sum, self.chip_parts, self.dp_parts = refs
        self.sem, self.back_recv = sems
        self.part = self.packed.shape[1]
        self.core = lax.rem(place.me, 2)
        self.chip = place.me // 2
        self.sibling = place.me + 1 - 2 * self.core

    def put(self, at, value):
        count, part = value.shape[0], self.part
        while count:
            room = min(count, part - at % part)
            self.packed[at // part, at % part : at % part + room, :] = value[:room].astype(BF16)
            at, value, count = at + room, value[room:], count - room

    def pair_copy(self):
        return self.place.copy(
            self.packed.at[pl.ds(8 - 8 * self.core, 8)],
            self.pair_part,
            self.sem.at[0],
            self.sem.at[1],
            self.sibling,
        )

    def start(self):
        self.pair_copy().start()

    def to_chips(self):
        self.pair_copy().wait()

        def add(t):
            n = lax.rem(self.chip + t, 8)
            self.chip_sum[n] = (
                self.packed[self.core * 8 + n].astype(F32) + self.pair_part[n].astype(F32)
            ).astype(BF16)

        def add_and_send(t):
            add(t)
            n = lax.rem(self.chip + t, 8)
            self.place.copy(
                self.chip_sum.at[n],
                self.chip_parts.at[t],
                self.sem.at[2],
                self.sem.at[3],
                n * 2 + self.core,
            ).start()

        loop(1, 8, add_and_send)
        add(0)

    def to_dp(self):
        wait_bytes(self.chip_parts.at[1:8], self.sem.at[3])
        total = self.chip_sum[self.chip].astype(F32)
        for t in range(1, 8):
            total += self.chip_parts[t].astype(F32)
        self.send_dp(total)

    def send_dp(self, total):
        dp = self.place.dp
        self.dp_parts[dp] = total.astype(BF16)
        loop(
            1,
            8,
            lambda t: self.place.copy_dp(
                self.dp_parts.at[dp], self.sem.at[4], self.sem.at[5], t
            ).start(),
        )

    def block(self, chip):
        at = self.first + (self.core * 8 + chip) * self.part
        return self.total.at[rows_of(at, self.part)]

    def back_copy(self, t):
        block = self.block(self.chip)
        return self.place.copy(
            block,
            block,
            self.sem.at[6],
            self.back_recv.at[t],
            lax.rem(self.chip + t, 8) * 2 + self.core,
        )

    def pass_copy(self, t):
        block = self.block(lax.rem(self.chip + 8 - t, 8))
        return self.place.copy(block, block, self.sem.at[7], self.sem.at[8], self.sibling)

    def dp_total(self):
        wait_bytes(self.dp_parts.at[1:8], self.sem.at[5])
        total = self.dp_parts[0].astype(F32)
        for n in range(1, 8):
            total += self.dp_parts[n].astype(F32)
        return (total * self.scale).astype(BF16)

    def to_all(self):
        self.block(self.chip)[...] = self.dp_total()
        loop(1, 8, lambda t: self.back_copy(t).start())
        self.pass_copy(0).start()

    def to_sibling(self):
        def pass_on(t):
            self.back_copy(t).wait_recv()
            self.pass_copy(t).start()

        loop(1, 8, pass_on)

    def finish(self):
        half = self.total.at[pl.ds(self.first, 8 * self.part)]
        wait_bytes(half, self.sem.at[7])
        wait_bytes(half, self.sem.at[8])
        for n in (2, 4, 6):
            wait_bytes(self.chip_parts.at[1:8], self.sem.at[n])


class Direct(Total):
    def start(self):
        def send(t):
            n = lax.rem(self.place.me + t, 16)
            self.place.copy(
                self.packed.at[n], self.chip_parts.at[t], self.sem.at[2], self.sem.at[3], n
            ).start()

        loop(1, 16, send)

    def block(self, me):
        return self.total.at[rows_of(self.first + me * self.part, self.part)]

    def to_dp(self):
        wait_bytes(self.chip_parts.at[1:16], self.sem.at[3])
        total = self.packed[self.place.me].astype(F32)
        for t in range(1, 16):
            total += self.chip_parts[t].astype(F32)
        self.send_dp(total)

    def to_all(self):
        block = self.block(self.place.me)
        block[...] = self.dp_total()

        def send(t):
            self.place.copy(
                block, block, self.sem.at[6], self.sem.at[7], lax.rem(self.place.me + t, 16)
            ).start()

        loop(1, 16, send)

    def finish(self):
        for n in (2, 6, 7):
            wait_bytes(self.chip_parts.at[1:16], self.sem.at[n])
        wait_bytes(self.dp_parts.at[1:8], self.sem.at[4])


def trunk_kernel(
    scale,
    single_ref,
    single_gain_ref,
    single_bias_ref,
    left_weight_ref,
    right_weight_ref,
    pair_ref,
    cotangent_ref,
    outer_proj_ref,
    residue_ref,
    outer_bias_ref,
    norm_gain_ref,
    norm_bias_ref,
    out_gain_ref,
    out_bias_ref,
    front_ref,
    back_ref,
    out_ref,
    pair_grad_ref,
    single_grad_ref,
    total_ref,
    every_ref,
    cube_ref,
    right_total_ref,
    right_parts,
    single_standard,
    front0_sum,
    front1_sum,
    out0_sum,
    out1_sum,
    first,
    second,
    gate_grad0,
    gate_grad1,
    grad_second,
    sends,
    arrived,
    staged,
    left0,
    right0,
    left1,
    right1,
    grad1,
    grad0,
    kept_sum,
    sent_sum,
    received_sum,
    cells,
    mixed_cells,
    outer_cells,
    wides,
    sums,
    right_total,
    whole,
    mask_ref,
    send_sem,
    recv_sem,
    local_sem,
    half_send,
    half_recv,
    few_sem,
    total_sem,
    total_back,
    *total_refs,
):
    place = Place()
    place.greet()
    me, dp = place.me, place.dp
    own = own_weights(residue_ref, me)
    totals = [
        (Direct if n == 2 else Total)(
            place,
            scale,
            total_ref,
            first_part,
            total_refs[5 * n : 5 * n + 5],
            (total_sem.at[n], total_back.at[n]),
        )
        for n, first_part in enumerate((0, 1024, 2816))
    ]
    standard, single_inverse = norm(single_ref[...].astype(F32), axis=1)
    single_standard[...] = standard
    normed_single = (standard * single_gain_ref[...] + single_bias_ref[...]).astype(BF16)
    factors = nt(normed_single, factor_weights(left_weight_ref, right_weight_ref))
    mine = rows_of(me * I)
    every_ref[mine, :] = (factors * own).astype(BF16)
    place.met()

    def factor_copy(t):
        block = every_ref.at[mine]
        return place.copy(block, block, few_sem.at[0], few_sem.at[1], lax.rem(me + t, 16))

    loop(1, 16, lambda t: factor_copy(t).start())
    for h in range(2):
        mask_ref[h] = own * weight_rows(residue_ref)[h : h + 1]
    for t in range(2):
        for n, ref in enumerate((norm_gain_ref, norm_bias_ref, out_gain_ref, out_bias_ref)):
            wides[4 * t + n] = jnp.broadcast_to(ref[t : t + 1, :], (C, C)).T
    wides[8] = jnp.broadcast_to(outer_bias_ref[...], (C, C)).T
    clear(sums, front0_sum, front1_sum, out0_sum, out1_sum, right_total, outer_cells)
    own_left = every_ref[mine, :][:, :B]
    mixed_rows(own_left, outer_proj_ref, cells.at[0], cube_ref, mixed_cells)
    wait_bytes(every_ref.at[: 15 * I], few_sem.at[1])
    right_rows = every_ref[...].astype(F32).T[B : 2 * B].astype(BF16)

    sems = (send_sem, recv_sem, local_sem)
    swap_sems = (half_send, half_recv)
    me_row, group_row = place.me * I, place.group * I
    travel = [
        Spread(place, sends.at[0], left0, group_row, sems, 0),
        Spread(place, sends.at[1], right0, me_row, sems, 1),
        Collect(place, staged.at[0], arrived.at[0], sems, 2),
        Spread(place, sends.at[2], left1, group_row, sems, 3),
        Spread(place, sends.at[3], right1, group_row, sems, 4),
        Collect(place, staged.at[1], arrived.at[1], sems, 5),
        Spread(place, sends.at[4], grad1, me_row, sems, 6),
        Collect(place, staged.at[2], arrived.at[2], sems, 7),
        Collect(place, staged.at[3], arrived.at[3], sems, 8),
        Spread(place, sends.at[5], grad0, group_row, sems, 9),
        Collect(place, staged.at[4], arrived.at[4], sems, 10),
        Collect(place, staged.at[5], arrived.at[5], sems, 11),
    ]
    (
        send_left0,
        send_right0,
        send_product0,
        send_left1,
        send_right1,
        send_product1,
        send_grad1,
        send_left_grad1,
        send_right_grad1,
        send_grad0,
        send_left_grad0,
        send_right_grad0,
    ) = travel
    swaps = [Swap(place, swap_sems, n) for n in range(4)]

    def over_channels(q, do):
        def step(n):
            for m in range(UNROLL):
                do(q * CQ + n * UNROLL + m, m)

        loop(0, CQ // UNROLL, step)

    def front_first(h, hook=None):
        gain, bias, outer_bias = wide(wides.at[0]), wide(wides.at[1]), wide(wides.at[8])

        def body(p):
            mask_row = mask_pair(mask_ref, p, h)
            mixed = [mixed_cells[pl.ds(2 * p + n, B, stride=I), :].astype(BF16) for n in range(2)]
            term = side_by_side(*[tn(m, right_rows[:, lanes(h)]) for m in mixed]) + outer_bias
            value = (rows_in(pair_ref, p, h) + mask_row * term).astype(BF16)
            first[h, p] = value
            send_factors(
                value.astype(F32), mask_row, gain, bias, front_ref.at[0], cells.at[0], cells.at[1], p
            )

        over_pairs(body, hook)
        cells_out(cells.at[1], sends.at[1], h)
        send_right0.send(h)
        cells_out(cells.at[0], sends.at[0], h)
        send_left0.send(h)

    def forward_right(h):
        send_right0.here(h)
        pieces = range(Q)
        order = [(h, q, 0) for q in pieces] + [(0, q, 1) for q in pieces[h * Q // 2 : (h + 1) * Q // 2]]
        if h == 1:
            order += [(1, q, 1) for q in pieces]
        for half, q, r in order:
            if half == h and r == 0:
                send_right0.arrive(h, q)
            swaps[0].rows(right0, half, q, r)

    def forward_grad(h):
        send_grad1.here(h)
        order = [(q, r) for q in range(Q) for r in range(2)]
        for q, r in order if h == 0 else sorted(order, key=lambda at: at[1]):
            if r == 0:
                send_grad1.arrive(h, q)
            swaps[2].rows(grad1, h, q, r)

    front_first(0)
    front_first(1, lambda: forward_right(0))
    forward_right(1)
    send_left0.arrive_half(0)
    send_left0.arrive_half(1)
    for h in range(2):
        for q in range(Q):
            for n in range(2):
                swaps[0].arrive(right0, n, q, h)

            def multiply(c, m):
                staged[0, c, :, lanes(h)] = nt(left0[c], right0[c, lanes(h), :]).astype(BF16)

            over_channels(q, multiply)
            send_product0.send_piece(h, q)
        send_product0.local(h)

    def middle(h):
        send_product0.arrive_half(h)
        cells_in(arrived.at[0], cells.at[2], h)
        gain0, bias0 = wide(wides.at[0]), wide(wides.at[1])
        out_gain0, out_bias0 = wide(wides.at[2]), wide(wides.at[3])
        gain1, bias1 = wide(wides.at[4]), wide(wides.at[5])

        def body(p):
            product_standard, _ = norm(get_pair(cells.at[2], p))
            product_norm = (product_standard * out_gain0 + out_bias0).astype(BF16)
            linear = tn(out_ref[0], product_norm)
            value = first[h, p].astype(F32)
            standard, _ = norm(value)
            normed = (standard * gain0 + bias0).astype(BF16)
            gate = sigmoid(nn(front_ref[0, 4 * C :, :], normed))
            value = (value + gate * linear).astype(BF16)
            second[h, p] = value
            send_factors(
                value.astype(F32),
                mask_pair(mask_ref, p, h),
                gain1,
                bias1,
                front_ref.at[1],
                cells.at[0],
                cells.at[1],
                p,
            )

        over_pairs(body)
        for n, way in ((0, send_left1), (1, send_right1)):
            cells_out(cells.at[n], sends.at[2 + n], h)
            way.local(h)
        for way in (send_left1, send_right1):
            for q in range(Q):
                way.send_piece(h, q)

    middle(0)
    middle(1)
    def incoming_sums(q, h, r):
        def multiply_sums(c, m):
            whole[m, :, :C] = tn(left1[c, :, lanes(r)], right1[c, :, lanes(h)])
            split_rows(
                place, whole.at[m], kept_sum, sent_sum.at[0], c, r, lanes(h), slice(0, C)
            )

        over_channels(q, multiply_sums)
        swaps[1].sums(sent_sum.at[0], received_sum.at[0], h, q, r)

    for n in range(2):
        for way in (send_left1, send_right1):
            way.here(n)
        for q in range(Q):
            send_left1.arrive(n, q)
            if n == 0:
                send_right1.arrive(0, q)
            incoming_sums(q, 0, n)
    for q in range(Q):
        send_right1.arrive(1, q)
        for r in range(2):
            incoming_sums(q, 1, r)

    def add_halves(swap, received, target, way, h):
        for q in range(Q):
            for r in range(2):
                swap.arrive(received, h, q, r)

            def add(c, m):
                target[c, :, lanes(h)] = (
                    kept_sum[c, :, lanes(h)] + received[c, :, lanes(h)].astype(F32)
                ).astype(BF16)

            over_channels(q, add)
            way.send_piece(h, q)
        way.local(h)

    def back_second(h, hook=None):
        send_product1.arrive_half(h)
        cells_in(arrived.at[1], cells.at[2], h)
        gain, bias = wide(wides.at[4]), wide(wides.at[5])
        out_gain, out_bias = wide(wides.at[6]), wide(wides.at[7])

        def body(p):
            gate_grad, product_grad = back_out(
                rows_in(cotangent_ref, p, h),
                get_pair(cells.at[2], p),
                second[h, p].astype(F32),
                gain,
                bias,
                front_ref.at[1],
                out_gain,
                out_bias,
                out_ref.at[1],
                (out1_sum, sums.at[6], sums.at[7]),
            )
            gate_grad1[h, p] = gate_grad
            put_pair(cells.at[3], p, product_grad)

        over_pairs(body, hook)
        cells_out(cells.at[3], sends.at[4], h)
        send_grad1.send(h)

    add_halves(swaps[1], received_sum.at[0], staged.at[1], send_product1, 0)
    back_second(0)
    add_halves(swaps[1], received_sum.at[0], staged.at[1], send_product1, 1)
    forward_grad(0)
    back_second(1)

    def send_right_back(h, q):
        for r in range(2):
            if h == 0 or r == 1:
                swaps[2].arrive(grad1, h, q, r)

        def right_back(c, m):
            staged[3, c, :, lanes(h)] = nn(left1[c], grad1[c, :, lanes(h)]).astype(BF16)

        over_channels(q, right_back)
        send_right_grad1.send_piece(h, q)

    def send_left_back(h, q):
        if h == 0:
            swaps[2].arrive(grad1, 1, q, 0)

        def left_back(c, m):
            staged[2, c, :, lanes(h)] = nt(right1[c], grad1[c, lanes(h), :]).astype(BF16)

        over_channels(q, left_back)
        send_left_grad1.send_piece(h, q)

    for q in range(Q // 2):
        send_right_back(0, q)
    forward_grad(1)
    for q in range(Q // 2, Q):
        send_right_back(0, q)
    send_right_grad1.local(0)
    for q in range(Q):
        send_left_back(0, q)
    send_left_grad1.local(0)
    for q in range(Q):
        send_right_back(1, q)
    send_right_grad1.local(1)
    for q in range(Q):
        send_left_back(1, q)
    send_left_grad1.local(1)

    def back_middle(h, hook=None):
        send_left_grad1.arrive_half(h)
        send_right_grad1.arrive_half(h)
        cells_in(arrived.at[2], cells.at[0], h)
        cells_in(arrived.at[3], cells.at[1], h)
        cells_in(arrived.at[0], cells.at[2], h)
        gain1, bias1, gain0, bias0 = (wide(wides.at[n]) for n in (4, 5, 0, 1))
        out_gain0, out_bias0 = wide(wides.at[2]), wide(wides.at[3])

        def body(p):
            value = back_in(
                rows_in(cotangent_ref, p, h),
                gate_grad1[h, p],
                get_pair(cells.at[0], p),
                get_pair(cells.at[1], p),
                second[h, p].astype(F32),
                mask_pair(mask_ref, p, h),
                gain1,
                bias1,
                front_ref.at[1],
                back_ref.at[1],
                (front1_sum, sums.at[4], sums.at[5]),
            )
            grad_second[h, p] = value
            gate_grad, product_grad = back_out(
                value.astype(F32),
                get_pair(cells.at[2], p),
                first[h, p].astype(F32),
                gain0,
                bias0,
                front_ref.at[0],
                out_gain0,
                out_bias0,
                out_ref.at[0],
                (out0_sum, sums.at[2], sums.at[3]),
            )
            gate_grad0[h, p] = gate_grad
            put_pair(cells.at[3], p, product_grad)

        over_pairs(body, hook)
        cells_out(cells.at[3], sends.at[5], h)
        send_grad0.send(h)

    def right_sums(r):
        send_grad0.here(r)
        for q in range(Q):
            send_grad0.arrive(r, q)

            def multiply_back(c, m):
                whole[m] = tn(grad0[c, :, lanes(r)], left0[c])
                split_rows(
                    place, whole.at[m], kept_sum, sent_sum.at[1], c, r, slice(None), slice(None)
                )

            over_channels(q, multiply_back)
            swaps[3].sums(sent_sum.at[1], received_sum.at[1], 0, q, r)
            if r == 0:
                swaps[3].sums(sent_sum.at[1], received_sum.at[1], 1, q, r)
        if r == 1:
            for q in range(Q):
                swaps[3].sums(sent_sum.at[1], received_sum.at[1], 1, q, r)

    back_middle(0)
    back_middle(1, lambda: right_sums(0))
    for n in range(5):
        totals[0].put(n * C, front1_sum[:, n * C : (n + 1) * C])
    totals[0].put(5 * C, out0_sum[...])
    totals[0].put(6 * C, out1_sum[...])
    totals[0].put(7 * C, jnp.zeros((C, C), F32))
    totals[0].start()
    right_sums(1)
    totals[0].to_chips()
    for h in range(2):
        for q in range(Q):

            def left_back_out(c, m):
                staged[4, c, :, lanes(h)] = nn(grad0[c], right0[c, :, lanes(h)]).astype(BF16)

            over_channels(q, left_back_out)
            send_left_grad0.send_piece(h, q)
        send_left_grad0.local(h)

    def back_first(h):
        send_left_grad0.arrive_half(h)
        send_right_grad0.arrive_half(h)
        cells_in(arrived.at[4], cells.at[0], h)
        cells_in(arrived.at[5], cells.at[1], h)
        gain, bias = wide(wides.at[0]), wide(wides.at[1])

        def body(p):
            mask_row = mask_pair(mask_ref, p, h)
            value = back_in(
                grad_second[h, p].astype(F32),
                gate_grad0[h, p],
                get_pair(cells.at[0], p),
                get_pair(cells.at[1], p),
                first[h, p].astype(F32),
                mask_row,
                gain,
                bias,
                front_ref.at[0],
                back_ref.at[0],
                (front0_sum, sums.at[0], sums.at[1]),
            ).astype(F32)
            outer_grad = value * mask_row
            sums[8] += outer_grad
            outer_grad = outer_grad.astype(BF16)
            for n in range(2):
                pair_grad_ref[2 * p + n, lanes(h), :] = value[:, lanes(n)].T.astype(BF16)
                grad_row = outer_grad[:, lanes(n)]
                rows = pl.ds(2 * p + n, B, stride=I)
                outer_cells[rows, :] += nt(right_rows[:, lanes(h)], grad_row)
                mixed_left = mixed_cells[rows, :].astype(BF16)
                right_total[:B, lanes(h)] += nn(mixed_left, grad_row)

        over_pairs(body)

    add_halves(swaps[3], received_sum.at[1], staged.at[5], send_right_grad0, 0)
    totals[0].to_dp()
    back_first(0)
    add_halves(swaps[3], received_sum.at[1], staged.at[5], send_right_grad0, 1)
    totals[0].to_all()
    back_first(1)

    right_total_ref[...] = right_total[...].T

    def right_copy(t):
        target = lax.rem(me + t, 16)
        return place.copy(
            right_total_ref.at[rows_of(target * I)],
            right_parts.at[t],
            few_sem.at[2],
            few_sem.at[3],
            target,
        )

    loop(1, 16, lambda t: right_copy(t).start())
    for n in range(5):
        totals[1].put(n * C, front0_sum[:, n * C : (n + 1) * C])
    left_single = jnp.zeros((I, B), F32)
    for b in range(B):
        rows = outer_cells[b * I : (b + 1) * I, :].astype(BF16)
        totals[1].put(5 * C + b * B, tn(own_left, rows))
        left_single += nt(rows, cube_ref[b])
    totals[1].put(13 * C, columns(*[sums.at[n] for n in range(9)]))
    totals[1].start()

    wait_bytes(right_parts.at[1:16], few_sem.at[3])
    right_single = right_total_ref[mine, :]
    for t in range(1, 16):
        right_single += right_parts[t]
    both = jnp.concatenate(
        [left_single, right_single[:, :B], jnp.zeros((I, C - 2 * B), F32)], axis=1
    )
    both = (both * own).astype(BF16)
    single_grad = nn(both, factor_weights(left_weight_ref, right_weight_ref))
    standard = single_standard[...]
    normed_single = (standard * single_gain_ref[...] + single_bias_ref[...]).astype(BF16)
    factor_sums = tn(both, normed_single)
    totals[1].to_chips()
    for n in range(8):
        totals[2].put(n * 64, factor_sums[:64, lanes(n)])
    gain_sum = jnp.sum(single_grad * standard, axis=0, keepdims=True)
    bias_sum = jnp.sum(single_grad, axis=0, keepdims=True)
    tail = [gain_sum[:, lanes(n)] for n in range(8)] + [bias_sum[:, lanes(n)] for n in range(8)]
    totals[2].put(4 * C, jnp.concatenate(tail + [jnp.zeros((2 * C - 16, C), F32)], axis=0))
    totals[2].start()
    single_grad_ref[...] = norm_back(
        single_grad * single_gain_ref[...], standard, single_inverse, axis=1
    ).astype(BF16)
    totals[0].to_sibling()
    totals[1].to_dp()
    totals[2].to_dp()
    totals[1].to_all()
    totals[2].to_all()
    totals[1].to_sibling()
    for batch in totals:
        batch.finish()
    wait_bytes(every_ref.at[: 15 * I], few_sem.at[0])
    wait_bytes(right_parts.at[1:16], few_sem.at[2])
    for way in travel:
        way.sent()
    swaps[0].sent(left0)
    swaps[1].sent(left0)
    swaps[2].sent(left0)
    swaps[3].sent(left0)


def unpack_kernel(
    total_ref,
    single_from,
    pair_from,
    single_to,
    pair_to,
    outer_gain_ref,
    outer_bias_ref,
    outer_left_ref,
    outer_right_ref,
    cube_ref,
    pair_bias_ref,
    norm_gain_ref,
    norm_bias_ref,
    proj_ref,
    gate_ref,
    out_gain_ref,
    out_bias_ref,
    out_ref,
):
    pair_to[...] = pair_from[...]
    single_to[...] = single_from[...]
    for t in range(2):
        front = 8 - 8 * t
        for n in range(4):
            at = (front + n) * C
            proj_ref[t, :, n * C : (n + 1) * C] = total_ref[at : at + C, :].astype(F32)
        at = (front + 4) * C
        gate_ref[t] = total_ref[at : at + C, :].astype(F32)
        out_ref[t] = total_ref[(5 + t) * C : (6 + t) * C, :].astype(F32)
    cube = total_ref[13 * C : 21 * C, :].astype(F32).reshape(B, B, C)
    cube_ref[...] = jnp.swapaxes(cube, 0, 1).reshape(B * B, C)
    for n in range(8):
        at = 22 * C + n * 64
        outer_left_ref[:, n * C : (n + 1) * C] = total_ref[at : at + B, :].astype(F32)
        outer_right_ref[:, n * C : (n + 1) * C] = total_ref[at + B : at + 2 * B, :].astype(F32)
    small = total_ref[21 * C : 22 * C, :].astype(F32).T
    for t in range(2):
        norm_gain_ref[t : t + 1, :] = small[4 * t : 4 * t + 1]
        norm_bias_ref[t : t + 1, :] = small[4 * t + 1 : 4 * t + 2]
        out_gain_ref[t : t + 1, :] = small[4 * t + 2 : 4 * t + 3]
        out_bias_ref[t : t + 1, :] = small[4 * t + 3 : 4 * t + 4]
    pair_bias_ref[...] = small[8:9]
    rows = total_ref[26 * C : 26 * C + 16, :].astype(F32)
    outer_gain_ref[...] = rows[:8]
    outer_bias_ref[...] = rows[8:16]


def call(kernel, outs, scratch, args, name, collective=None):
    return pl.pallas_call(
        kernel,
        out_shape=[jax.ShapeDtypeStruct(shape, dtype) for shape, dtype in outs],
        in_specs=[pl.BlockSpec(memory_space=pltpu.VMEM)] * len(args),
        out_specs=[pl.BlockSpec(memory_space=pltpu.VMEM)] * len(outs),
        scratch_shapes=scratch,
        name=name,
        compiler_params=pltpu.CompilerParams(
            collective_id=collective,
            has_side_effects=collective is not None,
            vmem_limit_bytes=VMEM_LIMIT,
        ),
    )(*args)


DMA = pltpu.SemaphoreType.DMA
BY_CHANNEL = (C, I, J)
BY_PAIR = (2, I // 2, C, J)
HALF = (16, C, J)
EVERY = (16, J, J)


def local(
    single_state,
    pair_state,
    residue_mask,
    pair_cotangent,
    outer_norm_gain,
    outer_norm_bias,
    outer_left,
    outer_right,
    outer_proj,
    outer_bias,
    triangle_norm_gain,
    triangle_norm_bias,
    triangle_proj,
    triangle_gate,
    triangle_out_gain,
    triangle_out_bias,
    triangle_out,
):
    residues = residue_mask.reshape(2, C)
    left_weight, right_weight = outer_left.T, outer_right.T
    single = single_state[0]
    single_gain, single_bias = outer_norm_gain[None, :], outer_norm_bias[None, :]
    back_weight = jnp.concatenate([triangle_proj, triangle_gate], axis=2)
    front_weight = jnp.swapaxes(back_weight, 1, 2)

    scale = 1.0 / float(lax.axis_size("dp") * J)
    pair_gradient, single_gradient, total = call(
        functools.partial(trunk_kernel, scale),
        [((I, J, C), BF16), ((I, single.shape[1]), BF16), ((28 * C, C), BF16)],
        [
            pltpu.VMEM((J, C), BF16),
            pltpu.VMEM((B, B, C), BF16),
            pltpu.VMEM((J, C), F32),
            pltpu.VMEM((16, I, C), F32),
            pltpu.VMEM((I, single.shape[1]), F32),
            pltpu.VMEM((C, 5 * C), F32),
            pltpu.VMEM((C, 5 * C), F32),
            pltpu.VMEM((C, C), F32),
            pltpu.VMEM((C, C), F32),
        ]
        + [pltpu.VMEM(BY_PAIR, BF16)] * 5
        + [pltpu.VMEM((6,) + BY_CHANNEL, BF16)] * 2
        + [pltpu.VMEM((6,) + HALF, BF16)]
        + [pltpu.VMEM(shape, BF16) for shape in (HALF, EVERY, HALF, HALF, EVERY, HALF)]
        + [
            pltpu.VMEM(HALF, F32),
            pltpu.VMEM((2,) + HALF, BF16),
            pltpu.VMEM((2,) + HALF, BF16),
            pltpu.VMEM((4, C * I, C), F32),
            pltpu.VMEM((B * I, C), F32),
            pltpu.VMEM((B * I, C), F32),
            pltpu.VMEM((9, C, C), F32),
            pltpu.VMEM((9, C, J), F32),
            pltpu.VMEM((C, J), F32),
            pltpu.VMEM((UNROLL, C, J), F32),
            pltpu.VMEM((2, I, C), F32),
            DMA((12,)),
            DMA((12, 2, Q)),
            DMA((12, 2)),
            DMA((4,)),
            DMA((4, 2, Q, 2)),
            DMA((4,)),
            DMA((3, 9)),
            DMA((3, 8)),
        ]
        + [
            pltpu.VMEM((count, part, C), BF16)
            for part, parts in ((64, 8), (112, 8), (48, 16))
            for count in (16, 8, 8, parts, 8)
        ],
        (
            single,
            single_gain,
            single_bias,
            left_weight,
            right_weight,
            pair_state[0],
            pair_cotangent[0],
            outer_proj,
            residues,
            outer_bias[None, :],
            triangle_norm_gain,
            triangle_norm_bias,
            triangle_out_gain,
            triangle_out_bias,
            front_weight,
            back_weight,
            triangle_out,
        ),
        "trunk",
        collective=0,
    )
    unpacked = call(
        unpack_kernel,
        [
            (single_gradient.shape, BF16),
            (pair_gradient.shape, BF16),
            ((8, C), F32),
            ((8, C), F32),
            (left_weight.shape, F32),
            (right_weight.shape, F32),
            (outer_proj.shape, F32),
            ((1, C), F32),
            ((2, C), F32),
            ((2, C), F32),
            (triangle_proj.shape, F32),
            (triangle_gate.shape, F32),
            ((2, C), F32),
            ((2, C), F32),
            (triangle_out.shape, F32),
        ],
        [],
        (total, single_gradient, pair_gradient),
        "unpack",
    )
    single_gradient, pair_gradient, *unpacked = unpacked
    unpacked[0] = unpacked[0].reshape(-1)
    unpacked[1] = unpacked[1].reshape(-1)
    unpacked[5] = unpacked[5].reshape(-1)
    unpacked[2] = unpacked[2].T
    unpacked[3] = unpacked[3].T
    return (single_gradient[None], pair_gradient[None]) + tuple(unpacked)


def solution(mesh):
    whole = P()
    rows = P("dp", "axial", None)
    cells = P("dp", "axial", None, None)
    return jax.shard_map(
        local,
        mesh=mesh,
        in_specs=(rows, cells, P("dp", None), cells) + (whole,) * 13,
        out_specs=(rows, cells) + (whole,) * 13,
        check_vma=False,
    )
```
